32 devices in a mesh: dp: 8 (over z, core), seq: 4 (over y, x).
Axes of the slice: x: 2, y: 2, z: 4, core: 2. Of those that a mesh axis runs over, the one named last changes fastest.
Arguments:
- tokens: bfloat16 [16, 2048, 1024], P('dp', 'seq'), may hold values from -6 to 6
- cotangent: bfloat16 [16, 2048, 1024], P('dp', 'seq'), may hold values from -6 to 6
- lengths: int32 [16], P('dp'), may hold values from 1 to 2048, 20480 in all
- species: int32 [16], P('dp'), may hold values from 0 to 7
- ln1_gain: bfloat16 [1024], P(('dp', 'seq')), may hold values from 0.5 to 1.5
- ln1_bias: bfloat16 [1024], P(('dp', 'seq')), may hold values from -3 to 3
- w_query: bfloat16 [1024, 1024], P(('dp', 'seq')), may hold values from -0.1875 to 0.1875
- w_key: bfloat16 [1024, 1024], P(('dp', 'seq')), may hold values from -0.1875 to 0.1875
- w_value: bfloat16 [1024, 1024], P(('dp', 'seq')), may hold values from -0.1875 to 0.1875
- w_out: bfloat16 [1024, 1024], P(('dp', 'seq')), may hold values from -1.5 to 1.5
- ln2_gain: bfloat16 [1024], P(('dp', 'seq')), may hold values from 0.5 to 1.5
- ln2_bias: bfloat16 [1024], P(('dp', 'seq')), may hold values from -3 to 3
- w_gate: bfloat16 [1024, 4096], P(('dp', 'seq')), may hold values from -0.1875 to 0.1875
- w_up: bfloat16 [1024, 4096], P(('dp', 'seq')), may hold values from -0.1875 to 0.1875
- w_down: bfloat16 [4096, 1024], P(('dp', 'seq')), may hold values from -0.09375 to 0.09375
Outputs:
- output: float32 [16, 2048, 1024], P('dp', 'seq')
- grad_tokens: float32 [16, 2048, 1024], P('dp', 'seq')
- grad_ln1_gain: float32 [1024], P(('dp', 'seq'))
- grad_ln1_bias: float32 [1024], P(('dp', 'seq'))
- grad_w_query: float32 [1024, 1024], P(('dp', 'seq'))
- grad_w_key: float32 [1024, 1024], P(('dp', 'seq'))
- grad_w_value: float32 [1024, 1024], P(('dp', 'seq'))
- grad_w_out: float32 [1024, 1024], P(('dp', 'seq'))
- grad_ln2_gain: float32 [1024], P(('dp', 'seq'))
- grad_ln2_bias: float32 [1024], P(('dp', 'seq'))
- grad_w_gate: float32 [1024, 4096], P(('dp', 'seq'))
- grad_w_up: float32 [1024, 4096], P(('dp', 'seq'))
- grad_w_down: float32 [4096, 1024], P(('dp', 'seq'))
The draws below stay inside these ranges and needn't reach their ends.
Inputs may be any that keep to these rules, and one draw needn't show every extreme that they name: The lengths of all windows sum to 16 * 2048 * 5 // 8 and the longest is exactly 2048.
All inputs are finite; a program needn't handle non-finite values. No bound on the sum of `lengths` on one device may be relied on, other than what follows from the above.
Results may differ from the reference program's by a relative error of at most 0.015.
Values may be sent and summed in bfloat16 or wider, within the bound.
No kernel may reach another device: no remote copies, remote signals or barrier semaphores. Data moves between devices by JAX's collectives and lax.ppermute only.
A program may use at most 256 MiB of HBM per device.

```python
import math
import jax
import jax.numpy as jnp
import numpy as np
from jax import lax

D = 1024
HEADS = 16
HEAD_DIM = 64
FF = 4096
WINDOW = 2048
SPECIES = 8
WINDOWS = 16


def set_ends(values, key, smallest, high):
    extent = values.shape
    spot = [jax.random.randint(jax.random.fold_in(key, axis), (), 0, extent[axis]) for axis in range(len(extent))]
    values = values.at[tuple(spot)].set(smallest)
    longest = extent.index(max(extent))
    spot[longest] = (spot[longest] + 1) % extent[longest]
    return values.at[tuple(spot)].set(high)


def steps_of(own_key, shape, cuts, low, top_value):
    level, own = 1.0, jax.random.fold_in(own_key, 6)
    for dim, blocks in cuts:
        steps = jnp.exp(jax.random.uniform(jax.random.fold_in(own, dim), (blocks,), jnp.float32, low / len(cuts), top_value / len(cuts)))
        level = level * jnp.repeat(steps, shape[dim] // blocks).reshape([-1 if axis == dim else 1 for axis in range(len(shape))])
    return level


def profile(number_of, total, reach, slope):
    portions = [(1 << 20) // math.isqrt(standing ** slope) + 1 for standing in range(2, number_of + 1)]
    surplus, given = total - reach - (number_of - 1), [1] * (number_of - 1)
    while surplus > 0:
        free = [i for i in range(number_of - 1) if given[i] < reach]
        mass, left = sum([portions[i] for i in free]), surplus
        for i in free:
            extra = min(reach - given[i], max(1, left * portions[i] // mass), surplus)
            given[i] = given[i] + extra
            surplus = surplus - extra
    return np.array([reach] + given)


def uneven_parts(rng, count, total, limit, skew):
    if count == 2:
        one = jax.random.randint(rng, (), max(1, total - limit), min(limit, total - 1) + 1)
        return jnp.stack([one, total - one])
    sizes = jnp.asarray(profile(count, total, limit, skew), jnp.int32)
    twos = (count - 1) // 2
    giver, taker = sizes[1:1 + 2 * twos:2], sizes[2:2 + 2 * twos:2]
    margin = jnp.minimum(giver - 1, limit - taker)
    passed = jax.random.randint(jax.random.fold_in(rng, 1), (twos,), 0, 1 << 20) % (margin + 1)
    sizes = sizes.at[1:1 + 2 * twos:2].set(giver - passed).at[2:2 + 2 * twos:2].set(taker + passed)
    return sizes[jax.random.permutation(jax.random.fold_in(rng, 2), count)]


def gaussian(own_key, dims, width, limit, pieces=(), kind=jnp.bfloat16):
    drawn = jax.random.normal(own_key, dims, jnp.float32) * width
    if len(pieces) > 0:
        drawn = steps_of(own_key, dims, pieces, -0.22, 0.18) * drawn
    return jnp.clip(drawn, min=-limit, max=limit).astype(kind)


def setup_inputs(seed: int = 0) -> dict:
    arg_keys = jax.random.split(jax.random.key(seed), 16)
    return {
        "tokens": gaussian(arg_keys[0], (WINDOWS, WINDOW, D), 1.0, 6.0, ((0, 8), (1, 4))),
        "cotangent": gaussian(arg_keys[1], (WINDOWS, WINDOW, D), 1.0, 6.0, ((0, 8), (1, 4))),
        "lengths": uneven_parts(arg_keys[2], WINDOWS, WINDOWS * WINDOW * 5 // 8, WINDOW, 2).astype(jnp.int32),
        "species": set_ends(jax.random.randint(arg_keys[3], (WINDOWS,), 0, SPECIES), jax.random.fold_in(arg_keys[3], 1), 0, SPECIES - 1).astype(jnp.int32),
        "ln1_gain": jnp.clip(1.0 + 0.1 * jax.random.normal(arg_keys[4], (D,), jnp.float32), 0.5, 1.5).astype(jnp.bfloat16),
        "ln1_bias": gaussian(arg_keys[5], (D,), 0.3, 3.0, ((0, 32),)),
        "w_query": gaussian(arg_keys[6], (D, D), D ** -0.5, 0.1875, ((0, 32),)),
        "w_key": gaussian(arg_keys[7], (D, D), D ** -0.5, 0.1875, ((0, 32),)),
        "w_value": gaussian(arg_keys[8], (D, D), D ** -0.5, 0.1875, ((0, 32),)),
        "w_out": gaussian(arg_keys[9], (D, D), (D // 64) ** -0.5, 1.5, ((0, 32),)),
        "ln2_gain": jnp.clip(1.0 + 0.1 * jax.random.normal(arg_keys[10], (D,), jnp.float32), 0.5, 1.5).astype(jnp.bfloat16),
        "ln2_bias": gaussian(arg_keys[11], (D,), 0.3, 3.0, ((0, 32),)),
        "w_gate": gaussian(arg_keys[12], (D, FF), D ** -0.5, 0.1875, ((0, 32),)),
        "w_up": gaussian(arg_keys[13], (D, FF), D ** -0.5, 0.1875, ((0, 32),)),
        "w_down": gaussian(arg_keys[14], (FF, D), FF ** -0.5, 0.09375, ((0, 32),)),
    }


@jax.custom_vjp
def low(v):
    return lax.optimization_barrier(v.astype(jnp.bfloat16)).astype(jnp.float32)

@jax.custom_vjp
def low_back(v):
    return v

def low_keep(v):
    return (low(v), None)

def low_pass(kept, grad):
    return (grad,)

def back_keep(v):
    return (v, None)

def back_low(kept, grad):
    return (low(grad),)
low.defvjp(low_keep, low_pass)
low_back.defvjp(back_keep, back_low)
EPS = 1e-05
HIGH = lax.Precision.HIGHEST

def layer_norm(value, gain, bias):
    mean_v = lax.optimization_barrier(jnp.mean(value, axis=-1, keepdims=True))
    centered = value - mean_v
    var_v = lax.optimization_barrier(jnp.mean(centered * centered, axis=-1, keepdims=True))
    return centered * lax.rsqrt(var_v + EPS) * gain + bias

def rotary(value, positions):
    half = value.shape[-1] // 2
    freq = 10000.0 ** (-2.0 * jnp.arange(half, dtype=jnp.float32) / value.shape[-1])
    angle = positions.astype(jnp.float32)[:, None] * freq[None, :]
    cosine = jnp.cos(angle)[:, None, :]
    sine = jnp.sin(angle)[:, None, :]
    first = value[..., :half]
    second = value[..., half:]
    return jnp.concatenate([first * cosine - second * sine, second * cosine + first * sine], axis=-1)

def head_attend(query, key, value, valid):
    raw = jnp.dot(query, key.T, precision=HIGH)
    scores = low_back(raw * HEAD_DIM ** (-0.5))
    scores = jnp.where(valid[None, :], scores, -1e+30)
    top = lax.optimization_barrier(jnp.max(scores, axis=-1, keepdims=True))
    lse = top + jnp.log(lax.optimization_barrier(jnp.sum(jnp.exp(scores - top), axis=-1, keepdims=True)))
    probs = low(jnp.exp(scores - lse))
    return jnp.dot(probs, value, precision=HIGH)

def forward(params, tokens, length):
    ln1_gain, ln1_bias, w_query, w_key, w_value, w_out, ln2_gain, ln2_bias, w_gate, w_up, w_down = params
    positions = jnp.arange(WINDOW)
    valid = positions < length
    normed = low(layer_norm(tokens, ln1_gain, ln1_bias))

    def project(weight):
        return low_back(jnp.dot(normed, weight, precision=HIGH)).reshape(WINDOW, HEADS, HEAD_DIM)
    query = low(rotary(project(w_query), positions))
    key = low(rotary(project(w_key), positions))
    value = low(project(w_value))

    def attend(items):
        return head_attend(items[0], items[1], items[2], valid)
    heads_out = lax.map(jax.checkpoint(attend), (query.transpose(1, 0, 2), key.transpose(1, 0, 2), value.transpose(1, 0, 2)))
    mixed = low(low_back(heads_out.transpose(1, 0, 2).reshape(WINDOW, D)))
    middle = tokens + low_back(jnp.dot(mixed, w_out, precision=HIGH))
    normed_two = low(layer_norm(middle, ln2_gain, ln2_bias))
    gate = low_back(jnp.dot(normed_two, w_gate, precision=HIGH))
    upper = low_back(jnp.dot(normed_two, w_up, precision=HIGH))
    hidden = low(jax.nn.silu(gate) * upper)
    return middle + low_back(jnp.dot(hidden, w_down, precision=HIGH))

def reference(tokens, cotangent, lengths, species, ln1_gain, ln1_bias, w_query, w_key, w_value, w_out, ln2_gain, ln2_bias, w_gate, w_up, w_down):
    params = (ln1_gain.astype(jnp.float32), ln1_bias.astype(jnp.float32), w_query.astype(jnp.float32), w_key.astype(jnp.float32), w_value.astype(jnp.float32), w_out.astype(jnp.float32), ln2_gain.astype(jnp.float32), ln2_bias.astype(jnp.float32), w_gate.astype(jnp.float32), w_up.astype(jnp.float32), w_down.astype(jnp.float32))
    species_ids = jnp.arange(SPECIES)
    onehot = (species[:, None] == species_ids[None, :]).astype(jnp.float32)
    counts = lax.optimization_barrier(jnp.sum(onehot * lengths[:, None].astype(jnp.float32), axis=0))
    window_weight = SPECIES * lax.optimization_barrier(jnp.sum(onehot * counts[None, :], axis=1)) / jnp.sum(counts)

    def step(carry, items):
        window, cot, length, weight = items
        positions = jnp.arange(WINDOW)
        row_scale = jnp.where(positions < length, weight, 0.0)

        def run(weights, inputs):
            return forward(weights, inputs, length)
        out, pullback = jax.vjp(run, params, window.astype(jnp.float32))
        grads, grad_in = pullback(cot.astype(jnp.float32) * row_scale[:, None])
        summed = tuple((c + g for c, g in zip(carry, grads)))
        return (summed, (out, grad_in))
    zeros = tuple((jnp.zeros(p.shape, jnp.float32) for p in params))
    grads, (outputs, grad_inputs) = lax.scan(step, zeros, (tokens, cotangent, lengths, window_weight))
    return (outputs, grad_inputs, grads[0], grads[1], grads[2], grads[3], grads[4], grads[5], grads[6], grads[7], grads[8], grads[9], grads[10])
```

```python
import functools

import jax
import jax.numpy as jnp
from jax import lax
from jax.experimental import pallas as pl
from jax.experimental.pallas import tpu as pltpu
from jax.sharding import PartitionSpec as P

HEAD_DIM = 64
SPECIES = 8
EPS = 1e-05
LOG2E = 1.4426950408889634
BOTH = ("dp", "seq")
F32 = jnp.float32
BF16 = jnp.bfloat16
QUERIES = 512
KEYS = 512
VMEM = 60 * 2**20

NN = (((1,), (0,)), ((), ()))
NT = (((1,), (1,)), ((), ()))


def dot(a, b, dims=NN):
    return lax.dot_general(a, b, dims, preferred_element_type=F32)


def attend_kernel(len_ref, q_ref, k_ref, v_ref, o_ref, l_ref, vt_ref):
    length = len_ref[pl.program_id(0)]
    lane = lax.broadcasted_iota(jnp.int32, (1, 128), 1)
    rows = q_ref.shape[2]

    @pl.when(pl.program_id(2) == 0)
    def _():
        vt_ref[...] = v_ref[0, 0].T

    q2 = q_ref[0, 0] * BF16(0.125)

    def run(n):
        k2 = k_ref[0, 0, :n]
        outs = []
        for h in range(2):
            qh = jnp.where((lane // 64) == h, q2, BF16(0))
            s = dot(k2, qh, NT)
            row = lax.broadcasted_iota(jnp.int32, (KEYS, rows), 0) + (n - KEYS)
            last = jnp.where(row < length, s[n - KEYS :], -1e30)
            s = jnp.concatenate([s[: n - KEYS], last], 0) if n > KEYS else last
            m = jnp.max(s, axis=0, keepdims=True)
            p = jnp.exp2((s - m) * LOG2E)
            total = jnp.sum(p, axis=0, keepdims=True)
            o = dot(vt_ref[h * 64 : h * 64 + 64, :n], p.astype(BF16))
            outs.append(o / total)
            l_ref[0, 0, h : h + 1] = m + jnp.log(total)
        o_ref[0] = jnp.concatenate(outs, 0).T.astype(BF16)

    blocks = (length + KEYS - 1) // KEYS
    for i in range(k_ref.shape[2] // KEYS):
        pl.when(blocks == i + 1)(functools.partial(run, KEYS * (i + 1)))


def attend(lengths, qkv):
    three, wins, span, width = qkv.shape
    pairs = width // 128
    rows = min(QUERIES, span)

    def whole(which):
        return pl.BlockSpec((1, 1, span, 128), lambda w, h, i, _: (which, w, 0, h))

    return pl.pallas_call(
        attend_kernel,
        grid_spec=pltpu.PrefetchScalarGridSpec(
            num_scalar_prefetch=1,
            grid=(wins, pairs, span // rows),
            in_specs=[
                pl.BlockSpec((1, 1, rows, 128), lambda w, h, i, _: (0, w, i, h)),
                whole(1),
                whole(2),
            ],
            out_specs=[
                pl.BlockSpec((1, rows, 128), lambda w, h, i, _: (w, i, h)),
                pl.BlockSpec((1, 1, 2, rows), lambda w, h, i, _: (w, h, 0, i)),
            ],
            scratch_shapes=[pltpu.VMEM((128, span), BF16)],
        ),
        out_shape=[
            jax.ShapeDtypeStruct((wins, span, width), BF16),
            jax.ShapeDtypeStruct((wins, pairs, 2, span), F32),
        ],
        compiler_params=pltpu.CompilerParams(vmem_limit_bytes=VMEM),
        cost_estimate=pl.CostEstimate(
            flops=4 * wins * span * span * width * 4,
            bytes_accessed=8 * wins * span * width,
            transcendentals=wins * span * span * width // 64,
        ),
        name="attend",
    )(lengths, qkv, qkv, qkv)


def attend_back_kernel(
    len_ref, q_ref, k_ref, v_ref, o_ref, g_ref, l_ref, d_ref, kt_ref, dq_ref, dk_ref, dv_ref
):
    step = pl.program_id(2)
    length = len_ref[pl.program_id(0)]
    rows = q_ref.shape[2]
    lane = lax.broadcasted_iota(jnp.int32, (1, 128), 1)

    @pl.when(step == 0)
    def _():
        kt_ref[...] = (k_ref[0, 0] * BF16(0.125)).T
        dk_ref[...] = jnp.zeros_like(dk_ref)
        dv_ref[...] = jnp.zeros_like(dv_ref)

    here = pl.ds(pl.multiple_of(step * rows, rows), rows)

    @pl.when(step * rows >= length)
    def _():
        dq_ref[here] = jnp.zeros((rows, 128), BF16)

    @pl.when(step * rows < length)
    def _():
        q2 = q_ref[0, 0] * BF16(0.125)
        g2 = g_ref[0]
        products = (g2.astype(F32) * o_ref[0].astype(F32)).T
        qs, gs, ls, ds = [], [], [], []
        for h in range(2):
            mine = (lane // 64) == h
            qs.append(jnp.where(mine, q2, BF16(0)))
            gs.append(jnp.where(mine, g2, BF16(0)))
            ls.append(l_ref[0, 0, h : h + 1] * LOG2E)
            ds.append(jnp.sum(products[h * 64 : h * 64 + 64], axis=0, keepdims=True))
        qc = jnp.concatenate(qs, 0)
        gc = jnp.concatenate(gs, 0)
        lc = jnp.concatenate(ls, 1)
        dc = jnp.concatenate(ds, 1)

        def chunk(c, acc, masked):
            base = c * KEYS
            sl = pl.ds(pl.multiple_of(base, KEYS), KEYS)
            k2 = k_ref[0, 0, sl]
            v2 = v_ref[0, 0, sl]
            p = jnp.exp2(dot(k2, qc, NT) * LOG2E - lc)
            if masked:
                row = lax.broadcasted_iota(jnp.int32, (KEYS, 1), 0) + base
                p = jnp.where(row < length, p, 0.0)
            gp = dot(v2, gc, NT)
            gs_low = (p * (gp - dc)).astype(BF16)
            dv_ref[sl] += dot(p.astype(BF16), gc)
            dk_ref[sl] += dot(gs_low, qc)
            return tuple(
                acc[h] + dot(kt_ref[h * 64 : h * 64 + 64, sl], gs_low[:, h * rows : (h + 1) * rows])
                for h in range(2)
            )

        acc = (jnp.zeros((64, rows), F32),) * 2
        full = length // KEYS
        acc = lax.fori_loop(0, full, lambda c, a: chunk(c, a, False), acc)
        acc = lax.cond(full * KEYS < length, lambda a: chunk(full, a, True), lambda a: a, acc)
        dq_ref[here] = jnp.concatenate(acc, 0).T.astype(BF16)

    @pl.when(step == pl.num_programs(2) - 1)
    def _():
        d_ref[0, 0] = dq_ref[...]
        d_ref[1, 0] = dk_ref[...].astype(BF16)
        d_ref[2, 0] = dv_ref[...].astype(BF16)


def attend_back(lengths, qkv, mixed, grad, lse):
    three, wins, span, width = qkv.shape
    pairs = width // 128
    rows = min(QUERIES, span)
    block = pl.BlockSpec((1, rows, 128), lambda w, h, i, _: (w, i, h))

    def whole(which):
        return pl.BlockSpec((1, 1, span, 128), lambda w, h, i, _: (which, w, 0, h))

    return pl.pallas_call(
        attend_back_kernel,
        grid_spec=pltpu.PrefetchScalarGridSpec(
            num_scalar_prefetch=1,
            grid=(wins, pairs, span // rows),
            in_specs=[
                pl.BlockSpec((1, 1, rows, 128), lambda w, h, i, _: (0, w, i, h)),
                whole(1),
                whole(2),
                block,
                block,
                pl.BlockSpec((1, 1, 2, rows), lambda w, h, i, _: (w, h, 0, i)),
            ],
            out_specs=pl.BlockSpec((3, 1, span, 128), lambda w, h, i, _: (0, w, 0, h)),
            scratch_shapes=[
                pltpu.VMEM((128, span), BF16),
                pltpu.VMEM((span, 128), BF16),
                pltpu.VMEM((span, 128), F32),
                pltpu.VMEM((span, 128), F32),
            ],
        ),
        out_shape=jax.ShapeDtypeStruct((3, wins, span, width), BF16),
        compiler_params=pltpu.CompilerParams(vmem_limit_bytes=VMEM),
        cost_estimate=pl.CostEstimate(
            flops=10 * wins * span * span * width * 3,
            bytes_accessed=16 * wins * span * width,
            transcendentals=wins * span * span * width // 64,
        ),
        name="attend_back",
    )(lengths, qkv, qkv, qkv, mixed, grad, lse)


def normalise(value):
    centered = value - jnp.mean(value, axis=-1, keepdims=True)
    inverse = lax.rsqrt(jnp.mean(centered * centered, axis=-1, keepdims=True) + EPS)
    return centered * inverse, inverse


def norm_back(grad, normal, inverse, gain):
    scaled = grad * gain
    centered = scaled - jnp.mean(scaled, axis=-1, keepdims=True)
    return inverse * (centered - normal * jnp.mean(scaled * normal, axis=-1, keepdims=True))


def rotary(value, cosine, sine):
    half = HEAD_DIM // 2
    rows, width = value.shape[-2:]
    split = value.reshape(value.shape[:-1] + (width // HEAD_DIM, HEAD_DIM))
    first, second = split[..., :half], split[..., half:]
    cos_wide, sin_wide = cosine[:, None, :], sine[:, None, :]
    turned = jnp.concatenate(
        [first * cos_wide - second * sin_wide, second * cos_wide + first * sin_wide], axis=-1
    )
    return turned.reshape(value.shape)


def angles_of(positions):
    half = HEAD_DIM // 2
    freq = 10000.0 ** (-2.0 * jnp.arange(half, dtype=F32) / HEAD_DIM)
    angle = positions.astype(F32)[:, None] * freq[None, :]
    return (jnp.cos(angle), jnp.sin(angle))


class Links:
    def __init__(self, mesh):
        self.dp, self.seq = mesh.shape["dp"], mesh.shape["seq"]
        self.count = self.dp * self.seq
        self.bits = self.count.bit_length() - 1
        self.core = self.seq.bit_length() - 1
        self.seq_bits = list(range(self.core))
        self.dp_bits = list(range(self.core, self.bits))
        self.chips = self.seq_bits + self.dp_bits[1:]

    def me(self):
        return lax.axis_index("dp") * self.seq + lax.axis_index("seq")

    def swap(self, value, bit):
        pairs = [(i, i ^ (1 << bit)) for i in range(self.count)]
        return lax.ppermute(value, BOTH, pairs)

    def orders(self, turn):
        turn = turn % len(self.chips)
        return [self.core] + self.chips[turn:] + self.chips[:turn]

    def scatter_sum(self, value, order, wire):
        blocks = value.reshape((2,) * self.bits + (value.shape[0] // self.count,) + value.shape[1:])
        axes = list(range(self.bits - 1, -1, -1))
        me = self.me()
        for bit in order:
            at = axes.index(bit)
            own = (me >> bit) & 1
            away = lax.dynamic_index_in_dim(blocks, 1 - own, at, keepdims=False).astype(wire)
            kept = lax.dynamic_index_in_dim(blocks, own, at, keepdims=False)
            blocks = kept.astype(F32) + self.swap(away, bit).astype(F32)
            axes.pop(at)
        return blocks

    def window_sum(self, value):
        for bit in self.dp_bits:
            value = value + self.swap(value, bit)
        return value


def to_heads(value):
    return lax.all_to_all(value, "seq", split_axis=3, concat_axis=2, tiled=True)


def to_positions(value):
    return lax.all_to_all(value, "seq", split_axis=2, concat_axis=3, tiled=True)


def body(
    links,
    tokens,
    cotangent,
    lengths,
    species,
    ln1_gain,
    ln1_bias,
    w_query,
    w_key,
    w_value,
    w_out,
    ln2_gain,
    ln2_bias,
    w_gate,
    w_up,
    w_down,
):
    wins, rows, width = tokens.shape
    flat = wins * rows
    ff = w_gate.shape[1]
    species_ids = jnp.arange(SPECIES)
    onehot = (species[:, None] == species_ids[None, :]).astype(F32)
    counts = links.window_sum(jnp.sum(onehot * lengths[:, None].astype(F32), axis=0))
    window_weight = SPECIES * jnp.sum(onehot * counts[None, :], axis=1) / jnp.sum(counts)

    def gathered(value):
        return lax.all_gather(value, BOTH, axis=0, tiled=True)

    small = jnp.stack([ln1_gain, ln1_bias, ln2_gain, ln2_bias], axis=1)
    small = jnp.pad(small, ((0, 0), (0, 124)))
    first = gathered(jnp.concatenate([w_query, w_key, w_value, small], axis=1))
    second = gathered(jnp.concatenate([w_out, w_gate, w_up], axis=1))
    down_w = gathered(w_down)
    qkv_w = first[:, : 3 * width]
    gain_one, bias_one, gain_two, bias_two = (
        first[:, 3 * width : 3 * width + 4].T.astype(F32).reshape(4, 1, width)
    )
    out_w = second[:, :width]
    both_w = second[:, width:]

    positions = lax.axis_index("seq") * rows + jnp.arange(rows)
    cosine, sine = angles_of(positions)
    row_scale = jnp.where(positions[None, :] < lengths[:, None], window_weight[:, None], 0.0)
    row_scale = row_scale.reshape(flat, 1)
    inputs = tokens.astype(F32).reshape(flat, width)
    normal_one, inverse_one = normalise(inputs)
    normed_low = (normal_one * gain_one + bias_one).astype(BF16)

    qkv = dot(normed_low, qkv_w).reshape(wins, rows, 3, width)
    query = rotary(qkv[:, :, 0], cosine, sine).astype(BF16)
    key = rotary(qkv[:, :, 1], cosine, sine).astype(BF16)
    value = qkv[:, :, 2].astype(BF16)

    qkv_heads = to_heads(jnp.stack([query, key, value]))
    mixed_heads, lse = attend(lengths, qkv_heads)
    mixed = to_positions(mixed_heads[None])[0].reshape(flat, width)
    middle = inputs + dot(mixed, out_w)
    normal_two, inverse_two = normalise(middle)
    normed_two_low = (normal_two * gain_two + bias_two).astype(BF16)
    both = dot(normed_two_low, both_w)
    gate, upper = both[:, :ff], both[:, ff:]
    sigma = jax.nn.sigmoid(gate)
    hidden = (gate * sigma * upper).astype(BF16)
    output = middle + dot(hidden, down_w)

    grad_out = cotangent.astype(F32).reshape(flat, width) * row_scale
    grad_low = grad_out.astype(BF16)
    grad_down = dot(hidden.T, grad_low).astype(BF16)
    sum_down = links.scatter_sum(grad_down, links.orders(0), BF16)
    grad_hidden = dot(grad_low, down_w, NT)
    grad_up = (grad_hidden * gate * sigma).astype(BF16)
    grad_gate = (grad_hidden * upper * sigma * (1.0 + gate * (1.0 - sigma))).astype(BF16)
    normed_two_t = normed_two_low.T
    sum_gate = links.scatter_sum(dot(normed_two_t, grad_gate).astype(BF16), links.orders(1), BF16)
    sum_up = links.scatter_sum(dot(normed_two_t, grad_up).astype(BF16), links.orders(2), BF16)
    grad_normed_two = dot(grad_gate, both_w[:, :ff], NT) + dot(grad_up, both_w[:, ff:], NT)
    grad_gain_two = jnp.sum(grad_normed_two * normal_two, axis=0)
    grad_bias_two = jnp.sum(grad_normed_two, axis=0)
    grad_middle = grad_out + norm_back(grad_normed_two, normal_two, inverse_two, gain_two)
    grad_middle_low = grad_middle.astype(BF16)
    grad_mixed = dot(grad_middle_low, out_w, NT).astype(BF16)
    grad_heads = to_heads(grad_mixed.reshape(1, wins, rows, width))[0]
    sum_out = links.scatter_sum(
        dot(mixed.T, grad_middle_low).astype(BF16), links.orders(0), BF16
    )

    grad_qkv = to_positions(attend_back(lengths, qkv_heads, mixed_heads, grad_heads, lse))
    grad_q_low = rotary(grad_qkv[0].astype(F32), cosine, -sine).astype(BF16).reshape(flat, width)
    grad_k_low = rotary(grad_qkv[1].astype(F32), cosine, -sine).astype(BF16).reshape(flat, width)
    grad_v_low = grad_qkv[2].reshape(flat, width)
    low = jnp.concatenate([grad_q_low, grad_k_low, grad_v_low], axis=1)
    sum_qkv = links.scatter_sum(dot(normed_low.T, low).astype(BF16), links.orders(1), BF16)
    grad_normed = dot(low, qkv_w, NT)
    grad_gain_one = jnp.sum(grad_normed * normal_one, axis=0)
    grad_bias_one = jnp.sum(grad_normed, axis=0)
    grad_inputs = grad_middle + norm_back(grad_normed, normal_one, inverse_one, gain_one)
    vectors = jnp.stack([grad_gain_one, grad_bias_one, grad_gain_two, grad_bias_two])
    vectors = vectors.reshape(4, links.count, width // links.count).transpose(1, 0, 2)
    vectors = links.scatter_sum(vectors.reshape(links.count * 4, -1), links.orders(0), F32)
    return (
        output.reshape(wins, rows, width),
        grad_inputs.reshape(wins, rows, width),
        vectors[0],
        vectors[1],
        sum_qkv[:, :width],
        sum_qkv[:, width : 2 * width],
        sum_qkv[:, 2 * width :],
        sum_out,
        vectors[2],
        vectors[3],
        sum_gate,
        sum_up,
        sum_down,
    )


def solution(mesh):
    token = P("dp", "seq", None)
    vector = P(BOTH)
    matrix = P(BOTH, None)
    return jax.shard_map(
        functools.partial(body, Links(mesh)),
        mesh=mesh,
        in_specs=(
            (token, token, P("dp"), P("dp"), vector, vector)
            + (matrix,) * 4
            + (vector, vector)
            + (matrix,) * 3
        ),
        out_specs=(
            (token, token, vector, vector) + (matrix,) * 4 + (vector, vector) + (matrix,) * 3
        ),
        check_vma=False,
    )
```

```python
import functools

import jax
import jax.numpy as jnp
from jax import lax
from jax.experimental import pallas as pl
from jax.experimental.pallas import tpu as pltpu
from jax.sharding import PartitionSpec as P

HEAD_DIM = 64
SPECIES = 8
EPS = 1e-05
LOG2E = 1.4426950408889634
BOTH = ("dp", "seq")
F32 = jnp.float32
BF16 = jnp.bfloat16
FF_BLOCK = 512
FEED_ROWS = 512
PARTS = 2
ROW_UNIT = 32
VMEM = 60 * 2**20

NN = (((1,), (0,)), ((), ()))
NT = (((1,), (1,)), ((), ()))


def dot(a, b, dims=NN):
    return lax.dot_general(a, b, dims, preferred_element_type=F32)


def shape(dims, dtype):
    return jax.ShapeDtypeStruct(dims, dtype)


def params():
    return pltpu.CompilerParams(vmem_limit_bytes=VMEM)


def cost(flops, moved, exps=0):
    return pl.CostEstimate(flops=flops, bytes_accessed=moved, transcendentals=exps)


def normalise(value):
    centered = value - jnp.mean(value, axis=-1, keepdims=True)
    inverse = lax.rsqrt(jnp.mean(centered * centered, axis=-1, keepdims=True) + EPS)
    return centered * inverse, inverse


def norm_back(grad, normal, inverse, gain):
    scaled = grad * gain
    centered = scaled - jnp.mean(scaled, axis=-1, keepdims=True)
    return inverse * (centered - normal * jnp.mean(scaled * normal, axis=-1, keepdims=True))


def turn(value, cosine, early, late):
    return value * cosine + pltpu.roll(value, 96, 1) * early + pltpu.roll(value, 32, 1) * late


def tables(positions):
    half = HEAD_DIM // 2
    freq = 10000.0 ** (-2.0 * jnp.arange(half, dtype=F32) / HEAD_DIM)
    angle = positions.astype(F32)[:, None] * freq[None, :]
    cosine, sine = jnp.cos(angle), jnp.sin(angle)
    zero = jnp.zeros_like(sine)
    return (
        jnp.concatenate([cosine] * 4, axis=1),
        jnp.concatenate([-sine, zero, -sine, zero], axis=1),
        jnp.concatenate([zero, sine, zero, sine], axis=1),
    )


def arrange_kernel(base_ref, *refs):
    for k, ref in enumerate(refs[:-1]):
        refs[-1][base_ref[0] ^ k] = ref[...]


def arrange(base, blocks):
    rows, width = blocks[0].shape
    return pl.pallas_call(
        arrange_kernel,
        grid_spec=pltpu.PrefetchScalarGridSpec(
            num_scalar_prefetch=1,
            grid=(1,),
            in_specs=[pl.BlockSpec((rows, width), lambda i, _: (0, 0))] * len(blocks),
            out_specs=pl.BlockSpec((len(blocks), rows, width), lambda i, _: (0, 0, 0)),
        ),
        out_shape=shape((len(blocks), rows, width), blocks[0].dtype),
        compiler_params=params(),
        cost_estimate=cost(0, 16 * rows * width),
        name="arrange",
    )(base, *blocks).reshape(len(blocks) * rows, width)


def settle_kernel(base_ref, *refs):
    blocks, added, out_ref = refs[:4], refs[4:-1], refs[-1]
    here = pl.program_id(0)

    for k, ref in enumerate(blocks):

        @pl.when((base_ref[0] ^ k) == here)
        def _(ref=ref):
            value = ref[...].astype(F32)
            out_ref[0] = value + added[0][0].astype(F32) if added else value


def settle(base, blocks, added):
    rows, width = blocks[0].shape
    block = pl.BlockSpec((1, rows, width), lambda i, _: (i, 0, 0))
    return pl.pallas_call(
        settle_kernel,
        grid_spec=pltpu.PrefetchScalarGridSpec(
            num_scalar_prefetch=1,
            grid=(4,),
            in_specs=[pl.BlockSpec((rows, width), lambda i, _: (0, 0))] * 4
            + [block] * len(added),
            out_specs=block,
        ),
        out_shape=shape((4, rows, width), F32),
        compiler_params=params(),
        cost_estimate=cost(0, 32 * rows * width),
        name="settle",
    )(base, *blocks, *[a.reshape(4, rows, width) for a in added])


def project_kernel(at_ref, x_ref, w_ref, vec_ref, c_ref, e_ref, l_ref, send_ref, n_ref):
    which = pl.program_id(0)
    _, rows, lanes = send_ref.shape

    @pl.when(which == 0)
    def _():
        normal, _ = normalise(x_ref[...].astype(F32))
        n_ref[...] = (normal * vec_ref[0:1] + vec_ref[1:2]).astype(BF16)

    product = dot(n_ref[...], w_ref[0])
    cosine, early, late = c_ref[...], e_ref[...], l_ref[...]

    def put(rotate):
        for at in range(0, lanes, 128):
            piece = product[:, at : at + 128]
            if rotate:
                piece = turn(piece, cosine, early, late)
            send_ref[0, :, at : at + 128] = piece.astype(BF16)

    pl.when(which < 2)(lambda: put(True))
    pl.when(which == 2)(lambda: put(False))


def project(at, tokens, weights, vectors, table, lanes):
    rows, width = tokens.shape
    wide = pl.BlockSpec((rows, 128), lambda j, _: (0, 0))
    return pl.pallas_call(
        project_kernel,
        grid_spec=pltpu.PrefetchScalarGridSpec(
            num_scalar_prefetch=1,
            grid=(3,),
            in_specs=[
                pl.BlockSpec((rows, width), lambda j, _: (0, 0)),
                pl.BlockSpec((1, width, lanes), lambda j, at: (j, 0, at[0])),
                pl.BlockSpec((4, width), lambda j, _: (0, 0)),
                wide,
                wide,
                wide,
            ],
            out_specs=[
                pl.BlockSpec((1, rows, lanes), lambda j, _: (j, 0, 0)),
                pl.BlockSpec((rows, width), lambda j, _: (0, 0)),
            ],
        ),
        out_shape=[shape((3, rows, lanes), BF16), shape((rows, width), BF16)],
        compiler_params=params(),
        cost_estimate=cost(6 * rows * width * lanes, 6 * rows * lanes + 6 * width * lanes),
        name="project",
    )(at, tokens, weights, vectors, *table)


def attend_kernel(info_ref, *refs, team):
    q_refs, k_refs, v_refs = refs[:team], refs[team : 2 * team], refs[2 * team : 3 * team]
    o_refs, (l_ref, vt_ref) = refs[3 * team : 4 * team], refs[4 * team :]
    length, side, upper = info_ref[0], info_ref[1], info_ref[2]
    lane = lax.broadcasted_iota(jnp.int32, (1, 128), 1)
    block = q_refs[0].shape[0]
    keys, ups = 2 * block, team // 2
    up = pl.program_id(2)

    def chunk(arrays, p, b):
        rows = slice(b * block, (b + 1) * block)
        return jnp.concatenate([arrays[2 * p][rows], arrays[2 * p + 1][rows]], axis=0)

    @pl.when((pl.program_id(1) == 0) & (up == 0))
    def _():
        for p in range(ups):
            for b in range(4):
                at = (4 * p + b) * keys
                vt_ref[:, at : at + keys] = chunk(v_refs, p, b).T

    q2 = jnp.concatenate([q_refs[0][...], q_refs[1][...]], axis=0)
    for p in range(1, ups):
        other = jnp.concatenate([q_refs[2 * p][...], q_refs[2 * p + 1][...]], axis=0)
        q2 = jnp.where(up == p, other, q2)
    q2 = q2 * BF16(0.125)

    def positions(p, b):
        row = lax.broadcasted_iota(jnp.int32, (keys, keys), 0)
        return row ^ (side * block) | (4 * (upper ^ p) + b) * keys

    def run(chunks):
        k2 = jnp.concatenate([chunk(k_refs, c // 4, c % 4) for c in range(chunks)], axis=0)
        n = chunks * keys
        outs = []
        for h in range(2):
            qh = jnp.where((lane // 64) == h, q2, BF16(0))
            s = dot(k2, qh, NT)
            if ups == 1:
                last = jnp.where(positions(0, chunks - 1) < length, s[n - keys :], -1e30)
                s = jnp.concatenate([s[: n - keys], last], 0) if chunks > 1 else last
            else:
                valid = [positions(c // 4, c % 4) < length for c in range(chunks)]
                s = jnp.concatenate(
                    [jnp.where(v, s[c * keys : (c + 1) * keys], -1e30) for c, v in enumerate(valid)],
                    axis=0,
                )
            m = jnp.max(s, axis=0, keepdims=True)
            p = jnp.exp2((s - m) * LOG2E)
            all_p = jnp.sum(p, axis=0, keepdims=True)
            o = dot(vt_ref[h * 64 : h * 64 + 64, :n], p.astype(BF16))
            outs.append(o / all_p)
            l_ref[0, h : h + 1] = m + jnp.log(all_p)
        result = jnp.concatenate(outs, 0).T.astype(BF16)
        for p in range(ups):

            @pl.when(up == p)
            def _(p=p):
                o_refs[2 * p][...] = result[:block]
                o_refs[2 * p + 1][...] = result[block:]

    if ups == 1:
        blocks = (length + keys - 1) // keys
        for i in range(4):
            pl.when(blocks == i + 1)(functools.partial(run, i + 1))
    else:
        run(4 * ups)


def attend(info, qkv):
    team = len(qkv)
    _, rows, lanes = qkv[0].shape
    span, pairs, ups = team * rows, lanes // 128, team // 2
    block = rows // 4

    def whole(which):
        return [pl.BlockSpec((None, rows, 128), lambda h, b, u, _: (which, 0, h))] * team

    return pl.pallas_call(
        functools.partial(attend_kernel, team=team),
        grid_spec=pltpu.PrefetchScalarGridSpec(
            num_scalar_prefetch=1,
            grid=(pairs, 4, ups),
            in_specs=[pl.BlockSpec((None, block, 128), lambda h, b, u, _: (0, b, h))] * team
            + whole(1)
            + whole(2),
            out_specs=[pl.BlockSpec((block, 128), lambda h, b, u, _: (b, h))] * team
            + [pl.BlockSpec((1, 2, 2 * block), lambda h, b, u, _: (h, 0, b * ups + u))],
            scratch_shapes=[pltpu.VMEM((128, span), BF16)],
        ),
        out_shape=[shape((rows, lanes), BF16)] * team + [shape((pairs, 2, span), F32)],
        compiler_params=params(),
        cost_estimate=cost(16 * span * span * lanes, 8 * span * lanes, span * span * lanes // 64),
        name="attend",
    )(info, *qkv, *qkv, *qkv)


def attend_back_kernel(info_ref, *refs, team):
    q_refs, k_refs, v_refs, o_refs, g_refs = (refs[i * team : (i + 1) * team] for i in range(5))
    l_ref, d_refs = refs[5 * team], refs[5 * team + 1 : 6 * team + 1]
    kt_ref, dk_ref, dv_ref = refs[6 * team + 1 :]
    length, side, upper = info_ref[0], info_ref[1], info_ref[2]
    lane = lax.broadcasted_iota(jnp.int32, (1, 128), 1)
    block = q_refs[0].shape[0]
    keys, ups = 2 * block, team // 2
    b, up = pl.program_id(1), pl.program_id(2)
    first = (4 * (upper ^ up) + b) * keys

    def chunk(arrays, p, c):
        rows = pl.ds(pl.multiple_of(c * block, block), block)
        return jnp.concatenate([arrays[2 * p][rows], arrays[2 * p + 1][rows]], axis=0)

    def queries(arrays):
        value = jnp.concatenate([arrays[0][...], arrays[1][...]], axis=0)
        for p in range(1, ups):
            other = jnp.concatenate([arrays[2 * p][...], arrays[2 * p + 1][...]], axis=0)
            value = jnp.where(up == p, other, value)
        return value

    @pl.when((b == 0) & (up == 0))
    def _():
        for p in range(ups):
            for c in range(4):
                at = (4 * p + c) * keys
                kt_ref[:, at : at + keys] = (chunk(k_refs, p, c) * BF16(0.125)).T
        dk_ref[...] = jnp.zeros_like(dk_ref)
        dv_ref[...] = jnp.zeros_like(dv_ref)

    here = pl.ds(pl.multiple_of(b * block, block), block)

    def put(value):
        for p in range(ups):

            @pl.when(up == p)
            def _(p=p):
                d_refs[2 * p][0, here] = value[:block]
                d_refs[2 * p + 1][0, here] = value[block:]

    @pl.when(first >= length)
    def _():
        put(jnp.zeros((keys, 128), BF16))

    @pl.when(first < length)
    def _():
        q2 = queries(q_refs) * BF16(0.125)
        g2 = queries(g_refs)
        products = (g2.astype(F32) * queries(o_refs).astype(F32)).T
        qs, gs, ls, ds = [], [], [], []
        for h in range(2):
            mine = (lane // 64) == h
            qs.append(jnp.where(mine, q2, BF16(0)))
            gs.append(jnp.where(mine, g2, BF16(0)))
            ls.append(l_ref[0, h : h + 1] * LOG2E)
            ds.append(jnp.sum(products[h * 64 : h * 64 + 64], axis=0, keepdims=True))
        qc = jnp.concatenate(qs, 0)
        gc = jnp.concatenate(gs, 0)
        lc = jnp.concatenate(ls, 1)
        dc = jnp.concatenate(ds, 1)
        acc = (jnp.zeros((64, keys), F32),) * 2
        for p in range(ups):
            start = 4 * (upper ^ p) * keys

            def step(c, acc, masked, p=p, start=start):
                sl = pl.ds(pl.multiple_of((4 * p + c) * keys, keys), keys)
                k2 = chunk(k_refs, p, c)
                v2 = chunk(v_refs, p, c)
                prob = jnp.exp2(dot(k2, qc, NT) * LOG2E - lc)
                if masked:
                    row = lax.broadcasted_iota(jnp.int32, (keys, 1), 0)
                    row = row ^ (side * block) | (start + c * keys)
                    prob = jnp.where(row < length, prob, 0.0)
                gp = dot(v2, gc, NT)
                gs_low = (prob * (gp - dc)).astype(BF16)
                dv_ref[sl] += dot(prob.astype(BF16), gc)
                dk_ref[sl] += dot(gs_low, qc)
                return tuple(
                    acc[h]
                    + dot(kt_ref[h * 64 : h * 64 + 64, sl], gs_low[:, h * keys : (h + 1) * keys])
                    for h in range(2)
                )

            valid = jnp.clip(length - start, 0, 4 * keys)
            full = valid // keys
            acc = lax.fori_loop(0, full, lambda c, a: step(c, a, False), acc)
            acc = lax.cond(
                full * keys < valid, lambda a: step(full, a, True), lambda a: a, acc
            )
        put(jnp.concatenate(acc, 0).T.astype(BF16))

    @pl.when((b == 3) & (up == ups - 1))
    def _():
        for p in range(ups):
            for c in range(4):
                at = (4 * p + c) * keys
                for t, ref in ((1, dk_ref), (2, dv_ref)):
                    for m in range(2):
                        rows = slice(c * block, (c + 1) * block)
                        piece = ref[at + m * block : at + (m + 1) * block]
                        d_refs[2 * p + m][t, rows] = piece.astype(BF16)


def attend_back(info, qkv, mixed, grad, lse, part):
    team = len(qkv)
    _, rows, lanes = qkv[0].shape
    span, pairs, ups = team * rows, lanes // 128 // PARTS, team // 2
    block = rows // 4
    spot = pl.BlockSpec((block, 128), lambda h, b, u, _: (b, part * pairs + h))

    def whole(which):
        return [
            pl.BlockSpec((None, rows, 128), lambda h, b, u, _: (which, 0, part * pairs + h))
        ] * team

    return pl.pallas_call(
        functools.partial(attend_back_kernel, team=team),
        grid_spec=pltpu.PrefetchScalarGridSpec(
            num_scalar_prefetch=1,
            grid=(pairs, 4, ups),
            in_specs=[
                pl.BlockSpec((None, block, 128), lambda h, b, u, _: (0, b, part * pairs + h))
            ]
            * team
            + whole(1)
            + whole(2)
            + [spot] * (2 * team)
            + [
                pl.BlockSpec(
                    (1, 2, 2 * block), lambda h, b, u, _: (part * pairs + h, 0, b * ups + u)
                )
            ],
            out_specs=[pl.BlockSpec((3, rows, 128), lambda h, b, u, _: (0, 0, h))] * team,
            scratch_shapes=[
                pltpu.VMEM((128, span), BF16),
                pltpu.VMEM((span, 128), F32),
                pltpu.VMEM((span, 128), F32),
            ],
        ),
        out_shape=[shape((3, rows, pairs * 128), BF16)] * team,
        compiler_params=params(),
        cost_estimate=cost(
            30 * span * span * pairs * 128, 16 * span * pairs * 128, 2 * span * span * pairs
        ),
        name="attend_back",
    )(info, *qkv, *qkv, *qkv, *mixed, *grad, lse)


def feed_kernel(
    at_ref, x_ref, cot_ref, scale_ref, vec_ref, wo_ref, wg_ref, wu_ref, wd_ref, *refs, team
):
    mix_refs, send_refs = refs[:team], refs[team : 2 * team]
    (
        delta_ref, gm_ref, gml_ref, n_ref, gl_ref, hid_ref, gg_ref, gu_ref, sum_ref, rows_ref,
        acc_ref, normal_ref, inv_ref,
    ) = refs[2 * team :]
    step = pl.program_id(1)
    lanes = mix_refs[0].shape[1]

    def whole(ref):
        return ref[...].reshape(-1, ref.shape[-1])

    def spot(m):
        return pl.ds(pl.multiple_of((at_ref[0] ^ m) * lanes, lanes), lanes)

    @pl.when(step == 0)
    def _():
        for m in range(team):
            rows_ref[:, spot(m)] = mix_refs[m][...]
        added = dot(rows_ref[...], whole(wo_ref))
        acc_ref[...] = added
        normal, inverse = normalise(x_ref[...].astype(F32) + added)
        normal_ref[...] = normal
        inv_ref[...] = inverse
        n_ref[...] = (normal * vec_ref[2:3] + vec_ref[3:4]).astype(BF16)
        gl_ref[...] = (cot_ref[...].astype(F32) * scale_ref[...]).astype(BF16)
        gm_ref[...] = jnp.zeros_like(gm_ref)

    wg, wu, wd = whole(wg_ref), whole(wu_ref), whole(wd_ref)
    normed = n_ref[...]
    gate = dot(normed, wg)
    upper = dot(normed, wu)
    sigma = jax.nn.sigmoid(gate)
    silu = gate * sigma
    hidden = (silu * upper).astype(BF16)
    hid_ref[...] = hidden
    grad_hidden = dot(gl_ref[...], wd, NT)
    grad_up = (grad_hidden * silu).astype(BF16)
    grad_gate = (grad_hidden * upper * sigma * (1.0 + gate * (1.0 - sigma))).astype(BF16)
    gu_ref[...] = grad_up
    gg_ref[...] = grad_gate
    acc_ref[...] += dot(hidden, wd)
    gm_ref[...] += dot(grad_gate, wg, NT) + dot(grad_up, wu, NT)

    @pl.when(step == pl.num_programs(1) - 1)
    def _():
        delta_ref[...] = acc_ref[...].astype(BF16)
        grad = gm_ref[...]
        normal = normal_ref[...]

        @pl.when(pl.program_id(0) == 0)
        def _():
            sum_ref[...] = jnp.zeros_like(sum_ref)

        sum_ref[0:1] += jnp.sum(grad * normal, axis=0, keepdims=True)
        sum_ref[1:2] += jnp.sum(grad, axis=0, keepdims=True)
        total_grad = cot_ref[...].astype(F32) * scale_ref[...] + norm_back(
            grad, normal, inv_ref[...], vec_ref[2:3]
        )
        gm_ref[...] = total_grad
        low = total_grad.astype(BF16)
        gml_ref[...] = low
        acc_ref[...] = dot(low, whole(wo_ref), NT)
        for m in range(team):
            send_refs[m][...] = acc_ref[:, spot(m)].astype(BF16)


def feed(at, tokens, cotangent, scale, mixed, vectors, weights):
    team = len(mixed)
    rows, width = tokens.shape
    lanes = width // team
    units = weights.shape[0]
    tall = 4 * ROW_UNIT
    ff = units * tall
    columns = width // FF_BLOCK
    each = min(FEED_ROWS, rows)
    const = pl.BlockSpec((each, width), lambda i, j, _: (i, 0))
    block = pl.BlockSpec((each, FF_BLOCK), lambda i, j, _: (i, j))
    mix = pl.BlockSpec((each, lanes), lambda i, j, _: (i, 0))

    def part(first):
        return pl.BlockSpec(
            (units, ROW_UNIT, FF_BLOCK), lambda i, j, _: (0, first + j // columns, j % columns)
        )

    return pl.pallas_call(
        functools.partial(feed_kernel, team=team),
        grid_spec=pltpu.PrefetchScalarGridSpec(
            num_scalar_prefetch=1,
            grid=(rows // each, ff // FF_BLOCK),
            in_specs=[
                const,
                const,
                pl.BlockSpec((each, 1), lambda i, j, _: (i, 0)),
                pl.BlockSpec((4, width), lambda i, j, _: (0, 0)),
                pl.BlockSpec((units, ROW_UNIT, width), lambda i, j, _: (0, 4, 0)),
                part(5),
                part(9),
                pl.BlockSpec((FF_BLOCK // tall, tall, width), lambda i, j, _: (j, 0, 0)),
            ]
            + [mix] * team,
            out_specs=[mix] * team
            + [const, const, const, const, const, block, block, block]
            + [pl.BlockSpec((2, width), lambda i, j, _: (0, 0)), const],
            scratch_shapes=[
                pltpu.VMEM((each, width), F32),
                pltpu.VMEM((each, width), F32),
                pltpu.VMEM((each, 1), F32),
            ],
        ),
        out_shape=[shape((rows, lanes), BF16)] * team
        + [
            shape((rows, width), BF16),
            shape((rows, width), F32),
            shape((rows, width), BF16),
            shape((rows, width), BF16),
            shape((rows, width), BF16),
            shape((rows, ff), BF16),
            shape((rows, ff), BF16),
            shape((rows, ff), BF16),
            shape((2, width), F32),
            shape((rows, width), BF16),
        ],
        compiler_params=params(),
        cost_estimate=cost(
            12 * rows * width * ff + 4 * rows * width * width,
            12 * width * ff + 6 * rows * ff + 30 * rows * width,
            rows * ff,
        ),
        name="feed",
    )(at, tokens, cotangent, scale, vectors, weights, weights, weights, weights, *mixed)


def weight_kernel(core_ref, a_ref, b_ref, own_ref, away_ref, at_ref, *, size):
    rows, tall = a_ref.shape
    core = core_ref[0]
    outs = (own_ref, away_ref)

    @pl.when(pl.program_id(1) == 0)
    def _():
        for side in range(2):
            half = core if side == 0 else 1 - core
            for c in range(tall // (2 * size)):
                start = pl.multiple_of((2 * c + half) * size, 128)
                at_ref[side, c * size : (c + 1) * size] = a_ref[:, pl.ds(start, size)].T

    wide = own_ref.shape[-1]
    for side in range(2):
        outs[side][...] = dot(at_ref[side], b_ref[...].reshape(rows, wide)).astype(BF16)


def weight_grad(core, a, b, chunk):
    rows, tall = a.shape
    stacked = b.ndim == 3
    wide = b.shape[0] * b.shape[2] if stacked else b.shape[1]
    if chunk < 128:
        a = a.reshape(rows, tall // (2 * chunk), 2, chunk).swapaxes(1, 2).reshape(rows, tall)
        chunk = tall // 2
    columns = b.shape[2] if stacked else min(1024, wide)
    block = max(1024, 2 * chunk)
    if stacked:
        right = pl.BlockSpec((1, rows, columns), lambda i, j, _: (j, 0, 0))
    else:
        right = pl.BlockSpec((rows, columns), lambda i, j, _: (0, j))
    out = pl.BlockSpec((block // 2, columns), lambda i, j, _: (i, j))
    return pl.pallas_call(
        functools.partial(weight_kernel, size=chunk),
        grid_spec=pltpu.PrefetchScalarGridSpec(
            num_scalar_prefetch=1,
            grid=(tall // block, wide // columns),
            in_specs=[pl.BlockSpec((rows, block), lambda i, j, _: (0, i)), right],
            out_specs=[out, out],
            scratch_shapes=[pltpu.VMEM((2, block // 2, rows), BF16)],
        ),
        out_shape=[shape((tall // 2, wide), BF16)] * 2,
        compiler_params=params(),
        cost_estimate=cost(2 * rows * tall * wide, 2 * (rows * tall + rows * wide + tall * wide)),
        name="weight_grad",
    )(core, a, b)


def unturn_kernel(at_ref, c_ref, e_ref, l_ref, *refs):
    blocks, out_ref = refs[:-1], refs[-1]
    cosine, early, late = c_ref[...], e_ref[...], l_ref[...]
    which = pl.program_id(0)
    lanes = blocks[0].shape[-1]
    for m, ref in enumerate(blocks):
        for at in range(0, lanes, 128):
            spot = pl.ds(pl.multiple_of((at_ref[0] ^ m) * lanes + at, 128), 128)

            @pl.when(which < 2)
            def _(ref=ref, at=at, spot=spot):
                piece = turn(ref[0, :, at : at + 128].astype(F32), cosine, -early, -late)
                out_ref[0, :, spot] = piece.astype(BF16)

            @pl.when(which == 2)
            def _(ref=ref, at=at, spot=spot):
                out_ref[0, :, spot] = ref[0, :, at : at + 128]


def unturn(at, blocks, table):
    _, rows, lanes = blocks[0].shape
    wide = pl.BlockSpec((rows, 128), lambda j, _: (0, 0))
    team = len(blocks)
    return pl.pallas_call(
        unturn_kernel,
        grid_spec=pltpu.PrefetchScalarGridSpec(
            num_scalar_prefetch=1,
            grid=(3,),
            in_specs=[wide] * 3 + [pl.BlockSpec((1, rows, lanes), lambda j, _: (j, 0, 0))] * team,
            out_specs=pl.BlockSpec((1, rows, team * lanes), lambda j, _: (j, 0, 0)),
        ),
        out_shape=shape((3, rows, team * lanes), BF16),
        compiler_params=params(),
        cost_estimate=cost(0, 12 * rows * team * lanes),
        name="unturn",
    )(at, *table, *blocks)


def project_back_kernel(x_ref, gm_ref, vec_ref, w_ref, low_ref, *refs, part, lanes, first, last):
    which = pl.program_id(0)
    acc_ref = refs[-1]

    @pl.when(which == 0)
    def _():
        acc_ref[...] = jnp.zeros_like(acc_ref) if first else refs[0][...]

    width = w_ref.shape[-1]
    weight = jnp.concatenate(
        [
            w_ref[0, :, at : at + lanes]
            for at in range(part * lanes, width, PARTS * lanes)
        ],
        axis=1,
    )
    acc_ref[...] += dot(low_ref[0], weight, NT)

    if last:
        out_ref, sum_ref = refs[-3:-1]

        @pl.when(which == 2)
        def _():
            grad = acc_ref[...]
            normal, inverse = normalise(x_ref[...].astype(F32))
            sum_ref[0:1] = jnp.sum(grad * normal, axis=0, keepdims=True)
            sum_ref[1:2] = jnp.sum(grad, axis=0, keepdims=True)
            grad = gm_ref[...] + norm_back(grad, normal, inverse, vec_ref[0:1])
            out_ref[...] = grad.astype(BF16)


def project_back(tokens, grad_middle, vectors, weights, low, part, team, partial):
    rows, width = tokens.shape
    wide = low.shape[-1]
    last = part == PARTS - 1
    const = pl.BlockSpec((rows, width), lambda j: (0, 0))
    return pl.pallas_call(
        functools.partial(
            project_back_kernel, part=part, lanes=wide // team, first=not partial, last=last
        ),
        grid=(3,),
        in_specs=[
            const,
            const,
            pl.BlockSpec((4, width), lambda j: (0, 0)),
            pl.BlockSpec((1, width, width), lambda j: (j, 0, 0)),
            pl.BlockSpec((1, rows, wide), lambda j: (j, 0, 0)),
        ]
        + [const] * len(partial),
        out_specs=[const, pl.BlockSpec((2, width), lambda j: (0, 0))] if last else [const],
        out_shape=(
            [shape((rows, width), BF16), shape((2, width), F32)]
            if last
            else [shape((rows, width), F32)]
        ),
        scratch_shapes=[pltpu.VMEM((rows, width), F32)] if last else [],
        compiler_params=params(),
        cost_estimate=cost(6 * rows * width * wide, 18 * rows * width + 6 * width * width),
        name="project_back",
    )(tokens, grad_middle, vectors, weights, low, *partial)


def place_kernel(me_ref, *refs, masks):
    count = len(masks)
    halves, (wide_ref, small_ref, sem) = refs[: 2 * count], refs[2 * count :]
    me = me_ref[0]
    for wait in (False, True):
        for t in range(count):
            half = len(masks[t]) // 2
            for j, mask in enumerate(masks[t]):
                source = halves[2 * t + j // half].at[j % half]
                place = wide_ref.at[t, me ^ mask] if t < count - 1 else small_ref.at[me ^ mask]
                copy = pltpu.make_async_copy(source, place, sem.at[t, j])
                copy.wait() if wait else copy.start()


class Chain:
    def __init__(self, links, own, away, rounds, wire=BF16):
        self.links, self.rounds, self.wire = links, [list(r) for r in rounds], wire
        self.axes = [b for b in range(links.bits - 1, -1, -1) if b != links.core]
        self.dims = (2,) * len(self.axes) + (own.shape[0] * 2 // links.count,) + own.shape[1:]
        self.terms = [own.reshape(self.dims), links.swap(away, 1 << links.core).reshape(self.dims)]

    def pick(self, mask):
        me, parts, axes = self.links.me() ^ mask, self.terms, list(self.axes)
        for bit in self.rounds[0]:
            at = axes.index(bit)
            parts = [
                lax.dynamic_index_in_dim(p, (me >> bit) & 1, at, keepdims=False) for p in parts
            ]
            axes.pop(at)
        return parts

    def split(self):
        self.masks = [0]
        for bit in self.rounds[0]:
            self.masks += [m | 1 << bit for m in self.masks]
        sent = [total(self.pick(m)).astype(self.wire) for m in self.masks[1:]]
        self.kept = self.pick(0)
        return sent

    def swap(self, sent):
        return [self.links.swap(v, m) for v, m in zip(sent, self.masks[1:])]

    def take(self, received):
        for bit in self.rounds.pop(0):
            self.axes.remove(bit)
        self.terms = self.kept + list(received)

    def result(self):
        return total(self.terms)


def total(terms):
    return functools.reduce(jnp.add, [t.astype(F32) for t in terms])


def tie(values, *others):
    return lax.optimization_barrier((values, others))[0]


def beside(chains, work, *values):
    chains = [c for c in chains if c.rounds]
    sent = [c.split() for c in chains]
    values, sent = lax.optimization_barrier((values, sent))
    received = [c.swap(v) for c, v in zip(chains, sent)]
    result = work(*values)
    for c, r in zip(chains, tie(received, jax.tree.leaves(result))):
        c.take(r)
    return result


class Links:
    def __init__(self, mesh):
        self.dp, self.seq = mesh.shape["dp"], mesh.shape["seq"]
        self.count = self.dp * self.seq
        self.bits = self.count.bit_length() - 1
        self.core = self.seq.bit_length() - 1
        seq_bits = list(range(self.core))
        dp_bits = list(range(self.core + 1, self.bits))
        self.dp_bits = [self.core] + dp_bits
        first, last = dp_bits[:1], dp_bits[1:]
        self.seq_first = [[seq_bits[0]], seq_bits[1:], dp_bits]
        self.seq_last = [[seq_bits[-1]], seq_bits[:-1], dp_bits]
        self.dp_first = [first, [seq_bits[0]], seq_bits[1:] + last]
        self.dp_last = [first, [seq_bits[-1]], seq_bits[:-1] + last]
        self.direct = [seq_bits, dp_bits]
        self.direct_back = [dp_bits, seq_bits]
        self.orders = [
            seq_bits + dp_bits,
            seq_bits[::-1] + dp_bits,
            dp_bits[:1] + seq_bits + dp_bits[1:],
            dp_bits[:1] + seq_bits[::-1] + dp_bits[1:],
        ]

        self.team_bits = [self.core] + seq_bits[2:]
        self.team = 2 ** len(self.team_bits)

    def bit(self, which):
        return (self.me() >> which) & 1

    def route(self, k):
        pairs = []
        for i in range(self.count):
            core, y, x = (i >> self.core) & 1, (i >> 1) & 1, i & 1
            rest = i & ~((1 << self.core) | 3)
            pairs.append((i, rest | (y ^ (k >> 1)) << self.core | core << 1 | (x ^ (k & 1))))
        return pairs

    def to_team(self, value):
        wins, rows, width = value.shape
        blocks = value.reshape(wins * 2, rows // 2, width)
        place = 2 * self.bit(0) + self.bit(1)
        received = []
        for k in range(4):
            away = lax.dynamic_index_in_dim(
                blocks, place ^ (2 * (k & 1) + (k >> 1)), 0, keepdims=False
            )
            received.append(lax.ppermute(away, BOTH, self.route(k)))
        return received

    def from_team(self, value):
        rows, width = value.shape
        blocks = value.reshape(4, rows // 4, width)
        base = self.base()
        received = []
        for k in range(4):
            away = lax.dynamic_index_in_dim(blocks, base ^ k, 0, keepdims=False)
            back = [(j, i) for i, j in self.route(k)]
            received.append(lax.ppermute(away, BOTH, back))
        return [received[k] for k in (0, 2, 1, 3)]

    def base(self):
        return 2 * self.bit(self.core) + self.bit(0)

    def member(self):
        return sum(self.bit(b) << i for i, b in enumerate(self.team_bits))

    def exchange(self, values):
        masks = [
            sum(1 << b for i, b in enumerate(self.team_bits) if m >> i & 1)
            for m in range(self.team)
        ]
        return [v if m == 0 else self.swap(v, masks[m]) for m, v in enumerate(values)]

    def me(self):
        return lax.axis_index("dp") * self.seq + lax.axis_index("seq")

    def swap(self, value, mask):
        return lax.ppermute(value, BOTH, [(i, i ^ mask) for i in range(self.count)])

    def chip_sum(self, own, away):
        both = total([own, self.swap(away, 1 << self.core)]).astype(BF16)
        groups = [
            [d * self.seq + s for d in range(c, self.dp, 2) for s in range(self.seq)]
            for c in range(2)
        ]
        summed = lax.psum_scatter(
            both, BOTH, scatter_dimension=0, axis_index_groups=groups, tiled=True
        )
        return summed.astype(F32)

    def own(self):
        return jnp.reshape(lax.axis_index("dp") % 2, (1,))

    def gather(self, values, orders):
        args, masks, early = [], [], []
        for value, order in zip(values, orders):
            order = order[::-1] + [self.core]
            held, mask = value[None], [0]
            for bit in order:
                got = self.swap(held, 1 << bit)
                if bit == order[-3]:
                    early.append(got)
                mask = mask + [m | 1 << bit for m in mask]
                if bit == self.core:
                    args += [held, got]
                else:
                    held = jnp.concatenate([held, got], axis=0)
            masks.append(mask)
        wide = (len(values) - 1, self.count) + values[0].shape
        narrow = (self.count,) + values[-1].shape
        placed = pl.pallas_call(
            functools.partial(place_kernel, masks=masks),
            grid_spec=pltpu.PrefetchScalarGridSpec(
                num_scalar_prefetch=1,
                grid=(1,),
                in_specs=[pl.BlockSpec(memory_space=pl.ANY)] * len(args),
                out_specs=[
                    pl.BlockSpec(wide, lambda i, _: (0, 0, 0, 0)),
                    pl.BlockSpec(narrow, lambda i, _: (0, 0, 0)),
                ],
                scratch_shapes=[pltpu.SemaphoreType.DMA((len(values), self.count))],
            ),
            out_shape=[shape(wide, BF16), shape(narrow, BF16)],
            compiler_params=params(),
            name="place",
        )(jnp.reshape(self.me(), (1,)), *args)
        return placed, early

    def window_sum(self, value):
        for bit in self.dp_bits:
            value = value + self.swap(value, 1 << bit)
        return value


def packed(w_down, w_out, w_gate, w_up, width):
    parts = [w_down, w_out]
    for weight in (w_gate, w_up):
        parts += [weight[:, c : c + width] for c in range(0, weight.shape[1], width)]
    return jnp.concatenate(parts, axis=0)


def regrouped(gathered, each, width):
    if each == ROW_UNIT:
        return gathered
    tall = 4 * each
    down = gathered[:, :tall].reshape(-1, 4 * ROW_UNIT, width)
    parts = [down]
    for at in range(tall, gathered.shape[1], each):
        parts.append(gathered[:, at : at + each].reshape(-1, ROW_UNIT, width))
    return jnp.concatenate(parts, axis=1)


def body(
    links,
    tokens,
    cotangent,
    lengths,
    species,
    ln1_gain,
    ln1_bias,
    w_query,
    w_key,
    w_value,
    w_out,
    ln2_gain,
    ln2_bias,
    w_gate,
    w_up,
    w_down,
):
    wins, rows, width = tokens.shape
    each = w_query.shape[0]
    team = links.team
    lanes = width // team
    share = wins * rows
    scalar = functools.partial(jnp.reshape, shape=(1,))
    member = links.member()
    base = scalar(links.base())

    small = jnp.stack([ln1_gain, ln1_bias, ln2_gain, ln2_bias], axis=1)
    small = jnp.pad(small, ((0, 0), (0, 124)))
    local = [w_query, w_key, w_value, small]
    moved = links.to_team(tokens)
    told = jnp.stack([lengths, species])
    told = jnp.stack([told, links.swap(told, 1 << links.core)])
    (qkv_w, small), early = links.gather(local, links.orders)
    mine = tie(packed(w_down, w_out, w_gate, w_up, width), early)
    weights = regrouped(lax.all_gather(mine, BOTH, axis=0), each, width)
    qkv_w = qkv_w.reshape(3, width, width)
    vectors = small.reshape(width, 128)[:, :4].T.astype(F32)

    told = lax.dynamic_index_in_dim(told, links.bit(1) ^ links.bit(links.core), 0, keepdims=False)
    told = lax.dynamic_index_in_dim(told, links.bit(0), 1, keepdims=False)
    length, kind = told[0], told[1]
    upper = member >> 1
    half = rows // 2
    block = (4 * upper + jnp.arange(4))[:, None] * rows + links.bit(links.core) * half
    positions = (block + jnp.arange(half)[None, :]).reshape(share)
    table = tables(positions)
    info = jnp.stack([length, member & 1, upper])

    rows_in = arrange(base, moved)
    projected = []
    for m in range(team)[::-1]:
        projected.append(project(scalar(member ^ m), rows_in, qkv_w, vectors, table, lanes))
    projected = projected[::-1]
    normed_one = projected[0][1]
    cot_moved = links.to_team(tie(cotangent, [p[0] for p in projected[1:]]))
    species_ids = jnp.arange(SPECIES)
    onehot = (species[:, None] == species_ids[None, :]).astype(F32)
    counts = jnp.sum(onehot * lengths[:, None].astype(F32), axis=0)
    counts = links.window_sum(tie(counts, projected[-1][0]))
    window_weight = SPECIES * jnp.sum((kind == species_ids) * counts) / jnp.sum(counts)
    row_scale = jnp.where(positions < length, window_weight, 0.0)[:, None]

    qkv = links.exchange([p[0] for p in projected])
    *mixed_heads, lse = attend(info, qkv)
    mixed = links.exchange(mixed_heads)
    cot_in = arrange(base, cot_moved)
    fed = feed(scalar(member), rows_in, cot_in, row_scale, mixed, vectors, weights)
    grad_mixed = fed[:team]
    (
        delta, grad_middle, grad_middle_low, normed_two, grad_low, hidden, grad_gate, grad_up,
        sums_two, mixed_rows,
    ) = fed[team:]
    grad_heads = links.exchange(grad_mixed)

    narrow, broad = width // links.dp, hidden.shape[1] // links.dp
    core = links.own()
    terms = [
        (hidden, grad_low, broad, links.dp_first),
        (normed_two, grad_gate, narrow, links.seq_first),
        (normed_two, grad_up, narrow, links.seq_last),
        (mixed_rows, grad_middle_low, narrow, links.dp_last),
    ]
    chains = [Chain(links, *weight_grad(core, *t[:3]), t[3]) for t in terms]
    sum_down, sum_gate, sum_up, sum_out = chains

    blocks, made = [], []
    for part in range(PARTS):
        made = beside(
            chains, lambda *g: attend_back(info, qkv, mixed_heads, g, lse, part), *grad_heads
        )
        grad_heads = tie(list(grad_heads), made)
        blocks.append(links.exchange(made))
    returned = links.from_team(tie(delta, made))

    sums, partial, fresh = [], [], []
    for part in range(PARTS):

        def through(value):
            return project_back(
                rows_in, grad_middle, vectors, qkv_w, value, part, team, partial
            )

        def weigh(*received):
            low = unturn(scalar(member), received, table)
            return (low,) + tuple(weight_grad(core, normed_one, low, narrow))

        if part < PARTS - 1:
            low, own, away = weigh(*tie(blocks[part], made))
            fresh = [Chain(links, own, away, links.direct_back)]
            sums.append(fresh)
            partial = beside(chains, through, tie(low, own))
            chains = chains + fresh
        else:
            low, own, away = beside(chains, weigh, *tie(blocks[part], partial))
            half = own.shape[1] // 2
            fresh = [
                Chain(links, own[:, :half], away[:, :half], links.direct),
                Chain(links, own[:, half:], away[:, half:], links.direct),
            ]
            sums.append(fresh)
            grad_in, sums_one = beside(chains, through, tie(low, own))
            chains = chains + fresh

    home = links.from_team(grad_in)
    place = scalar(2 * links.bit(0) + links.bit(1))
    gains = jnp.concatenate([sums_one, sums_two], axis=0)
    gains = gains.reshape(4, links.dp // 2, 2, links.seq, each).transpose(2, 1, 3, 0, 4)
    gains = gains.reshape(2, links.count // 2 * 4, each)
    own, away = (
        lax.dynamic_index_in_dim(gains, c, 0, keepdims=False) for c in (core[0], 1 - core[0])
    )
    gains = Chain(links, own, away, links.direct, F32)
    output = settle(place, tie(returned, sums_one), [tokens])
    chains = chains + [gains]
    while any(c.rounds for c in chains):
        beside(chains, lambda: [])
    grad_tokens = settle(place, home, [])

    merged = [jnp.concatenate([c.result() for c in s], axis=1) for s in sums]
    merged = jnp.concatenate([m.reshape(each, 3, team, 1, -1) for m in merged], axis=3)
    merged = merged.reshape(each, 3, width)
    gains = gains.result()
    return (
        output.reshape(wins, rows, width),
        grad_tokens.reshape(wins, rows, width),
        gains[0],
        gains[1],
        merged[:, 0],
        merged[:, 1],
        merged[:, 2],
        sum_out.result(),
        gains[2],
        gains[3],
        sum_gate.result(),
        sum_up.result(),
        sum_down.result(),
    )


def solution(mesh):
    token = P("dp", "seq", None)
    vector = P(BOTH)
    matrix = P(BOTH, None)
    return jax.shard_map(
        functools.partial(body, Links(mesh)),
        mesh=mesh,
        in_specs=(
            (token, token, P("dp"), P("dp"), vector, vector)
            + (matrix,) * 4
            + (vector, vector)
            + (matrix,) * 3
        ),
        out_specs=(
            (token, token, vector, vector) + (matrix,) * 4 + (vector, vector) + (matrix,) * 3
        ),
        check_vma=False,
    )
```

```python
import functools

import jax
import jax.numpy as jnp
from jax import lax
from jax.experimental import pallas as pl
from jax.experimental.pallas import tpu as pltpu
from jax.sharding import PartitionSpec as P

HEAD_DIM = 64
SPECIES = 8
EPS = 1e-05
LOG2E = 1.4426950408889634
BOTH = ("dp", "seq")
F32 = jnp.float32
BF16 = jnp.bfloat16
FF_BLOCK = 512
FEED_ROWS = 512
PARTS = 2
ROW_UNIT = 32
VMEM = 60 * 2**20

NN = (((1,), (0,)), ((), ()))
NT = (((1,), (1,)), ((), ()))


def dot(a, b, dims=NN):
    return lax.dot_general(a, b, dims, preferred_element_type=F32)


def shape(dims, dtype):
    return jax.ShapeDtypeStruct(dims, dtype)


def params():
    return pltpu.CompilerParams(vmem_limit_bytes=VMEM)


def cost(flops, moved, exps=0):
    return pl.CostEstimate(flops=flops // 64, bytes_accessed=moved // 64, transcendentals=exps // 64)


def normalise(value):
    centered = value - jnp.mean(value, axis=-1, keepdims=True)
    inverse = lax.rsqrt(jnp.mean(centered * centered, axis=-1, keepdims=True) + EPS)
    return centered * inverse, inverse


def norm_back(grad, normal, inverse, gain):
    scaled = grad * gain
    centered = scaled - jnp.mean(scaled, axis=-1, keepdims=True)
    return inverse * (centered - normal * jnp.mean(scaled * normal, axis=-1, keepdims=True))


def turn(value, cosine, early, late):
    return value * cosine + pltpu.roll(value, 96, 1) * early + pltpu.roll(value, 32, 1) * late


def tables(positions):
    half = HEAD_DIM // 2
    freq = 10000.0 ** (-2.0 * jnp.arange(half, dtype=F32) / HEAD_DIM)
    angle = positions.astype(F32)[:, None] * freq[None, :]
    cosine, sine = jnp.cos(angle), jnp.sin(angle)
    zero = jnp.zeros_like(sine)
    return (
        jnp.concatenate([cosine] * 4, axis=1),
        jnp.concatenate([-sine, zero, -sine, zero], axis=1),
        jnp.concatenate([zero, sine, zero, sine], axis=1),
    )


def arrange_kernel(base_ref, *refs):
    for k, ref in enumerate(refs[:-1]):
        refs[-1][base_ref[0] ^ k] = ref[...]


def arrange(base, blocks):
    rows, width = blocks[0].shape
    return pl.pallas_call(
        arrange_kernel,
        grid_spec=pltpu.PrefetchScalarGridSpec(
            num_scalar_prefetch=1,
            grid=(1,),
            in_specs=[pl.BlockSpec((rows, width), lambda i, _: (0, 0))] * len(blocks),
            out_specs=pl.BlockSpec((len(blocks), rows, width), lambda i, _: (0, 0, 0)),
        ),
        out_shape=shape((len(blocks), rows, width), blocks[0].dtype),
        compiler_params=params(),
        cost_estimate=cost(0, 16 * rows * width),
        name="arrange",
    )(base, *blocks).reshape(len(blocks) * rows, width)


def settle_kernel(base_ref, *refs):
    blocks, added, out_ref = refs[:4], refs[4:-1], refs[-1]
    here = pl.program_id(0)

    for k, ref in enumerate(blocks):

        @pl.when((base_ref[0] ^ k) == here)
        def _(ref=ref):
            value = ref[...].astype(F32)
            out_ref[0] = value + added[0][0].astype(F32) if added else value


def settle(base, blocks, added):
    rows, width = blocks[0].shape
    block = pl.BlockSpec((1, rows, width), lambda i, _: (i, 0, 0))
    return pl.pallas_call(
        settle_kernel,
        grid_spec=pltpu.PrefetchScalarGridSpec(
            num_scalar_prefetch=1,
            grid=(4,),
            in_specs=[pl.BlockSpec((rows, width), lambda i, _: (0, 0))] * 4
            + [block] * len(added),
            out_specs=block,
        ),
        out_shape=shape((4, rows, width), F32),
        compiler_params=params(),
        cost_estimate=cost(0, 32 * rows * width),
        name="settle",
    )(base, *blocks, *[a.reshape(4, rows, width) for a in added])


def project_kernel(at_ref, x_ref, w_ref, vec_ref, c_ref, e_ref, l_ref, send_ref, n_ref):
    which = pl.program_id(0)
    _, rows, lanes = send_ref.shape

    @pl.when(which == 0)
    def _():
        normal, _ = normalise(x_ref[...].astype(F32))
        n_ref[...] = (normal * vec_ref[0:1] + vec_ref[1:2]).astype(BF16)

    product = dot(n_ref[...], w_ref[0])
    cosine, early, late = c_ref[...], e_ref[...], l_ref[...]

    def put(rotate):
        for at in range(0, lanes, 128):
            piece = product[:, at : at + 128]
            if rotate:
                piece = turn(piece, cosine, early, late)
            send_ref[0, :, at : at + 128] = piece.astype(BF16)

    pl.when(which < 2)(lambda: put(True))
    pl.when(which == 2)(lambda: put(False))


def project(at, tokens, weights, vectors, table, lanes):
    rows, width = tokens.shape
    wide = pl.BlockSpec((rows, 128), lambda j, _: (0, 0))
    return pl.pallas_call(
        project_kernel,
        grid_spec=pltpu.PrefetchScalarGridSpec(
            num_scalar_prefetch=1,
            grid=(3,),
            in_specs=[
                pl.BlockSpec((rows, width), lambda j, _: (0, 0)),
                pl.BlockSpec((1, width, lanes), lambda j, at: (j, 0, at[0])),
                pl.BlockSpec((4, width), lambda j, _: (0, 0)),
                wide,
                wide,
                wide,
            ],
            out_specs=[
                pl.BlockSpec((1, rows, lanes), lambda j, _: (j, 0, 0)),
                pl.BlockSpec((rows, width), lambda j, _: (0, 0)),
            ],
        ),
        out_shape=[shape((3, rows, lanes), BF16), shape((rows, width), BF16)],
        compiler_params=params(),
        cost_estimate=cost(6 * rows * width * lanes, 6 * rows * lanes + 6 * width * lanes),
        name="project",
    )(at, tokens, weights, vectors, *table)


def attend_kernel(info_ref, *refs, team):
    q_refs, k_refs, v_refs = refs[:team], refs[team : 2 * team], refs[2 * team : 3 * team]
    o_refs, (l_ref, vt_ref) = refs[3 * team : 4 * team], refs[4 * team :]
    length, side, upper = info_ref[0], info_ref[1], info_ref[2]
    lane = lax.broadcasted_iota(jnp.int32, (1, 128), 1)
    block = q_refs[0].shape[0]
    keys, ups = 2 * block, team // 2
    up = pl.program_id(2)

    def chunk(arrays, p, b):
        rows = slice(b * block, (b + 1) * block)
        return jnp.concatenate([arrays[2 * p][rows], arrays[2 * p + 1][rows]], axis=0)

    @pl.when((pl.program_id(1) == 0) & (up == 0))
    def _():
        for p in range(ups):
            for b in range(4):
                at = (4 * p + b) * keys
                vt_ref[:, at : at + keys] = chunk(v_refs, p, b).T

    q2 = jnp.concatenate([q_refs[0][...], q_refs[1][...]], axis=0)
    for p in range(1, ups):
        other = jnp.concatenate([q_refs[2 * p][...], q_refs[2 * p + 1][...]], axis=0)
        q2 = jnp.where(up == p, other, q2)
    q2 = q2 * BF16(0.125)

    def positions(p, b):
        row = lax.broadcasted_iota(jnp.int32, (keys, keys), 0)
        return row ^ (side * block) | (4 * (upper ^ p) + b) * keys

    def run(chunks):
        k2 = jnp.concatenate([chunk(k_refs, c // 4, c % 4) for c in range(chunks)], axis=0)
        n = chunks * keys
        outs = []
        for h in range(2):
            qh = jnp.where((lane // 64) == h, q2, BF16(0))
            s = dot(k2, qh, NT)
            if ups == 1:
                last = jnp.where(positions(0, chunks - 1) < length, s[n - keys :], -1e30)
                s = jnp.concatenate([s[: n - keys], last], 0) if chunks > 1 else last
            else:
                valid = [positions(c // 4, c % 4) < length for c in range(chunks)]
                s = jnp.concatenate(
                    [jnp.where(v, s[c * keys : (c + 1) * keys], -1e30) for c, v in enumerate(valid)],
                    axis=0,
                )
            m = jnp.max(s, axis=0, keepdims=True)
            p = jnp.exp2((s - m) * LOG2E)
            all_p = jnp.sum(p, axis=0, keepdims=True)
            o = dot(vt_ref[h * 64 : h * 64 + 64, :n], p.astype(BF16))
            outs.append(o / all_p)
            l_ref[0, h : h + 1] = m + jnp.log(all_p)
        result = jnp.concatenate(outs, 0).T.astype(BF16)
        for p in range(ups):

            @pl.when(up == p)
            def _(p=p):
                o_refs[2 * p][...] = result[:block]
                o_refs[2 * p + 1][...] = result[block:]

    if ups == 1:
        blocks = (length + keys - 1) // keys
        for i in range(4):
            pl.when(blocks == i + 1)(functools.partial(run, i + 1))
    else:
        run(4 * ups)


def attend(info, qkv, part):
    team = len(qkv)
    _, rows, lanes = qkv[0].shape
    span, pairs, ups = team * rows, lanes // 128 // PARTS, team // 2
    block = rows // 4

    def whole(which):
        return [
            pl.BlockSpec((None, rows, 128), lambda h, b, u, _: (which, 0, part * pairs + h))
        ] * team

    return pl.pallas_call(
        functools.partial(attend_kernel, team=team),
        grid_spec=pltpu.PrefetchScalarGridSpec(
            num_scalar_prefetch=1,
            grid=(pairs, 4, ups),
            in_specs=[
                pl.BlockSpec((None, block, 128), lambda h, b, u, _: (0, b, part * pairs + h))
            ]
            * team
            + whole(1)
            + whole(2),
            out_specs=[pl.BlockSpec((block, 128), lambda h, b, u, _: (b, h))] * team
            + [pl.BlockSpec((1, 2, 2 * block), lambda h, b, u, _: (h, 0, b * ups + u))],
            scratch_shapes=[pltpu.VMEM((128, span), BF16)],
        ),
        out_shape=[shape((rows, pairs * 128), BF16)] * team + [shape((pairs, 2, span), F32)],
        compiler_params=params(),
        cost_estimate=cost(
            16 * span * span * pairs * 128, 8 * span * pairs * 128, 2 * span * span * pairs
        ),
        name="attend",
    )(info, *qkv, *qkv, *qkv)


def attend_back_kernel(info_ref, *refs, team):
    q_refs, k_refs, v_refs, o_refs, g_refs = (refs[i * team : (i + 1) * team] for i in range(5))
    l_ref, d_refs = refs[5 * team], refs[5 * team + 1 : 6 * team + 1]
    kt_ref, dk_ref, dv_ref = refs[6 * team + 1 :]
    length, side, upper = info_ref[0], info_ref[1], info_ref[2]
    lane = lax.broadcasted_iota(jnp.int32, (1, 128), 1)
    block = q_refs[0].shape[0]
    keys, ups = 2 * block, team // 2
    b, up = pl.program_id(1), pl.program_id(2)
    first = (4 * (upper ^ up) + b) * keys

    def chunk(arrays, p, c):
        rows = pl.ds(pl.multiple_of(c * block, block), block)
        return jnp.concatenate([arrays[2 * p][rows], arrays[2 * p + 1][rows]], axis=0)

    def queries(arrays):
        value = jnp.concatenate([arrays[0][...], arrays[1][...]], axis=0)
        for p in range(1, ups):
            other = jnp.concatenate([arrays[2 * p][...], arrays[2 * p + 1][...]], axis=0)
            value = jnp.where(up == p, other, value)
        return value

    @pl.when((b == 0) & (up == 0))
    def _():
        for p in range(ups):
            for c in range(4):
                at = (4 * p + c) * keys
                kt_ref[:, at : at + keys] = (chunk(k_refs, p, c) * BF16(0.125)).T
        dk_ref[...] = jnp.zeros_like(dk_ref)
        dv_ref[...] = jnp.zeros_like(dv_ref)

    here = pl.ds(pl.multiple_of(b * block, block), block)

    def put(value):
        for p in range(ups):

            @pl.when(up == p)
            def _(p=p):
                d_refs[2 * p][0, here] = value[:block]
                d_refs[2 * p + 1][0, here] = value[block:]

    @pl.when(first >= length)
    def _():
        put(jnp.zeros((keys, 128), BF16))

    @pl.when(first < length)
    def _():
        q2 = queries(q_refs) * BF16(0.125)
        g2 = queries(g_refs)
        products = (g2.astype(F32) * queries(o_refs).astype(F32)).T
        qs, gs, ls, ds = [], [], [], []
        for h in range(2):
            mine = (lane // 64) == h
            qs.append(jnp.where(mine, q2, BF16(0)))
            gs.append(jnp.where(mine, g2, BF16(0)))
            ls.append(l_ref[0, h : h + 1] * LOG2E)
            ds.append(jnp.sum(products[h * 64 : h * 64 + 64], axis=0, keepdims=True))
        qc = jnp.concatenate(qs, 0)
        gc = jnp.concatenate(gs, 0)
        lc = jnp.concatenate(ls, 1)
        dc = jnp.concatenate(ds, 1)
        acc = (jnp.zeros((64, keys), F32),) * 2
        for p in range(ups):
            start = 4 * (upper ^ p) * keys

            def step(c, acc, masked, p=p, start=start):
                sl = pl.ds(pl.multiple_of((4 * p + c) * keys, keys), keys)
                k2 = chunk(k_refs, p, c)
                v2 = chunk(v_refs, p, c)
                prob = jnp.exp2(dot(k2, qc, NT) * LOG2E - lc)
                if masked:
                    row = lax.broadcasted_iota(jnp.int32, (keys, 1), 0)
                    row = row ^ (side * block) | (start + c * keys)
                    prob = jnp.where(row < length, prob, 0.0)
                gp = dot(v2, gc, NT)
                gs_low = (prob * (gp - dc)).astype(BF16)
                dv_ref[sl] += dot(prob.astype(BF16), gc)
                dk_ref[sl] += dot(gs_low, qc)
                return tuple(
                    acc[h]
                    + dot(kt_ref[h * 64 : h * 64 + 64, sl], gs_low[:, h * keys : (h + 1) * keys])
                    for h in range(2)
                )

            valid = jnp.clip(length - start, 0, 4 * keys)
            full = valid // keys
            acc = lax.fori_loop(0, full, lambda c, a: step(c, a, False), acc)
            acc = lax.cond(
                full * keys < valid, lambda a: step(full, a, True), lambda a: a, acc
            )
        put(jnp.concatenate(acc, 0).T.astype(BF16))

    @pl.when((b == 3) & (up == ups - 1))
    def _():
        for p in range(ups):
            for c in range(4):
                at = (4 * p + c) * keys
                for t, ref in ((1, dk_ref), (2, dv_ref)):
                    for m in range(2):
                        rows = slice(c * block, (c + 1) * block)
                        piece = ref[at + m * block : at + (m + 1) * block]
                        d_refs[2 * p + m][t, rows] = piece.astype(BF16)


def attend_back(info, qkv, mixed, grad, lse, part, sub, subs):
    team = len(qkv)
    _, rows, lanes = qkv[0].shape
    span, pairs, ups = team * rows, lanes // 128 // PARTS // subs, team // 2
    start, near = (part * subs + sub) * pairs, sub * pairs
    block = rows // 4
    spot = pl.BlockSpec((block, 128), lambda h, b, u, _: (b, start + h))

    def whole(which):
        return [
            pl.BlockSpec((None, rows, 128), lambda h, b, u, _: (which, 0, start + h))
        ] * team

    return pl.pallas_call(
        functools.partial(attend_back_kernel, team=team),
        grid_spec=pltpu.PrefetchScalarGridSpec(
            num_scalar_prefetch=1,
            grid=(pairs, 4, ups),
            in_specs=[
                pl.BlockSpec((None, block, 128), lambda h, b, u, _: (0, b, start + h))
            ]
            * team
            + whole(1)
            + whole(2)
            + [pl.BlockSpec((block, 128), lambda h, b, u, _: (b, near + h))] * team
            + [spot] * team
            + [pl.BlockSpec((1, 2, 2 * block), lambda h, b, u, _: (near + h, 0, b * ups + u))],
            out_specs=[pl.BlockSpec((3, rows, 128), lambda h, b, u, _: (0, 0, h))] * team,
            scratch_shapes=[
                pltpu.VMEM((128, span), BF16),
                pltpu.VMEM((span, 128), F32),
                pltpu.VMEM((span, 128), F32),
            ],
        ),
        out_shape=[shape((3, rows, pairs * 128), BF16)] * team,
        compiler_params=params(),
        cost_estimate=cost(
            30 * span * span * pairs * 128, 16 * span * pairs * 128, 2 * span * span * pairs
        ),
        name="attend_back",
    )(info, *qkv, *qkv, *qkv, *mixed, *grad, lse)


def feed_kernel(
    at_ref, x_ref, cot_ref, scale_ref, vec_ref, wo_ref, wg_ref, wu_ref, wd_ref, *refs, team
):
    mix_refs, send_refs = refs[: team * PARTS], refs[team * PARTS : team * (PARTS + 1)]
    (
        delta_ref, gm_ref, gml_ref, n_ref, gl_ref, hid_ref, gg_ref, gu_ref, sum_ref, rows_ref,
        acc_ref, normal_ref, inv_ref,
    ) = refs[team * (PARTS + 1) :]
    step = pl.program_id(1)
    lanes = send_refs[0].shape[1]
    some = mix_refs[0].shape[1]

    def whole(ref):
        return ref[...].reshape(-1, ref.shape[-1])

    def spot(m, first, size):
        return pl.ds(pl.multiple_of((at_ref[0] ^ m) * lanes + first, size), size)

    @pl.when(step == 0)
    def _():
        for i, ref in enumerate(mix_refs):
            rows_ref[:, spot(i % team, i // team * some, some)] = ref[...]
        added = dot(rows_ref[...], whole(wo_ref))
        acc_ref[...] = added
        normal, inverse = normalise(x_ref[...].astype(F32) + added)
        normal_ref[...] = normal
        inv_ref[...] = inverse
        n_ref[...] = (normal * vec_ref[2:3] + vec_ref[3:4]).astype(BF16)
        gl_ref[...] = (cot_ref[...].astype(F32) * scale_ref[...]).astype(BF16)
        gm_ref[...] = jnp.zeros_like(gm_ref)

    wg, wu, wd = whole(wg_ref), whole(wu_ref), whole(wd_ref)
    normed = n_ref[...]
    gate = dot(normed, wg)
    upper = dot(normed, wu)
    sigma = jax.nn.sigmoid(gate)
    silu = gate * sigma
    hidden = (silu * upper).astype(BF16)
    hid_ref[...] = hidden
    grad_hidden = dot(gl_ref[...], wd, NT)
    grad_up = (grad_hidden * silu).astype(BF16)
    grad_gate = (grad_hidden * upper * sigma * (1.0 + gate * (1.0 - sigma))).astype(BF16)
    gu_ref[...] = grad_up
    gg_ref[...] = grad_gate
    acc_ref[...] += dot(hidden, wd)
    gm_ref[...] += dot(grad_gate, wg, NT) + dot(grad_up, wu, NT)

    @pl.when(step == pl.num_programs(1) - 1)
    def _():
        delta_ref[...] = acc_ref[...].astype(BF16)
        grad = gm_ref[...]
        normal = normal_ref[...]

        @pl.when(pl.program_id(0) == 0)
        def _():
            sum_ref[...] = jnp.zeros_like(sum_ref)

        sum_ref[0:1] += jnp.sum(grad * normal, axis=0, keepdims=True)
        sum_ref[1:2] += jnp.sum(grad, axis=0, keepdims=True)
        total_grad = cot_ref[...].astype(F32) * scale_ref[...] + norm_back(
            grad, normal, inv_ref[...], vec_ref[2:3]
        )
        gm_ref[...] = total_grad
        low = total_grad.astype(BF16)
        gml_ref[...] = low
        acc_ref[...] = dot(low, whole(wo_ref), NT)
        for m in range(team):
            send_refs[m][...] = acc_ref[:, spot(m, 0, lanes)].astype(BF16)


def feed(at, tokens, cotangent, scale, mixed, vectors, weights):
    team = len(mixed) // PARTS
    rows, width = tokens.shape
    lanes = width // team
    units = weights.shape[0]
    tall = 4 * ROW_UNIT
    ff = units * tall
    columns = width // FF_BLOCK
    each = min(FEED_ROWS, rows)
    const = pl.BlockSpec((each, width), lambda i, j, _: (i, 0))
    block = pl.BlockSpec((each, FF_BLOCK), lambda i, j, _: (i, j))
    mix = pl.BlockSpec((each, lanes), lambda i, j, _: (i, 0))

    def part(first):
        return pl.BlockSpec(
            (units, ROW_UNIT, FF_BLOCK), lambda i, j, _: (0, first + j // columns, j % columns)
        )

    return pl.pallas_call(
        functools.partial(feed_kernel, team=team),
        grid_spec=pltpu.PrefetchScalarGridSpec(
            num_scalar_prefetch=1,
            grid=(rows // each, ff // FF_BLOCK),
            in_specs=[
                const,
                const,
                pl.BlockSpec((each, 1), lambda i, j, _: (i, 0)),
                pl.BlockSpec((4, width), lambda i, j, _: (0, 0)),
                pl.BlockSpec((units, ROW_UNIT, width), lambda i, j, _: (0, 4, 0)),
                part(5),
                part(9),
                pl.BlockSpec((FF_BLOCK // tall, tall, width), lambda i, j, _: (j, 0, 0)),
            ]
            + [pl.BlockSpec((each, lanes // PARTS), lambda i, j, _: (i, 0))] * len(mixed),
            out_specs=[mix] * team
            + [const, const, const, const, const, block, block, block]
            + [pl.BlockSpec((2, width), lambda i, j, _: (0, 0)), const],
            scratch_shapes=[
                pltpu.VMEM((each, width), F32),
                pltpu.VMEM((each, width), F32),
                pltpu.VMEM((each, 1), F32),
            ],
        ),
        out_shape=[shape((rows, lanes), BF16)] * team
        + [
            shape((rows, width), BF16),
            shape((rows, width), F32),
            shape((rows, width), BF16),
            shape((rows, width), BF16),
            shape((rows, width), BF16),
            shape((rows, ff), BF16),
            shape((rows, ff), BF16),
            shape((rows, ff), BF16),
            shape((2, width), F32),
            shape((rows, width), BF16),
        ],
        compiler_params=params(),
        cost_estimate=cost(
            12 * rows * width * ff + 4 * rows * width * width,
            12 * width * ff + 6 * rows * ff + 30 * rows * width,
            rows * ff,
        ),
        name="feed",
    )(at, tokens, cotangent, scale, vectors, weights, weights, weights, weights, *mixed)


def weight_kernel(core_ref, a_ref, b_ref, *refs, size):
    own_ref, away_ref, at_ref = refs[-3:]
    rows, tall = a_ref.shape
    core = core_ref[0]
    outs = (own_ref, away_ref)

    @pl.when(pl.program_id(1) == 0)
    def _():
        for side in range(2):
            half = core if side == 0 else 1 - core
            for c in range(tall // (2 * size)):
                start = pl.multiple_of((2 * c + half) * size, 128)
                at_ref[side, c * size : (c + 1) * size] = a_ref[:, pl.ds(start, size)].T

    wide = own_ref.shape[-1]
    for side in range(2):
        product = dot(at_ref[side], b_ref[...].reshape(rows, wide)).astype(BF16)
        outs[side][...] = product.reshape(own_ref.shape)


def weight_grad(core, a, b, chunk, shared=None, before=()):
    rows, tall = a.shape
    stacked = b.ndim == 3
    wide = b.shape[0] * b.shape[2] if stacked else b.shape[1]
    if chunk < 128:
        a = a.reshape(rows, tall // (2 * chunk), 2, chunk).swapaxes(1, 2).reshape(rows, tall)
        chunk = tall // 2
    columns = b.shape[2] if stacked else min(1024, wide)
    block = max(1024, 2 * chunk)
    if stacked:
        right = pl.BlockSpec((1, rows, columns), lambda i, j, _: (j, 0, 0))
    else:
        right = pl.BlockSpec((rows, columns), lambda i, j, _: (0, j))
    if shared:
        devices, height, at = shared
        one = tall // 2 // devices
        made = shape((devices, height, wide), BF16)
        out = pl.BlockSpec(
            (block // 2 // one, one, columns), lambda i, j, _: (i, at // one, j)
        )
    else:
        made = shape((tall // 2, wide), BF16)
        out = pl.BlockSpec((block // 2, columns), lambda i, j, _: (i, j))
    return pl.pallas_call(
        functools.partial(weight_kernel, size=chunk),
        grid_spec=pltpu.PrefetchScalarGridSpec(
            num_scalar_prefetch=1,
            grid=(tall // block, wide // columns),
            in_specs=[pl.BlockSpec((rows, block), lambda i, j, _: (0, i)), right]
            + [pl.BlockSpec(memory_space=pl.ANY)] * len(before),
            out_specs=[out, out],
            scratch_shapes=[pltpu.VMEM((2, block // 2, rows), BF16)],
        ),
        input_output_aliases={3: 0, 4: 1} if before else {},
        out_shape=[made] * 2,
        compiler_params=params(),
        cost_estimate=cost(2 * rows * tall * wide, 2 * (rows * tall + rows * wide + tall * wide)),
        name="weight_grad",
    )(core, a, b, *before)


def unturn_kernel(at_ref, c_ref, e_ref, l_ref, *refs, team):
    blocks, out_ref = refs[:-1], refs[-1]
    cosine, early, late = c_ref[...], e_ref[...], l_ref[...]
    which = pl.program_id(0)
    size = blocks[0].shape[-1]
    lanes = size * len(blocks) // team
    for i, ref in enumerate(blocks):
        for at in range(0, size, 128):
            first = (at_ref[0] ^ (i % team)) * lanes + i // team * size + at
            spot = pl.ds(pl.multiple_of(first, 128), 128)

            @pl.when(which < 2)
            def _(ref=ref, at=at, spot=spot):
                piece = turn(ref[0, :, at : at + 128].astype(F32), cosine, -early, -late)
                out_ref[0, :, spot] = piece.astype(BF16)

            @pl.when(which == 2)
            def _(ref=ref, at=at, spot=spot):
                out_ref[0, :, spot] = ref[0, :, at : at + 128]


def unturn(at, blocks, table, team):
    _, rows, lanes = blocks[0].shape
    wide = pl.BlockSpec((rows, 128), lambda j, _: (0, 0))
    count = len(blocks)
    return pl.pallas_call(
        functools.partial(unturn_kernel, team=team),
        grid_spec=pltpu.PrefetchScalarGridSpec(
            num_scalar_prefetch=1,
            grid=(3,),
            in_specs=[wide] * 3 + [pl.BlockSpec((1, rows, lanes), lambda j, _: (j, 0, 0))] * count,
            out_specs=pl.BlockSpec((1, rows, count * lanes), lambda j, _: (j, 0, 0)),
        ),
        out_shape=shape((3, rows, count * lanes), BF16),
        compiler_params=params(),
        cost_estimate=cost(0, 12 * rows * count * lanes),
        name="unturn",
    )(at, *table, *blocks)


def project_back_kernel(x_ref, gm_ref, vec_ref, w_ref, low_ref, *refs, part, lanes, first, last):
    which = pl.program_id(0)
    acc_ref = refs[-1]

    @pl.when(which == 0)
    def _():
        acc_ref[...] = jnp.zeros_like(acc_ref) if first else refs[0][...]

    width = w_ref.shape[-1]
    weight = jnp.concatenate(
        [
            w_ref[0, :, at : at + lanes]
            for at in range(part * lanes, width, PARTS * lanes)
        ],
        axis=1,
    )
    acc_ref[...] += dot(low_ref[0], weight, NT)

    if last:
        out_ref, sum_ref = refs[-3:-1]

        @pl.when(which == 2)
        def _():
            grad = acc_ref[...]
            normal, inverse = normalise(x_ref[...].astype(F32))
            sum_ref[0:1] = jnp.sum(grad * normal, axis=0, keepdims=True)
            sum_ref[1:2] = jnp.sum(grad, axis=0, keepdims=True)
            grad = gm_ref[...] + norm_back(grad, normal, inverse, vec_ref[0:1])
            out_ref[...] = grad.astype(BF16)


def project_back(tokens, grad_middle, vectors, weights, low, part, team, partial):
    rows, width = tokens.shape
    wide = low.shape[-1]
    last = part == PARTS - 1
    const = pl.BlockSpec((rows, width), lambda j: (0, 0))
    return pl.pallas_call(
        functools.partial(
            project_back_kernel, part=part, lanes=wide // team, first=not partial, last=last
        ),
        grid=(3,),
        in_specs=[
            const,
            const,
            pl.BlockSpec((4, width), lambda j: (0, 0)),
            pl.BlockSpec((1, width, width), lambda j: (j, 0, 0)),
            pl.BlockSpec((1, rows, wide), lambda j: (j, 0, 0)),
        ]
        + [const] * len(partial),
        out_specs=[const, pl.BlockSpec((2, width), lambda j: (0, 0))] if last else [const],
        out_shape=(
            [shape((rows, width), BF16), shape((2, width), F32)]
            if last
            else [shape((rows, width), F32)]
        ),
        scratch_shapes=[pltpu.VMEM((rows, width), F32)] if last else [],
        compiler_params=params(),
        cost_estimate=cost(6 * rows * width * wide, 18 * rows * width + 6 * width * width),
        name="project_back",
    )(tokens, grad_middle, vectors, weights, low, *partial)


def place_kernel(me_ref, *refs, masks, pieces):
    count = len(masks)
    halves, (wide_ref, small_ref, sem) = refs[: 2 * count], refs[2 * count :]
    me = me_ref[0]
    for wait in (False, True):
        for t in range(count):
            half = len(masks[t]) // 2
            for j, mask in enumerate(masks[t]):
                source = halves[2 * t + j // half].at[j % half]
                for lane, (first, size, which, to) in enumerate(pieces[t]):
                    origin = source.at[:, first : first + size]
                    if which is None:
                        place = small_ref.at[me ^ mask]
                    else:
                        place = wide_ref.at[which, me ^ mask, :, to : to + size]
                    copy = pltpu.make_async_copy(origin, place, sem.at[t, j, lane])
                    copy.wait() if wait else copy.start()


class Chain:
    def __init__(self, links, own, away, rounds, wire=BF16):
        self.links, self.rounds, self.wire = links, [list(r) for r in rounds], wire
        self.axes = [b for b in range(links.bits - 1, -1, -1) if b != links.core]
        self.dims = (2,) * len(self.axes)
        if own.ndim == 2:
            self.dims += (own.shape[0] * 2 // links.count,)
        self.dims += own.shape[1:]
        self.terms = [own.reshape(self.dims), links.swap(away, 1 << links.core).reshape(self.dims)]

    def hold(self, after):
        self.terms = tie(self.terms, after)
        return self

    def pick(self, mask):
        me, parts, axes = self.links.me() ^ mask, self.terms, list(self.axes)
        for bit in self.rounds[0]:
            at = axes.index(bit)
            parts = [
                lax.dynamic_index_in_dim(p, (me >> bit) & 1, at, keepdims=False) for p in parts
            ]
            axes.pop(at)
        return parts

    def split(self):
        self.masks = [0]
        for bit in self.rounds[0]:
            self.masks += [m | 1 << bit for m in self.masks]
        sent = [total(self.pick(m)).astype(self.wire) for m in self.masks[1:]]
        self.kept = self.pick(0)
        return sent

    def swap(self, sent):
        return [self.links.swap(v, m) for v, m in zip(sent, self.masks[1:])]

    def take(self, received):
        for bit in self.rounds.pop(0):
            self.axes.remove(bit)
        self.terms = self.kept + list(received)

    def result(self):
        return total(self.terms)


class Joined:
    def __init__(self, *chains):
        self.chains, self.links = chains, chains[0].links

    @property
    def rounds(self):
        return self.chains[0].rounds

    def split(self):
        sent = [c.split() for c in self.chains]
        return [jnp.concatenate(v, axis=-1) for v in zip(*sent)]

    def swap(self, sent):
        return self.chains[0].swap(sent)

    def take(self, received):
        first = 0
        for c in self.chains:
            last = first + c.terms[0].shape[-1]
            c.take([v[..., first:last] for v in received])
            first = last


def total(terms):
    return functools.reduce(jnp.add, [t.astype(F32) for t in terms])


def tie(values, *others):
    return lax.optimization_barrier((values, others))[0]


def begin(chains, values):
    sent = [c.split() for c in chains]
    values, sent = lax.optimization_barrier((values, sent))
    for c, v in zip(chains, sent):
        c.received = c.swap(v)
    return values


def finish(chains, after):
    received = tie([c.received for c in chains], after)
    for c, r in zip(chains, received):
        c.take(r)


class Links:
    def __init__(self, mesh):
        self.dp, self.seq = mesh.shape["dp"], mesh.shape["seq"]
        self.count = self.dp * self.seq
        self.bits = self.count.bit_length() - 1
        self.core = self.seq.bit_length() - 1
        seq_bits = list(range(self.core))
        dp_bits = list(range(self.core + 1, self.bits))
        self.dp_bits = [self.core] + dp_bits
        first, last = dp_bits[:1], dp_bits[1:]
        self.seq_first = [[b] for b in seq_bits + dp_bits]
        self.seq_last = [[b] for b in seq_bits[::-1] + dp_bits]
        self.dp_first = [first, seq_bits[:1], seq_bits[1:] + last]
        self.seq_then = [seq_bits[:1], seq_bits[1:], dp_bits]
        self.direct = [seq_bits, dp_bits]
        self.orders = [
            seq_bits + dp_bits,
            seq_bits[::-1] + dp_bits,
            dp_bits[:1] + seq_bits + dp_bits[1:],
            dp_bits[:1] + seq_bits[::-1] + dp_bits[1:],
        ]

        self.team_bits = [self.core] + seq_bits[2:]
        self.team = 2 ** len(self.team_bits)

    def bit(self, which):
        return (self.me() >> which) & 1

    def route(self, k):
        pairs = []
        for i in range(self.count):
            core, y, x = (i >> self.core) & 1, (i >> 1) & 1, i & 1
            rest = i & ~((1 << self.core) | 3)
            pairs.append((i, rest | (y ^ (k >> 1)) << self.core | core << 1 | (x ^ (k & 1))))
        return pairs

    def to_team(self, value):
        wins, rows, width = value.shape
        blocks = value.reshape(wins * 2, rows // 2, width)
        place = 2 * self.bit(0) + self.bit(1)
        return [
            lax.dynamic_index_in_dim(blocks, place ^ (2 * (k & 1) + (k >> 1)), 0, keepdims=False)
            for k in range(4)
        ]

    def move_one(self, sent, k):
        return lax.ppermute(sent, BOTH, self.route(k))

    def move(self, sent):
        return [self.move_one(v, k) for k, v in enumerate(sent)]

    def from_team_blocks(self, value):
        rows, width = value.shape
        blocks = value.reshape(4, rows // 4, width)
        return [
            lax.dynamic_index_in_dim(blocks, self.base() ^ k, 0, keepdims=False) for k in range(4)
        ]

    def back_one(self, sent, k):
        return lax.ppermute(sent, BOTH, [(j, i) for i, j in self.route(k)])

    def in_place(self, received):
        return [received[k] for k in (0, 2, 1, 3)]

    def base(self):
        return 2 * self.bit(self.core) + self.bit(0)

    def member(self):
        return sum(self.bit(b) << i for i, b in enumerate(self.team_bits))

    def exchange(self, values):
        masks = [
            sum(1 << b for i, b in enumerate(self.team_bits) if m >> i & 1)
            for m in range(self.team)
        ]
        return [v if m == 0 else self.swap(v, masks[m]) for m, v in enumerate(values)]

    def me(self):
        return lax.axis_index("dp") * self.seq + lax.axis_index("seq")

    def swap(self, value, mask):
        return lax.ppermute(value, BOTH, [(i, i ^ mask) for i in range(self.count)])

    def own(self):
        return jnp.reshape(lax.axis_index("dp") % 2, (1,))

    def gather(self, values, pieces, width, counts, moved):
        orders = self.orders
        held, masks = [v[None] for v in values], [[0] for v in values]
        levels = self.bits - 1
        early = None
        (held, counts, moved) = lax.optimization_barrier((held, counts, moved))
        for level in range(levels):
            order = [o[levels - 1 - level] for o in orders]
            got = [self.swap(h, 1 << b) for h, b in zip(held, order)]
            masks = [m + [i | 1 << b for i in m] for m, b in zip(masks, order)]
            if level in (0, 2):
                moved[level : level + 2] = [
                    self.move_one(moved[k], k) for k in (level, level + 1)
                ]
            if level < len(self.dp_bits):
                counts = counts + self.swap(counts, 1 << self.dp_bits[level])
            held = [jnp.concatenate([h, g], axis=0) for h, g in zip(held, got)]
            if level in (1, 3):
                held, counts, moved = lax.optimization_barrier((held, counts, moved))
            else:
                held, counts = lax.optimization_barrier((held, counts))
            if level == 1:
                early = held
        got = [self.swap(h, 1 << self.core) for h in held]
        masks = [m + [i | 1 << self.core for i in m] for m in masks]
        args = [v for pair in zip(held, got) for v in pair]
        rows = values[0].shape[0]
        wide = (3, self.count, rows, width)
        narrow = (self.count, rows, 128)
        placed = pl.pallas_call(
            functools.partial(place_kernel, masks=masks, pieces=pieces),
            grid_spec=pltpu.PrefetchScalarGridSpec(
                num_scalar_prefetch=1,
                grid=(1,),
                in_specs=[pl.BlockSpec(memory_space=pl.ANY)] * len(args),
                out_specs=[
                    pl.BlockSpec(wide, lambda i, _: (0, 0, 0, 0)),
                    pl.BlockSpec(narrow, lambda i, _: (0, 0, 0)),
                ],
                scratch_shapes=[pltpu.SemaphoreType.DMA((len(values), self.count, 3))],
            ),
            out_shape=[shape(wide, BF16), shape(narrow, BF16)],
            compiler_params=params(),
            name="place",
        )(jnp.reshape(self.me(), (1,)), *args)
        return placed, early, counts, moved


def packed(w_down, w_out, w_gate, w_up, width):
    parts = [w_down, w_out]
    for weight in (w_gate, w_up):
        parts += [weight[:, c : c + width] for c in range(0, weight.shape[1], width)]
    return jnp.concatenate(parts, axis=0)


def regrouped(gathered, each, width):
    if each == ROW_UNIT:
        return gathered
    tall = 4 * each
    down = gathered[:, :tall].reshape(-1, 4 * ROW_UNIT, width)
    parts = [down]
    for at in range(tall, gathered.shape[1], each):
        parts.append(gathered[:, at : at + each].reshape(-1, ROW_UNIT, width))
    return jnp.concatenate(parts, axis=1)


def body(
    links,
    tokens,
    cotangent,
    lengths,
    species,
    ln1_gain,
    ln1_bias,
    w_query,
    w_key,
    w_value,
    w_out,
    ln2_gain,
    ln2_bias,
    w_gate,
    w_up,
    w_down,
):
    wins, rows, width = tokens.shape
    each = w_query.shape[0]
    team = links.team
    lanes = width // team
    share = wins * rows
    scalar = functools.partial(jnp.reshape, shape=(1,))
    member = links.member()
    base = scalar(links.base())

    small = jnp.stack([ln1_gain, ln1_bias, ln2_gain, ln2_bias], axis=1)
    small = jnp.pad(small, ((0, 0), (0, 124)))
    cut = width // 2
    local = [
        jnp.concatenate([w_query, w_key[:, :cut]], axis=1),
        jnp.concatenate([w_key[:, cut:], w_value, small], axis=1),
    ]
    pieces = [
        [(0, width, 0, 0), (width, cut, 1, 0)],
        [(0, cut, 1, cut), (cut, width, 2, 0), (cut + width, 128, None, 0)],
    ]
    species_ids = jnp.arange(SPECIES)
    onehot = (species[:, None] == species_ids[None, :]).astype(F32)
    counts = jnp.sum(onehot * lengths[:, None].astype(F32), axis=0)
    told = jnp.stack([lengths, species])
    told = jnp.stack([told, links.swap(told, 1 << links.core)])
    (qkv_w, small), early, counts, moved = links.gather(
        local, pieces, width, counts, links.to_team(tokens)
    )
    mine = packed(*tie((w_down, w_out, w_gate, w_up), early), width)
    weights = regrouped(lax.all_gather(mine, BOTH, axis=0), each, width)
    qkv_w = qkv_w.reshape(3, width, width)
    vectors = small.reshape(width, 128)[:, :4].T.astype(F32)

    told = lax.dynamic_index_in_dim(told, links.bit(1) ^ links.bit(links.core), 0, keepdims=False)
    told = lax.dynamic_index_in_dim(told, links.bit(0), 1, keepdims=False)
    length, kind = told[0], told[1]
    upper = member >> 1
    half = rows // 2
    block = (4 * upper + jnp.arange(4))[:, None] * rows + links.bit(links.core) * half
    positions = (block + jnp.arange(half)[None, :]).reshape(share)
    table = tables(positions)
    info = jnp.stack([length, member & 1, upper])

    rows_in = arrange(base, moved)
    projected = []
    for m in range(team)[::-1]:
        projected.append(project(scalar(member ^ m), rows_in, qkv_w, vectors, table, lanes))
    projected = projected[::-1]
    normed_one = projected[0][1]
    window_weight = SPECIES * jnp.sum((kind == species_ids) * counts) / jnp.sum(counts)
    row_scale = jnp.where(positions < length, window_weight, 0.0)[:, None]

    qkv = links.exchange([p[0] for p in projected])
    qkv, cot_sent = lax.optimization_barrier((qkv, links.to_team(cotangent)))
    cot_moved = links.move(cot_sent)
    mixed_heads, lse, mixed = [], [], []
    for part in range(PARTS):
        *heads, sums = attend(info, qkv, part)
        mixed_heads.append(heads)
        lse.append(sums)
        mixed += links.exchange(heads)
        if part == 0:
            qkv, cot_moved = lax.optimization_barrier((qkv, tie(cot_moved, sums)))
    cot_in = arrange(base, cot_moved)
    fed = feed(scalar(member), rows_in, cot_in, row_scale, mixed, vectors, weights)
    grad_mixed = fed[:team]
    (
        delta, grad_middle, grad_middle_low, normed_two, grad_low, hidden, grad_gate, grad_up,
        sums_two, mixed_rows,
    ) = fed[team:]
    grad_heads = links.exchange(grad_mixed)

    narrow, broad = width // links.dp, hidden.shape[1] // links.dp
    core = links.own()
    place = scalar(2 * links.bit(0) + links.bit(1))
    shared = (links.count // 2, 5 * each)
    grad_low, sent = lax.optimization_barrier((grad_low, links.from_team_blocks(delta)))
    returned = [links.back_one(sent[k], k) for k in range(2)]
    before = weight_grad(core, hidden, grad_low, broad, shared + (0,))
    low, returned = lax.optimization_barrier((tie(grad_middle_low, before), returned))
    own, away = weight_grad(core, mixed_rows, low, narrow, shared + (4 * each,), before)
    sum_rest = Chain(links, own, away, links.dp_first)
    grad_gate, sent = lax.optimization_barrier((tie(grad_gate, own), sent[2:]))
    returned += [links.back_one(v, k) for k, v in enumerate(sent, 2)]
    own, away = weight_grad(core, normed_two, grad_gate, narrow)
    sum_gate = Chain(links, own, away, links.seq_first)
    grad_up = begin([sum_rest.hold((own, returned))], tie(grad_up, own))
    own, away = weight_grad(core, normed_two, grad_up, narrow)
    sum_up = Chain(links, own, away, links.seq_last)

    def back(part, grads, sub=0, subs=1):
        return attend_back(
            info, qkv, mixed_heads[part], grads, lse[part], part, sub, subs
        )

    def through(part, low, partial):
        return project_back(rows_in, grad_middle, vectors, qkv_w, low, part, team, partial)

    grad_heads = begin([sum_gate.hold(own)], tie(list(grad_heads), own))
    output = settle(place, links.in_place(tie(returned, own)), [tokens])
    grad_heads = begin([sum_up.hold(output)], tie(list(grad_heads), output))
    made = back(0, grad_heads)
    received = links.exchange(made)
    chains = [sum_rest, sum_gate, sum_up]
    finish(chains, made)
    received = begin(chains, tie(list(received), made))
    low = unturn(scalar(member), received, table, team)
    own_one, away_one = weight_grad(core, normed_one, low, narrow)
    sum_one = Chain(links, own_one, away_one, links.seq_then)
    (partial,) = through(0, tie(low, own_one), [])
    sum_one.hold(partial)
    if len(links.seq_first) == 4:
        sum_pair = [Joined(sum_gate, sum_up)]
    else:
        sum_pair = [sum_gate, sum_up]
    subs = 2 if lanes // 128 // PARTS > 1 else 1
    made = back(1, tie(list(grad_heads), partial), 0, subs)
    received = list(links.exchange(made))
    finish(chains, made)
    if subs > 1:
        grad_heads = begin(sum_pair + [sum_rest], tie(list(grad_heads), made))
        made = back(1, grad_heads, 1, subs)
        received += links.exchange(made)
    else:
        received = begin(sum_pair + [sum_rest], received)
    finish(sum_pair, made)
    received = begin(sum_pair + [sum_one], tie(received, made))
    low = unturn(scalar(member), received, table, team)
    grad_in, sums_one = through(1, low, [partial])
    finish(sum_pair + [sum_one, sum_rest], grad_in)
    chains = [c for c in sum_pair + [sum_one] if c.rounds]
    low, sent = begin(chains, (low, links.from_team_blocks(grad_in)))
    home = [links.back_one(v, k) for k, v in enumerate(sent)]
    own_two, away_two = weight_grad(core, normed_one, low, narrow)
    finish(chains, own_two)
    gains = jnp.concatenate([sums_one, sums_two], axis=0)
    gains = gains.reshape(4, links.dp // 2, 2, width // links.dp).transpose(2, 1, 3, 0)
    gains = gains.reshape(2, width // 2, 4)
    gains = jnp.pad(gains, ((0, 0), (0, 0), (0, 124))).astype(BF16)
    gains = [
        lax.dynamic_index_in_dim(gains, c, 0, keepdims=False) for c in (core[0], 1 - core[0])
    ]
    own = jnp.concatenate([own_two, gains[0]], axis=1)
    away = jnp.concatenate([away_two, gains[1]], axis=1)
    last = Chain(links, own, away, links.direct)
    chains = [c for c in sum_pair + [sum_rest, last] if c.rounds]
    nothing = begin(chains, [])
    finish(chains, nothing)
    pieces = [c for c in sum_pair + [sum_rest] if c.rounds]
    chains = pieces + [Joined(sum_one, last)]
    while chains:
        nothing = begin(chains, [])
        finish(chains, nothing)
        chains = [c for c in chains if c.rounds]
    grad_tokens = settle(place, links.in_place(home), [])

    last = last.result()
    gains = last[:, -128:].T
    merged = jnp.stack([sum_one.result(), last[:, :-128]], axis=1)
    merged = merged.reshape(each, PARTS, 3, team, -1).transpose(0, 2, 3, 1, 4)
    merged = merged.reshape(each, 3, width)
    rest = sum_rest.result()
    return (
        output.reshape(wins, rows, width),
        grad_tokens.reshape(wins, rows, width),
        gains[0],
        gains[1],
        merged[:, 0],
        merged[:, 1],
        merged[:, 2],
        rest[4 * each :],
        gains[2],
        gains[3],
        sum_gate.result(),
        sum_up.result(),
        rest[: 4 * each],
    )


def solution(mesh):
    token = P("dp", "seq", None)
    vector = P(BOTH)
    matrix = P(BOTH, None)
    return jax.shard_map(
        functools.partial(body, Links(mesh)),
        mesh=mesh,
        in_specs=(
            (token, token, P("dp"), P("dp"), vector, vector)
            + (matrix,) * 4
            + (vector, vector)
            + (matrix,) * 3
        ),
        out_specs=(
            (token, token, vector, vector) + (matrix,) * 4 + (vector, vector) + (matrix,) * 3
        ),
        check_vma=False,
    )
```

```python
import functools

import jax
import jax.numpy as jnp
from jax import lax
from jax.experimental import pallas as pl
from jax.experimental.pallas import tpu as pltpu
from jax.sharding import PartitionSpec as P

HEAD_DIM = 64
SPECIES = 8
EPS = 1e-05
LOG2E = 1.4426950408889634
BOTH = ("dp", "seq")
F32 = jnp.float32
BF16 = jnp.bfloat16
FF_BLOCK = 512
FEED_ROWS = 512
PARTS = 2
ROW_UNIT = 32
VMEM = 60 * 2**20

NN = (((1,), (0,)), ((), ()))
NT = (((1,), (1,)), ((), ()))


def dot(a, b, dims=NN):
    return lax.dot_general(a, b, dims, preferred_element_type=F32)


def shape(dims, dtype):
    return jax.ShapeDtypeStruct(dims, dtype)


def params():
    return pltpu.CompilerParams(vmem_limit_bytes=VMEM)


def cost(flops, moved, exps=0):
    return pl.CostEstimate(flops=flops // 64, bytes_accessed=moved // 64, transcendentals=exps // 64)


def normalise(value):
    centered = value - jnp.mean(value, axis=-1, keepdims=True)
    inverse = lax.rsqrt(jnp.mean(centered * centered, axis=-1, keepdims=True) + EPS)
    return centered * inverse, inverse


def norm_back(grad, normal, inverse, gain):
    scaled = grad * gain
    centered = scaled - jnp.mean(scaled, axis=-1, keepdims=True)
    return inverse * (centered - normal * jnp.mean(scaled * normal, axis=-1, keepdims=True))


def turn(value, cosine, early, late):
    return value * cosine + pltpu.roll(value, 96, 1) * early + pltpu.roll(value, 32, 1) * late


def tables(positions):
    half = HEAD_DIM // 2
    freq = 10000.0 ** (-2.0 * jnp.arange(half, dtype=F32) / HEAD_DIM)
    angle = positions.astype(F32)[:, None] * freq[None, :]
    cosine, sine = jnp.cos(angle), jnp.sin(angle)
    zero = jnp.zeros_like(sine)
    return (
        jnp.concatenate([cosine] * 4, axis=1),
        jnp.concatenate([-sine, zero, -sine, zero], axis=1),
        jnp.concatenate([zero, sine, zero, sine], axis=1),
    )


def arrange_kernel(base_ref, *refs):
    for k, ref in enumerate(refs[:-1]):
        refs[-1][base_ref[0] ^ k] = ref[...]


def arrange(base, blocks):
    rows, width = blocks[0].shape
    return pl.pallas_call(
        arrange_kernel,
        grid_spec=pltpu.PrefetchScalarGridSpec(
            num_scalar_prefetch=1,
            grid=(1,),
            in_specs=[pl.BlockSpec((rows, width), lambda i, _: (0, 0))] * len(blocks),
            out_specs=pl.BlockSpec((len(blocks), rows, width), lambda i, _: (0, 0, 0)),
        ),
        out_shape=shape((len(blocks), rows, width), blocks[0].dtype),
        compiler_params=params(),
        cost_estimate=cost(0, 16 * rows * width),
        name="arrange",
    )(base, *blocks).reshape(len(blocks) * rows, width)


def settle_kernel(base_ref, *refs):
    blocks, added, out_ref = refs[:4], refs[4:-1], refs[-1]
    here = pl.program_id(0)

    for k, ref in enumerate(blocks):

        @pl.when((base_ref[0] ^ k) == here)
        def _(ref=ref):
            value = ref[...].astype(F32)
            out_ref[0] = value + added[0][0].astype(F32) if added else value


def settle(base, blocks, added):
    rows, width = blocks[0].shape
    block = pl.BlockSpec((1, rows, width), lambda i, _: (i, 0, 0))
    return pl.pallas_call(
        settle_kernel,
        grid_spec=pltpu.PrefetchScalarGridSpec(
            num_scalar_prefetch=1,
            grid=(4,),
            in_specs=[pl.BlockSpec((rows, width), lambda i, _: (0, 0))] * 4
            + [block] * len(added),
            out_specs=block,
        ),
        out_shape=shape((4, rows, width), F32),
        compiler_params=params(),
        cost_estimate=cost(0, 32 * rows * width),
        name="settle",
    )(base, *blocks, *[a.reshape(4, rows, width) for a in added])


def project_kernel(at_ref, x_ref, w_ref, vec_ref, c_ref, e_ref, l_ref, send_ref, n_ref):
    which = pl.program_id(0)
    _, rows, lanes = send_ref.shape

    @pl.when(which == 0)
    def _():
        normal, _ = normalise(x_ref[...].astype(F32))
        n_ref[...] = (normal * vec_ref[0:1] + vec_ref[1:2]).astype(BF16)

    product = dot(n_ref[...], w_ref[0])
    cosine, early, late = c_ref[...], e_ref[...], l_ref[...]

    def put(rotate):
        for at in range(0, lanes, 128):
            piece = product[:, at : at + 128]
            if rotate:
                piece = turn(piece, cosine, early, late)
            send_ref[0, :, at : at + 128] = piece.astype(BF16)

    pl.when(which < 2)(lambda: put(True))
    pl.when(which == 2)(lambda: put(False))


def project(at, tokens, weights, vectors, table, lanes):
    rows, width = tokens.shape
    wide = pl.BlockSpec((rows, 128), lambda j, _: (0, 0))
    return pl.pallas_call(
        project_kernel,
        grid_spec=pltpu.PrefetchScalarGridSpec(
            num_scalar_prefetch=1,
            grid=(3,),
            in_specs=[
                pl.BlockSpec((rows, width), lambda j, _: (0, 0)),
                pl.BlockSpec((1, width, lanes), lambda j, at: (j, 0, at[0])),
                pl.BlockSpec((4, width), lambda j, _: (0, 0)),
                wide,
                wide,
                wide,
            ],
            out_specs=[
                pl.BlockSpec((1, rows, lanes), lambda j, _: (j, 0, 0)),
                pl.BlockSpec((rows, width), lambda j, _: (0, 0)),
            ],
        ),
        out_shape=[shape((3, rows, lanes), BF16), shape((rows, width), BF16)],
        compiler_params=params(),
        cost_estimate=cost(6 * rows * width * lanes, 6 * rows * lanes + 6 * width * lanes),
        name="project",
    )(at, tokens, weights, vectors, *table)


def attend_kernel(info_ref, *refs, team):
    q_refs, k_refs, v_refs = refs[:team], refs[team : 2 * team], refs[2 * team : 3 * team]
    o_refs, (l_ref, vt_ref) = refs[3 * team : 4 * team], refs[4 * team :]
    length, side, upper = info_ref[0], info_ref[1], info_ref[2]
    lane = lax.broadcasted_iota(jnp.int32, (1, 128), 1)
    block = q_refs[0].shape[0]
    keys, ups = 2 * block, team // 2
    up = pl.program_id(2)

    def chunk(arrays, p, b):
        rows = slice(b * block, (b + 1) * block)
        return jnp.concatenate([arrays[2 * p][rows], arrays[2 * p + 1][rows]], axis=0)

    @pl.when((pl.program_id(1) == 0) & (up == 0))
    def _():
        for p in range(ups):
            for b in range(4):
                at = (4 * p + b) * keys
                vt_ref[:, at : at + keys] = chunk(v_refs, p, b).T

    q2 = jnp.concatenate([q_refs[0][...], q_refs[1][...]], axis=0)
    for p in range(1, ups):
        other = jnp.concatenate([q_refs[2 * p][...], q_refs[2 * p + 1][...]], axis=0)
        q2 = jnp.where(up == p, other, q2)
    q2 = q2 * BF16(0.125)

    def positions(p, b):
        row = lax.broadcasted_iota(jnp.int32, (keys, keys), 0)
        return row ^ (side * block) | (4 * (upper ^ p) + b) * keys

    def run(chunks):
        k2 = jnp.concatenate([chunk(k_refs, c // 4, c % 4) for c in range(chunks)], axis=0)
        n = chunks * keys
        outs = []
        for h in range(2):
            qh = jnp.where((lane // 64) == h, q2, BF16(0))
            s = dot(k2, qh, NT)
            if ups == 1:
                last = jnp.where(positions(0, chunks - 1) < length, s[n - keys :], -1e30)
                s = jnp.concatenate([s[: n - keys], last], 0) if chunks > 1 else last
            else:
                valid = [positions(c // 4, c % 4) < length for c in range(chunks)]
                s = jnp.concatenate(
                    [jnp.where(v, s[c * keys : (c + 1) * keys], -1e30) for c, v in enumerate(valid)],
                    axis=0,
                )
            m = jnp.max(s, axis=0, keepdims=True)
            p = jnp.exp2((s - m) * LOG2E)
            all_p = jnp.sum(p, axis=0, keepdims=True)
            o = dot(vt_ref[h * 64 : h * 64 + 64, :n], p.astype(BF16))
            outs.append(o / all_p)
            l_ref[0, h : h + 1] = m + jnp.log(all_p)
        result = jnp.concatenate(outs, 0).T.astype(BF16)
        for p in range(ups):

            @pl.when(up == p)
            def _(p=p):
                o_refs[2 * p][...] = result[:block]
                o_refs[2 * p + 1][...] = result[block:]

    if ups == 1:
        blocks = (length + keys - 1) // keys
        for i in range(4):
            pl.when(blocks == i + 1)(functools.partial(run, i + 1))
    else:
        run(4 * ups)


def attend(info, qkv, part):
    team = len(qkv)
    _, rows, lanes = qkv[0].shape
    span, pairs, ups = team * rows, lanes // 128 // PARTS, team // 2
    block = rows // 4

    def whole(which):
        return [
            pl.BlockSpec((None, rows, 128), lambda h, b, u, _: (which, 0, part * pairs + h))
        ] * team

    return pl.pallas_call(
        functools.partial(attend_kernel, team=team),
        grid_spec=pltpu.PrefetchScalarGridSpec(
            num_scalar_prefetch=1,
            grid=(pairs, 4, ups),
            in_specs=[
                pl.BlockSpec((None, block, 128), lambda h, b, u, _: (0, b, part * pairs + h))
            ]
            * team
            + whole(1)
            + whole(2),
            out_specs=[pl.BlockSpec((block, 128), lambda h, b, u, _: (b, h))] * team
            + [pl.BlockSpec((1, 2, 2 * block), lambda h, b, u, _: (h, 0, b * ups + u))],
            scratch_shapes=[pltpu.VMEM((128, span), BF16)],
        ),
        out_shape=[shape((rows, pairs * 128), BF16)] * team + [shape((pairs, 2, span), F32)],
        compiler_params=params(),
        cost_estimate=cost(
            16 * span * span * pairs * 128, 8 * span * pairs * 128, 2 * span * span * pairs
        ),
        name="attend",
    )(info, *qkv, *qkv, *qkv)


def attend_back_kernel(info_ref, *refs, team):
    q_refs, k_refs, v_refs, o_refs, g_refs = (refs[i * team : (i + 1) * team] for i in range(5))
    l_ref, d_refs = refs[5 * team], refs[5 * team + 1 : 6 * team + 1]
    kt_ref, dk_ref, dv_ref = refs[6 * team + 1 :]
    length, side, upper = info_ref[0], info_ref[1], info_ref[2]
    lane = lax.broadcasted_iota(jnp.int32, (1, 128), 1)
    block = q_refs[0].shape[0]
    keys, ups = 2 * block, team // 2
    b, up = pl.program_id(1), pl.program_id(2)
    first = (4 * (upper ^ up) + b) * keys

    def chunk(arrays, p, c):
        rows = pl.ds(pl.multiple_of(c * block, block), block)
        return jnp.concatenate([arrays[2 * p][rows], arrays[2 * p + 1][rows]], axis=0)

    def queries(arrays):
        value = jnp.concatenate([arrays[0][...], arrays[1][...]], axis=0)
        for p in range(1, ups):
            other = jnp.concatenate([arrays[2 * p][...], arrays[2 * p + 1][...]], axis=0)
            value = jnp.where(up == p, other, value)
        return value

    @pl.when((b == 0) & (up == 0))
    def _():
        for p in range(ups):
            for c in range(4):
                at = (4 * p + c) * keys
                kt_ref[:, at : at + keys] = (chunk(k_refs, p, c) * BF16(0.125)).T
        dk_ref[...] = jnp.zeros_like(dk_ref)
        dv_ref[...] = jnp.zeros_like(dv_ref)

    here = pl.ds(pl.multiple_of(b * block, block), block)

    def put(value):
        for p in range(ups):

            @pl.when(up == p)
            def _(p=p):
                d_refs[2 * p][0, here] = value[:block]
                d_refs[2 * p + 1][0, here] = value[block:]

    @pl.when(first >= length)
    def _():
        put(jnp.zeros((keys, 128), BF16))

    @pl.when(first < length)
    def _():
        q2 = queries(q_refs) * BF16(0.125)
        g2 = queries(g_refs)
        products = (g2.astype(F32) * queries(o_refs).astype(F32)).T
        qs, gs, ls, ds = [], [], [], []
        for h in range(2):
            mine = (lane // 64) == h
            qs.append(jnp.where(mine, q2, BF16(0)))
            gs.append(jnp.where(mine, g2, BF16(0)))
            ls.append(l_ref[0, h : h + 1] * LOG2E)
            ds.append(jnp.sum(products[h * 64 : h * 64 + 64], axis=0, keepdims=True))
        qc = jnp.concatenate(qs, 0)
        gc = jnp.concatenate(gs, 0)
        lc = jnp.concatenate(ls, 1)
        dc = jnp.concatenate(ds, 1)
        acc = (jnp.zeros((64, keys), F32),) * 2
        for p in range(ups):
            start = 4 * (upper ^ p) * keys

            def step(c, acc, masked, p=p, start=start):
                sl = pl.ds(pl.multiple_of((4 * p + c) * keys, keys), keys)
                k2 = chunk(k_refs, p, c)
                v2 = chunk(v_refs, p, c)
                prob = jnp.exp2(dot(k2, qc, NT) * LOG2E - lc)
                if masked:
                    row = lax.broadcasted_iota(jnp.int32, (keys, 1), 0)
                    row = row ^ (side * block) | (start + c * keys)
                    prob = jnp.where(row < length, prob, 0.0)
                gp = dot(v2, gc, NT)
                gs_low = (prob * (gp - dc)).astype(BF16)
                dv_ref[sl] += dot(prob.astype(BF16), gc)
                dk_ref[sl] += dot(gs_low, qc)
                return tuple(
                    acc[h]
                    + dot(kt_ref[h * 64 : h * 64 + 64, sl], gs_low[:, h * keys : (h + 1) * keys])
                    for h in range(2)
                )

            valid = jnp.clip(length - start, 0, 4 * keys)
            full = valid // keys
            acc = lax.fori_loop(0, full, lambda c, a: step(c, a, False), acc)
            acc = lax.cond(
                full * keys < valid, lambda a: step(full, a, True), lambda a: a, acc
            )
        put(jnp.concatenate(acc, 0).T.astype(BF16))

    @pl.when((b == 3) & (up == ups - 1))
    def _():
        for p in range(ups):
            for c in range(4):
                at = (4 * p + c) * keys
                for t, ref in ((1, dk_ref), (2, dv_ref)):
                    for m in range(2):
                        rows = slice(c * block, (c + 1) * block)
                        piece = ref[at + m * block : at + (m + 1) * block]
                        d_refs[2 * p + m][t, rows] = piece.astype(BF16)


def attend_back(info, qkv, mixed, grad, lse, part, sub, subs):
    team = len(qkv)
    _, rows, lanes = qkv[0].shape
    span, pairs, ups = team * rows, lanes // 128 // PARTS // subs, team // 2
    start, near = (part * subs + sub) * pairs, sub * pairs
    block = rows // 4
    spot = pl.BlockSpec((block, 128), lambda h, b, u, _: (b, start + h))

    def whole(which):
        return [
            pl.BlockSpec((None, rows, 128), lambda h, b, u, _: (which, 0, start + h))
        ] * team

    return pl.pallas_call(
        functools.partial(attend_back_kernel, team=team),
        grid_spec=pltpu.PrefetchScalarGridSpec(
            num_scalar_prefetch=1,
            grid=(pairs, 4, ups),
            in_specs=[
                pl.BlockSpec((None, block, 128), lambda h, b, u, _: (0, b, start + h))
            ]
            * team
            + whole(1)
            + whole(2)
            + [pl.BlockSpec((block, 128), lambda h, b, u, _: (b, near + h))] * team
            + [spot] * team
            + [pl.BlockSpec((1, 2, 2 * block), lambda h, b, u, _: (near + h, 0, b * ups + u))],
            out_specs=[pl.BlockSpec((3, rows, 128), lambda h, b, u, _: (0, 0, h))] * team,
            scratch_shapes=[
                pltpu.VMEM((128, span), BF16),
                pltpu.VMEM((span, 128), F32),
                pltpu.VMEM((span, 128), F32),
            ],
        ),
        out_shape=[shape((3, rows, pairs * 128), BF16)] * team,
        compiler_params=params(),
        cost_estimate=cost(
            30 * span * span * pairs * 128, 16 * span * pairs * 128, 2 * span * span * pairs
        ),
        name="attend_back",
    )(info, *qkv, *qkv, *qkv, *mixed, *grad, lse)


def feed_kernel(
    at_ref, x_ref, cot_ref, scale_ref, vec_ref, wo_ref, wg_ref, wu_ref, wd_ref, *refs, team
):
    mix_refs, send_refs = refs[: team * PARTS], refs[team * PARTS : team * (PARTS + 1)]
    (
        delta_ref, gm_ref, gml_ref, n_ref, gl_ref, hid_ref, gg_ref, gu_ref, sum_ref, rows_ref,
        acc_ref, normal_ref, inv_ref,
    ) = refs[team * (PARTS + 1) :]
    step = pl.program_id(1)
    lanes = send_refs[0].shape[1]
    some = mix_refs[0].shape[1]

    def whole(ref):
        return ref[...].reshape(-1, ref.shape[-1])

    def spot(m, first, size):
        return pl.ds(pl.multiple_of((at_ref[0] ^ m) * lanes + first, size), size)

    @pl.when(step == 0)
    def _():
        for i, ref in enumerate(mix_refs):
            rows_ref[:, spot(i % team, i // team * some, some)] = ref[...]
        added = dot(rows_ref[...], whole(wo_ref))
        acc_ref[...] = added
        normal, inverse = normalise(x_ref[...].astype(F32) + added)
        normal_ref[...] = normal
        inv_ref[...] = inverse
        n_ref[...] = (normal * vec_ref[2:3] + vec_ref[3:4]).astype(BF16)
        gl_ref[...] = (cot_ref[...].astype(F32) * scale_ref[...]).astype(BF16)
        gm_ref[...] = jnp.zeros_like(gm_ref)

    wg, wu, wd = whole(wg_ref), whole(wu_ref), whole(wd_ref)
    normed = n_ref[...]
    gate = dot(normed, wg)
    upper = dot(normed, wu)
    sigma = jax.nn.sigmoid(gate)
    silu = gate * sigma
    hidden = (silu * upper).astype(BF16)
    hid_ref[...] = hidden
    grad_hidden = dot(gl_ref[...], wd, NT)
    grad_up = (grad_hidden * silu).astype(BF16)
    grad_gate = (grad_hidden * upper * sigma * (1.0 + gate * (1.0 - sigma))).astype(BF16)
    gu_ref[...] = grad_up
    gg_ref[...] = grad_gate
    acc_ref[...] += dot(hidden, wd)
    gm_ref[...] += dot(grad_gate, wg, NT) + dot(grad_up, wu, NT)

    @pl.when(step == pl.num_programs(1) - 1)
    def _():
        delta_ref[...] = acc_ref[...].astype(BF16)
        grad = gm_ref[...]
        normal = normal_ref[...]

        @pl.when(pl.program_id(0) == 0)
        def _():
            sum_ref[...] = jnp.zeros_like(sum_ref)

        sum_ref[0:1] += jnp.sum(grad * normal, axis=0, keepdims=True)
        sum_ref[1:2] += jnp.sum(grad, axis=0, keepdims=True)
        total_grad = cot_ref[...].astype(F32) * scale_ref[...] + norm_back(
            grad, normal, inv_ref[...], vec_ref[2:3]
        )
        gm_ref[...] = total_grad
        low = total_grad.astype(BF16)
        gml_ref[...] = low
        acc_ref[...] = dot(low, whole(wo_ref), NT)
        for m in range(team):
            send_refs[m][...] = acc_ref[:, spot(m, 0, lanes)].astype(BF16)


def feed(at, tokens, cotangent, scale, mixed, vectors, weights):
    team = len(mixed) // PARTS
    rows, width = tokens.shape
    lanes = width // team
    units = weights.shape[0]
    tall = 4 * ROW_UNIT
    ff = units * tall
    columns = width // FF_BLOCK
    each = min(FEED_ROWS, rows)
    const = pl.BlockSpec((each, width), lambda i, j, _: (i, 0))
    block = pl.BlockSpec((each, FF_BLOCK), lambda i, j, _: (i, j))
    mix = pl.BlockSpec((each, lanes), lambda i, j, _: (i, 0))

    def part(first):
        return pl.BlockSpec(
            (units, ROW_UNIT, FF_BLOCK), lambda i, j, _: (0, first + j // columns, j % columns)
        )

    return pl.pallas_call(
        functools.partial(feed_kernel, team=team),
        grid_spec=pltpu.PrefetchScalarGridSpec(
            num_scalar_prefetch=1,
            grid=(rows // each, ff // FF_BLOCK),
            in_specs=[
                const,
                const,
                pl.BlockSpec((each, 1), lambda i, j, _: (i, 0)),
                pl.BlockSpec((4, width), lambda i, j, _: (0, 0)),
                pl.BlockSpec((units, ROW_UNIT, width), lambda i, j, _: (0, 4, 0)),
                part(5),
                part(9),
                pl.BlockSpec((FF_BLOCK // tall, tall, width), lambda i, j, _: (j, 0, 0)),
            ]
            + [pl.BlockSpec((each, lanes // PARTS), lambda i, j, _: (i, 0))] * len(mixed),
            out_specs=[mix] * team
            + [const, const, const, const, const, block, block, block]
            + [pl.BlockSpec((2, width), lambda i, j, _: (0, 0)), const],
            scratch_shapes=[
                pltpu.VMEM((each, width), F32),
                pltpu.VMEM((each, width), F32),
                pltpu.VMEM((each, 1), F32),
            ],
        ),
        out_shape=[shape((rows, lanes), BF16)] * team
        + [
            shape((rows, width), BF16),
            shape((rows, width), F32),
            shape((rows, width), BF16),
            shape((rows, width), BF16),
            shape((rows, width), BF16),
            shape((rows, ff), BF16),
            shape((rows, ff), BF16),
            shape((rows, ff), BF16),
            shape((2, width), F32),
            shape((rows, width), BF16),
        ],
        compiler_params=params(),
        cost_estimate=cost(
            12 * rows * width * ff + 4 * rows * width * width,
            12 * width * ff + 6 * rows * ff + 30 * rows * width,
            rows * ff,
        ),
        name="feed",
    )(at, tokens, cotangent, scale, vectors, weights, weights, weights, weights, *mixed)


def weight_kernel(core_ref, a_ref, b_ref, *refs, size):
    own_ref, away_ref, at_ref = refs[-3:]
    rows, tall = a_ref.shape
    core = core_ref[0]
    outs = (own_ref, away_ref)

    @pl.when(pl.program_id(1) == 0)
    def _():
        for side in range(2):
            half = core if side == 0 else 1 - core
            for c in range(tall // (2 * size)):
                start = pl.multiple_of((2 * c + half) * size, 128)
                at_ref[side, c * size : (c + 1) * size] = a_ref[:, pl.ds(start, size)].T

    wide = own_ref.shape[-1]
    for side in range(2):
        product = dot(at_ref[side], b_ref[...].reshape(rows, wide)).astype(BF16)
        outs[side][...] = product.reshape(own_ref.shape)


def weight_grad(core, a, b, chunk, shared=None, before=()):
    rows, tall = a.shape
    stacked = b.ndim == 3
    wide = b.shape[0] * b.shape[2] if stacked else b.shape[1]
    if chunk < 128:
        a = a.reshape(rows, tall // (2 * chunk), 2, chunk).swapaxes(1, 2).reshape(rows, tall)
        chunk = tall // 2
    columns = b.shape[2] if stacked else min(1024, wide)
    block = max(1024, 2 * chunk)
    if stacked:
        right = pl.BlockSpec((1, rows, columns), lambda i, j, _: (j, 0, 0))
    else:
        right = pl.BlockSpec((rows, columns), lambda i, j, _: (0, j))
    if shared:
        devices, height, at = shared
        one = tall // 2 // devices
        made = shape((devices, height, wide), BF16)
        out = pl.BlockSpec(
            (block // 2 // one, one, columns), lambda i, j, _: (i, at // one, j)
        )
    else:
        made = shape((tall // 2, wide), BF16)
        out = pl.BlockSpec((block // 2, columns), lambda i, j, _: (i, j))
    return pl.pallas_call(
        functools.partial(weight_kernel, size=chunk),
        grid_spec=pltpu.PrefetchScalarGridSpec(
            num_scalar_prefetch=1,
            grid=(tall // block, wide // columns),
            in_specs=[pl.BlockSpec((rows, block), lambda i, j, _: (0, i)), right]
            + [pl.BlockSpec(memory_space=pl.ANY)] * len(before),
            out_specs=[out, out],
            scratch_shapes=[pltpu.VMEM((2, block // 2, rows), BF16)],
        ),
        input_output_aliases={3: 0, 4: 1} if before else {},
        out_shape=[made] * 2,
        compiler_params=params(),
        cost_estimate=cost(2 * rows * tall * wide, 2 * (rows * tall + rows * wide + tall * wide)),
        name="weight_grad",
    )(core, a, b, *before)


def unturn_kernel(at_ref, c_ref, e_ref, l_ref, *refs, team):
    blocks, out_ref = refs[:-1], refs[-1]
    cosine, early, late = c_ref[...], e_ref[...], l_ref[...]
    which = pl.program_id(0)
    size = blocks[0].shape[-1]
    lanes = size * len(blocks) // team
    for i, ref in enumerate(blocks):
        for at in range(0, size, 128):
            first = (at_ref[0] ^ (i % team)) * lanes + i // team * size + at
            spot = pl.ds(pl.multiple_of(first, 128), 128)

            @pl.when(which < 2)
            def _(ref=ref, at=at, spot=spot):
                piece = turn(ref[0, :, at : at + 128].astype(F32), cosine, -early, -late)
                out_ref[0, :, spot] = piece.astype(BF16)

            @pl.when(which == 2)
            def _(ref=ref, at=at, spot=spot):
                out_ref[0, :, spot] = ref[0, :, at : at + 128]


def unturn(at, blocks, table, team):
    _, rows, lanes = blocks[0].shape
    wide = pl.BlockSpec((rows, 128), lambda j, _: (0, 0))
    count = len(blocks)
    return pl.pallas_call(
        functools.partial(unturn_kernel, team=team),
        grid_spec=pltpu.PrefetchScalarGridSpec(
            num_scalar_prefetch=1,
            grid=(3,),
            in_specs=[wide] * 3 + [pl.BlockSpec((1, rows, lanes), lambda j, _: (j, 0, 0))] * count,
            out_specs=pl.BlockSpec((1, rows, count * lanes), lambda j, _: (j, 0, 0)),
        ),
        out_shape=shape((3, rows, count * lanes), BF16),
        compiler_params=params(),
        cost_estimate=cost(0, 12 * rows * count * lanes),
        name="unturn",
    )(at, *table, *blocks)


def project_back_kernel(x_ref, gm_ref, vec_ref, w_ref, low_ref, *refs, part, lanes, first, last):
    which = pl.program_id(0)
    acc_ref = refs[-1]

    @pl.when(which == 0)
    def _():
        acc_ref[...] = jnp.zeros_like(acc_ref) if first else refs[0][...]

    width = w_ref.shape[-1]
    weight = jnp.concatenate(
        [
            w_ref[0, :, at : at + lanes]
            for at in range(part * lanes, width, PARTS * lanes)
        ],
        axis=1,
    )
    acc_ref[...] += dot(low_ref[0], weight, NT)

    if last:
        out_ref, sum_ref = refs[-3:-1]

        @pl.when(which == 2)
        def _():
            grad = acc_ref[...]
            normal, inverse = normalise(x_ref[...].astype(F32))
            sum_ref[0:1] = jnp.sum(grad * normal, axis=0, keepdims=True)
            sum_ref[1:2] = jnp.sum(grad, axis=0, keepdims=True)
            grad = gm_ref[...] + norm_back(grad, normal, inverse, vec_ref[0:1])
            out_ref[...] = grad.astype(BF16)


def project_back(tokens, grad_middle, vectors, weights, low, part, team, partial):
    rows, width = tokens.shape
    wide = low.shape[-1]
    last = part == PARTS - 1
    const = pl.BlockSpec((rows, width), lambda j: (0, 0))
    return pl.pallas_call(
        functools.partial(
            project_back_kernel, part=part, lanes=wide // team, first=not partial, last=last
        ),
        grid=(3,),
        in_specs=[
            const,
            const,
            pl.BlockSpec((4, width), lambda j: (0, 0)),
            pl.BlockSpec((1, width, width), lambda j: (j, 0, 0)),
            pl.BlockSpec((1, rows, wide), lambda j: (j, 0, 0)),
        ]
        + [const] * len(partial),
        out_specs=[const, pl.BlockSpec((2, width), lambda j: (0, 0))] if last else [const],
        out_shape=(
            [shape((rows, width), BF16), shape((2, width), F32)]
            if last
            else [shape((rows, width), F32)]
        ),
        scratch_shapes=[pltpu.VMEM((rows, width), F32)] if last else [],
        compiler_params=params(),
        cost_estimate=cost(6 * rows * width * wide, 18 * rows * width + 6 * width * width),
        name="project_back",
    )(tokens, grad_middle, vectors, weights, low, *partial)


def place_kernel(me_ref, *refs, masks, pieces):
    count = len(masks)
    halves, (wide_ref, small_ref, sem) = refs[: 2 * count], refs[2 * count :]
    me = me_ref[0]
    for wait in (False, True):
        for t in range(count):
            half = len(masks[t]) // 2
            for j, mask in enumerate(masks[t]):
                source = halves[2 * t + j // half].at[j % half]
                for lane, (first, size, which, to) in enumerate(pieces[t]):
                    origin = source.at[:, first : first + size]
                    if which is None:
                        place = small_ref.at[me ^ mask]
                    else:
                        place = wide_ref.at[which, me ^ mask, :, to : to + size]
                    copy = pltpu.make_async_copy(origin, place, sem.at[t, j, lane])
                    copy.wait() if wait else copy.start()


class Chain:
    def __init__(self, links, own, away, rounds, wire=BF16):
        self.links, self.rounds, self.wire = links, [list(r) for r in rounds], wire
        self.axes = [b for b in range(links.bits - 1, -1, -1) if b != links.core]
        self.dims = (2,) * len(self.axes)
        if own.ndim == 2:
            self.dims += (own.shape[0] * 2 // links.count,)
        self.dims += own.shape[1:]
        self.terms = [own.reshape(self.dims), links.swap(away, 1 << links.core).reshape(self.dims)]

    def hold(self, after):
        self.terms = tie(self.terms, after)
        return self

    def pick(self, mask):
        me, parts, axes = self.links.me() ^ mask, self.terms, list(self.axes)
        for bit in self.rounds[0]:
            at = axes.index(bit)
            parts = [
                lax.dynamic_index_in_dim(p, (me >> bit) & 1, at, keepdims=False) for p in parts
            ]
            axes.pop(at)
        return parts

    def split(self):
        self.masks = [0]
        for bit in self.rounds[0]:
            self.masks += [m | 1 << bit for m in self.masks]
        sent = [total(self.pick(m)).astype(self.wire) for m in self.masks[1:]]
        self.kept = self.pick(0)
        return sent

    def swap(self, sent):
        return [self.links.swap(v, m) for v, m in zip(sent, self.masks[1:])]

    def take(self, received):
        for bit in self.rounds.pop(0):
            self.axes.remove(bit)
        self.terms = self.kept + list(received)

    def result(self):
        return total(self.terms)


class Joined:
    def __init__(self, *chains):
        self.chains, self.links = chains, chains[0].links

    @property
    def rounds(self):
        return self.chains[0].rounds

    def split(self):
        sent = [c.split() for c in self.chains]
        return [jnp.concatenate(v, axis=-1) for v in zip(*sent)]

    def swap(self, sent):
        return self.chains[0].swap(sent)

    def take(self, received):
        first = 0
        for c in self.chains:
            last = first + c.terms[0].shape[-1]
            c.take([v[..., first:last] for v in received])
            first = last


def total(terms):
    return functools.reduce(jnp.add, [t.astype(F32) for t in terms])


def tie(values, *others):
    return lax.optimization_barrier((values, others))[0]


def begin(chains, values):
    sent = [c.split() for c in chains]
    values, sent = lax.optimization_barrier((values, sent))
    for c, v in zip(chains, sent):
        c.received = c.swap(v)
    return values


def finish(chains, after):
    received = tie([c.received for c in chains], after)
    for c, r in zip(chains, received):
        c.take(r)


class Links:
    def __init__(self, mesh):
        self.dp, self.seq = mesh.shape["dp"], mesh.shape["seq"]
        self.count = self.dp * self.seq
        self.bits = self.count.bit_length() - 1
        self.core = self.seq.bit_length() - 1
        seq_bits = list(range(self.core))
        dp_bits = list(range(self.core + 1, self.bits))
        self.dp_bits = [self.core] + dp_bits
        first, last = dp_bits[:1], dp_bits[1:]
        self.seq_first = [[b] for b in seq_bits + dp_bits[::-1]]
        self.seq_last = [[b] for b in seq_bits[::-1] + dp_bits[::-1]]
        self.dp_first = [[b] for b in first + seq_bits + last]
        self.seq_then = [seq_bits[:1], seq_bits[1:], dp_bits]
        self.direct = [seq_bits, dp_bits]
        self.orders = [
            seq_bits + dp_bits,
            seq_bits[::-1] + dp_bits,
            dp_bits[:1] + seq_bits + dp_bits[1:],
            dp_bits[:1] + seq_bits[::-1] + dp_bits[1:],
        ]

        self.team_bits = [self.core] + seq_bits[2:]
        self.team = 2 ** len(self.team_bits)

    def bit(self, which):
        return (self.me() >> which) & 1

    def route(self, k):
        pairs = []
        for i in range(self.count):
            core, y, x = (i >> self.core) & 1, (i >> 1) & 1, i & 1
            rest = i & ~((1 << self.core) | 3)
            pairs.append((i, rest | (y ^ (k >> 1)) << self.core | core << 1 | (x ^ (k & 1))))
        return pairs

    def to_team(self, value):
        wins, rows, width = value.shape
        blocks = value.reshape(wins * 2, rows // 2, width)
        place = 2 * self.bit(0) + self.bit(1)
        return [
            lax.dynamic_index_in_dim(blocks, place ^ (2 * (k & 1) + (k >> 1)), 0, keepdims=False)
            for k in range(4)
        ]

    def move_one(self, sent, k):
        return lax.ppermute(sent, BOTH, self.route(k))

    def move(self, sent):
        return [self.move_one(v, k) for k, v in enumerate(sent)]

    def from_team_blocks(self, value):
        rows, width = value.shape
        blocks = value.reshape(4, rows // 4, width)
        return [
            lax.dynamic_index_in_dim(blocks, self.base() ^ k, 0, keepdims=False) for k in range(4)
        ]

    def back_one(self, sent, k):
        return lax.ppermute(sent, BOTH, [(j, i) for i, j in self.route(k)])

    def in_place(self, received):
        return [received[k] for k in (0, 2, 1, 3)]

    def base(self):
        return 2 * self.bit(self.core) + self.bit(0)

    def member(self):
        return sum(self.bit(b) << i for i, b in enumerate(self.team_bits))

    def exchange(self, values):
        masks = [
            sum(1 << b for i, b in enumerate(self.team_bits) if m >> i & 1)
            for m in range(self.team)
        ]
        return [v if m == 0 else self.swap(v, masks[m]) for m, v in enumerate(values)]

    def me(self):
        return lax.axis_index("dp") * self.seq + lax.axis_index("seq")

    def swap(self, value, mask):
        return lax.ppermute(value, BOTH, [(i, i ^ mask) for i in range(self.count)])

    def own(self):
        return jnp.reshape(lax.axis_index("dp") % 2, (1,))

    def gather(self, values, pieces, width, counts, moved):
        orders = self.orders
        held, masks = [v[None] for v in values], [[0] for v in values]
        levels = self.bits - 1
        early = None
        (held, counts, moved) = lax.optimization_barrier((held, counts, moved))
        for level in range(levels):
            order = [o[levels - 1 - level] for o in orders]
            got = [self.swap(h, 1 << b) for h, b in zip(held, order)]
            masks = [m + [i | 1 << b for i in m] for m, b in zip(masks, order)]
            if level in (0, 2):
                moved[level : level + 2] = [
                    self.move_one(moved[k], k) for k in (level, level + 1)
                ]
            if level < len(self.dp_bits):
                counts = counts + self.swap(counts, 1 << self.dp_bits[level])
            held = [jnp.concatenate([h, g], axis=0) for h, g in zip(held, got)]
            if level in (1, 3):
                held, counts, moved = lax.optimization_barrier((held, counts, moved))
            else:
                held, counts = lax.optimization_barrier((held, counts))
            if level == 1:
                early = held
        got = [self.swap(h, 1 << self.core) for h in held]
        masks = [m + [i | 1 << self.core for i in m] for m in masks]
        args = [v for pair in zip(held, got) for v in pair]
        rows = values[0].shape[0]
        wide = (3, self.count, rows, width)
        narrow = (self.count, rows, 128)
        placed = pl.pallas_call(
            functools.partial(place_kernel, masks=masks, pieces=pieces),
            grid_spec=pltpu.PrefetchScalarGridSpec(
                num_scalar_prefetch=1,
                grid=(1,),
                in_specs=[pl.BlockSpec(memory_space=pl.ANY)] * len(args),
                out_specs=[
                    pl.BlockSpec(wide, lambda i, _: (0, 0, 0, 0)),
                    pl.BlockSpec(narrow, lambda i, _: (0, 0, 0)),
                ],
                scratch_shapes=[pltpu.SemaphoreType.DMA((len(values), self.count, 3))],
            ),
            out_shape=[shape(wide, BF16), shape(narrow, BF16)],
            compiler_params=params(),
            name="place",
        )(jnp.reshape(self.me(), (1,)), *args)
        return placed, early, counts, moved


def packed(w_down, w_out, w_gate, w_up, width):
    parts = [w_down, w_out]
    for weight in (w_gate, w_up):
        parts += [weight[:, c : c + width] for c in range(0, weight.shape[1], width)]
    return jnp.concatenate(parts, axis=0)


def regrouped(gathered, each, width):
    if each == ROW_UNIT:
        return gathered
    tall = 4 * each
    down = gathered[:, :tall].reshape(-1, 4 * ROW_UNIT, width)
    parts = [down]
    for at in range(tall, gathered.shape[1], each):
        parts.append(gathered[:, at : at + each].reshape(-1, ROW_UNIT, width))
    return jnp.concatenate(parts, axis=1)


def body(
    links,
    tokens,
    cotangent,
    lengths,
    species,
    ln1_gain,
    ln1_bias,
    w_query,
    w_key,
    w_value,
    w_out,
    ln2_gain,
    ln2_bias,
    w_gate,
    w_up,
    w_down,
):
    wins, rows, width = tokens.shape
    each = w_query.shape[0]
    team = links.team
    lanes = width // team
    share = wins * rows
    scalar = functools.partial(jnp.reshape, shape=(1,))
    member = links.member()
    base = scalar(links.base())

    small = jnp.stack([ln1_gain, ln1_bias, ln2_gain, ln2_bias], axis=1)
    small = jnp.pad(small, ((0, 0), (0, 124)))
    cut = width // 2
    local = [
        jnp.concatenate([w_query, w_key[:, :cut]], axis=1),
        jnp.concatenate([w_key[:, cut:], w_value, small], axis=1),
    ]
    pieces = [
        [(0, width, 0, 0), (width, cut, 1, 0)],
        [(0, cut, 1, cut), (cut, width, 2, 0), (cut + width, 128, None, 0)],
    ]
    species_ids = jnp.arange(SPECIES)
    onehot = (species[:, None] == species_ids[None, :]).astype(F32)
    counts = jnp.sum(onehot * lengths[:, None].astype(F32), axis=0)
    told = jnp.stack([lengths, species])
    told = jnp.stack([told, links.swap(told, 1 << links.core)])
    (qkv_w, small), early, counts, moved = links.gather(
        local, pieces, width, counts, links.to_team(tokens)
    )
    mine = packed(*tie((w_down, w_out, w_gate, w_up), early), width)
    weights = regrouped(lax.all_gather(mine, BOTH, axis=0), each, width)
    qkv_w = qkv_w.reshape(3, width, width)
    vectors = small.reshape(width, 128)[:, :4].T.astype(F32)

    told = lax.dynamic_index_in_dim(told, links.bit(1) ^ links.bit(links.core), 0, keepdims=False)
    told = lax.dynamic_index_in_dim(told, links.bit(0), 1, keepdims=False)
    length, kind = told[0], told[1]
    upper = member >> 1
    half = rows // 2
    block = (4 * upper + jnp.arange(4))[:, None] * rows + links.bit(links.core) * half
    positions = (block + jnp.arange(half)[None, :]).reshape(share)
    table = tables(positions)
    info = jnp.stack([length, member & 1, upper])

    rows_in = arrange(base, moved)
    projected = []
    for m in range(team)[::-1]:
        projected.append(project(scalar(member ^ m), rows_in, qkv_w, vectors, table, lanes))
    projected = projected[::-1]
    normed_one = projected[0][1]
    window_weight = SPECIES * jnp.sum((kind == species_ids) * counts) / jnp.sum(counts)
    row_scale = jnp.where(positions < length, window_weight, 0.0)[:, None]

    qkv = links.exchange([p[0] for p in projected])
    qkv, cot_sent = lax.optimization_barrier((qkv, links.to_team(cotangent)))
    cot_moved = links.move(cot_sent)
    mixed_heads, lse, mixed = [], [], []
    for part in range(PARTS):
        *heads, sums = attend(info, qkv, part)
        mixed_heads.append(heads)
        lse.append(sums)
        mixed += links.exchange(heads)
        if part == 0:
            qkv, cot_moved = lax.optimization_barrier((qkv, tie(cot_moved, sums)))
    cot_in = arrange(base, cot_moved)
    fed = feed(scalar(member), rows_in, cot_in, row_scale, mixed, vectors, weights)
    grad_mixed = fed[:team]
    (
        delta, grad_middle, grad_middle_low, normed_two, grad_low, hidden, grad_gate, grad_up,
        sums_two, mixed_rows,
    ) = fed[team:]
    grad_heads = links.exchange(grad_mixed)

    narrow, broad = width // links.dp, hidden.shape[1] // links.dp
    core = links.own()
    place = scalar(2 * links.bit(0) + links.bit(1))
    shared = (links.count // 2, 5 * each)
    grad_low, sent = lax.optimization_barrier((grad_low, links.from_team_blocks(delta)))
    returned = [links.back_one(sent[k], k) for k in range(2)]
    before = weight_grad(core, hidden, grad_low, broad, shared + (0,))
    low, returned = lax.optimization_barrier((tie(grad_middle_low, before), returned))
    own, away = weight_grad(core, mixed_rows, low, narrow, shared + (4 * each,), before)
    sum_rest = Chain(links, own, away, links.dp_first)
    grad_gate, sent = lax.optimization_barrier((tie(grad_gate, own), sent[2:]))
    returned += [links.back_one(v, k) for k, v in enumerate(sent, 2)]
    own, away = weight_grad(core, normed_two, grad_gate, narrow)
    sum_gate = Chain(links, own, away, links.seq_first)
    grad_up = begin([sum_rest.hold((own, returned))], tie(grad_up, own))
    own, away = weight_grad(core, normed_two, grad_up, narrow)
    sum_up = Chain(links, own, away, links.seq_last)

    def back(part, grads, sub=0, subs=1):
        return attend_back(
            info, qkv, mixed_heads[part], grads, lse[part], part, sub, subs
        )

    def through(part, low, partial):
        return project_back(rows_in, grad_middle, vectors, qkv_w, low, part, team, partial)

    grad_heads = begin([sum_gate.hold(own)], tie(list(grad_heads), own))
    output = settle(place, links.in_place(tie(returned, own)), [tokens])
    grad_heads = begin([sum_up.hold(output)], tie(list(grad_heads), output))
    made = back(0, grad_heads)
    received = links.exchange(made)
    finish([sum_rest, sum_gate, sum_up], made)
    received = begin([sum_gate, sum_up], tie(list(received), made))
    low = unturn(scalar(member), received, table, team)
    own_one, away_one = weight_grad(core, normed_one, low, narrow)
    sum_one = Chain(links, own_one, away_one, links.seq_then)
    (partial,) = through(0, tie(low, own_one), [])
    finish([sum_gate, sum_up], partial)
    if len(links.seq_first) == 4:
        sum_pair = [Joined(sum_gate, sum_up)]
    else:
        sum_pair = [sum_gate, sum_up]
    grad_heads = begin(sum_pair + [sum_rest], tie(list(grad_heads), partial))
    made = back(1, grad_heads)
    received = links.exchange(made)
    chains = sum_pair + [sum_rest]
    finish(chains, made)
    chains.append(sum_one.hold(partial))
    received = begin(chains, tie(list(received), made))
    low = unturn(scalar(member), received, table, team)
    grad_in, sums_one = through(1, low, [partial])
    finish(chains, grad_in)
    chains = [c for c in chains if c.rounds]
    low, sent = begin(chains, (low, links.from_team_blocks(grad_in)))
    home = [links.back_one(v, k) for k, v in enumerate(sent[:2])]
    own_two, away_two = weight_grad(core, normed_one, low, narrow)
    pending = chains
    gains = jnp.concatenate([sums_one, sums_two], axis=0)
    gains = gains.reshape(4, links.dp // 2, 2, width // links.dp).transpose(2, 1, 3, 0)
    gains = gains.reshape(2, width // 2, 4)
    gains = jnp.pad(gains, ((0, 0), (0, 0), (0, 124))).astype(BF16)
    gains = [
        lax.dynamic_index_in_dim(gains, c, 0, keepdims=False) for c in (core[0], 1 - core[0])
    ]
    (own_two, away_two, gains), home = lax.optimization_barrier(((own_two, away_two, gains), home))
    own = jnp.concatenate([own_two, gains[0]], axis=1)
    away = jnp.concatenate([away_two, gains[1]], axis=1)
    last = Chain(links, own, away, links.direct)
    nothing = begin([last], [])
    finish(pending + [last], nothing)
    home += [links.back_one(v, k) for k, v in enumerate(tie(sent[2:], last.terms), 2)]
    pieces = [c for c in sum_pair + [sum_rest] if c.rounds]
    chains = pieces + [Joined(sum_one, last)]
    while chains:
        nothing = begin(chains, [])
        finish(chains, nothing)
        chains = [c for c in chains if c.rounds]
    grad_tokens = settle(place, links.in_place(home), [])

    last = last.result()
    gains = last[:, -128:].T
    merged = jnp.stack([sum_one.result(), last[:, :-128]], axis=1)
    merged = merged.reshape(each, PARTS, 3, team, -1).transpose(0, 2, 3, 1, 4)
    merged = merged.reshape(each, 3, width)
    rest = sum_rest.result()
    return (
        output.reshape(wins, rows, width),
        grad_tokens.reshape(wins, rows, width),
        gains[0],
        gains[1],
        merged[:, 0],
        merged[:, 1],
        merged[:, 2],
        rest[4 * each :],
        gains[2],
        gains[3],
        sum_gate.result(),
        sum_up.result(),
        rest[: 4 * each],
    )


def solution(mesh):
    token = P("dp", "seq", None)
    vector = P(BOTH)
    matrix = P(BOTH, None)
    return jax.shard_map(
        functools.partial(body, Links(mesh)),
        mesh=mesh,
        in_specs=(
            (token, token, P("dp"), P("dp"), vector, vector)
            + (matrix,) * 4
            + (vector, vector)
            + (matrix,) * 3
        ),
        out_specs=(
            (token, token, vector, vector) + (matrix,) * 4 + (vector, vector) + (matrix,) * 3
        ),
        check_vma=False,
    )
```

```python
import functools

import jax
import jax.numpy as jnp
from jax import lax
from jax.experimental import pallas as pl
from jax.experimental.pallas import tpu as pltpu
from jax.sharding import PartitionSpec as P

HEAD_DIM = 64
SPECIES = 8
EPS = 1e-05
LOG2E = 1.4426950408889634
BOTH = ("dp", "seq")
F32 = jnp.float32
BF16 = jnp.bfloat16
FF_BLOCK = 512
FEED_ROWS = 512
PARTS = 2
ROW_UNIT = 32
VMEM = 60 * 2**20

NN = (((1,), (0,)), ((), ()))
NT = (((1,), (1,)), ((), ()))


def dot(a, b, dims=NN):
    return lax.dot_general(a, b, dims, preferred_element_type=F32)


def shape(dims, dtype):
    return jax.ShapeDtypeStruct(dims, dtype)


def params():
    return pltpu.CompilerParams(vmem_limit_bytes=VMEM)


def cost(flops, moved, exps=0):
    return pl.CostEstimate(flops=flops // 64, bytes_accessed=moved // 64, transcendentals=exps // 64)


def normalise(value):
    centered = value - jnp.mean(value, axis=-1, keepdims=True)
    inverse = lax.rsqrt(jnp.mean(centered * centered, axis=-1, keepdims=True) + EPS)
    return centered * inverse, inverse


def norm_back(grad, normal, inverse, gain):
    scaled = grad * gain
    centered = scaled - jnp.mean(scaled, axis=-1, keepdims=True)
    return inverse * (centered - normal * jnp.mean(scaled * normal, axis=-1, keepdims=True))


def turn(value, cosine, early, late):
    return value * cosine + pltpu.roll(value, 96, 1) * early + pltpu.roll(value, 32, 1) * late


def tables(positions):
    half = HEAD_DIM // 2
    freq = 10000.0 ** (-2.0 * jnp.arange(half, dtype=F32) / HEAD_DIM)
    angle = positions.astype(F32)[:, None] * freq[None, :]
    cosine, sine = jnp.cos(angle), jnp.sin(angle)
    zero = jnp.zeros_like(sine)
    return (
        jnp.concatenate([cosine] * 4, axis=1),
        jnp.concatenate([-sine, zero, -sine, zero], axis=1),
        jnp.concatenate([zero, sine, zero, sine], axis=1),
    )


def arrange_kernel(base_ref, *refs):
    for k, ref in enumerate(refs[:-1]):
        refs[-1][base_ref[0] ^ k] = ref[...]


def arrange(base, blocks):
    rows, width = blocks[0].shape
    return pl.pallas_call(
        arrange_kernel,
        grid_spec=pltpu.PrefetchScalarGridSpec(
            num_scalar_prefetch=1,
            grid=(1,),
            in_specs=[pl.BlockSpec((rows, width), lambda i, _: (0, 0))] * len(blocks),
            out_specs=pl.BlockSpec((len(blocks), rows, width), lambda i, _: (0, 0, 0)),
        ),
        out_shape=shape((len(blocks), rows, width), blocks[0].dtype),
        compiler_params=params(),
        cost_estimate=cost(0, 16 * rows * width),
        name="arrange",
    )(base, *blocks).reshape(len(blocks) * rows, width)


def settle_kernel(base_ref, *refs):
    blocks, added, out_ref = refs[:4], refs[4:-1], refs[-1]
    here = pl.program_id(0)

    for k, ref in enumerate(blocks):

        @pl.when((base_ref[0] ^ k) == here)
        def _(ref=ref):
            value = ref[...].astype(F32)
            out_ref[0] = value + added[0][0].astype(F32) if added else value


def settle(base, blocks, added):
    rows, width = blocks[0].shape
    block = pl.BlockSpec((1, rows, width), lambda i, _: (i, 0, 0))
    return pl.pallas_call(
        settle_kernel,
        grid_spec=pltpu.PrefetchScalarGridSpec(
            num_scalar_prefetch=1,
            grid=(4,),
            in_specs=[pl.BlockSpec((rows, width), lambda i, _: (0, 0))] * 4
            + [block] * len(added),
            out_specs=block,
        ),
        out_shape=shape((4, rows, width), F32),
        compiler_params=params(),
        cost_estimate=cost(0, 32 * rows * width),
        name="settle",
    )(base, *blocks, *[a.reshape(4, rows, width) for a in added])


def project_kernel(at_ref, x_ref, w_ref, vec_ref, c_ref, e_ref, l_ref, send_ref, n_ref):
    which = pl.program_id(0)
    _, rows, lanes = send_ref.shape

    @pl.when(which == 0)
    def _():
        normal, _ = normalise(x_ref[...].astype(F32))
        n_ref[...] = (normal * vec_ref[0:1] + vec_ref[1:2]).astype(BF16)

    product = dot(n_ref[...], w_ref[0])
    cosine, early, late = c_ref[...], e_ref[...], l_ref[...]

    def put(rotate):
        for at in range(0, lanes, 128):
            piece = product[:, at : at + 128]
            if rotate:
                piece = turn(piece, cosine, early, late)
            send_ref[0, :, at : at + 128] = piece.astype(BF16)

    pl.when(which < 2)(lambda: put(True))
    pl.when(which == 2)(lambda: put(False))


def project(at, tokens, weights, vectors, table, lanes):
    rows, width = tokens.shape
    wide = pl.BlockSpec((rows, 128), lambda j, _: (0, 0))
    return pl.pallas_call(
        project_kernel,
        grid_spec=pltpu.PrefetchScalarGridSpec(
            num_scalar_prefetch=1,
            grid=(3,),
            in_specs=[
                pl.BlockSpec((rows, width), lambda j, _: (0, 0)),
                pl.BlockSpec((1, width, lanes), lambda j, at: (j, 0, at[0])),
                pl.BlockSpec((4, width), lambda j, _: (0, 0)),
                wide,
                wide,
                wide,
            ],
            out_specs=[
                pl.BlockSpec((1, rows, lanes), lambda j, _: (j, 0, 0)),
                pl.BlockSpec((rows, width), lambda j, _: (0, 0)),
            ],
        ),
        out_shape=[shape((3, rows, lanes), BF16), shape((rows, width), BF16)],
        compiler_params=params(),
        cost_estimate=cost(6 * rows * width * lanes, 6 * rows * lanes + 6 * width * lanes),
        name="project",
    )(at, tokens, weights, vectors, *table)


def attend_kernel(info_ref, *refs, team):
    q_refs, k_refs, v_refs = refs[:team], refs[team : 2 * team], refs[2 * team : 3 * team]
    o_refs, (l_ref, vt_ref) = refs[3 * team : 4 * team], refs[4 * team :]
    length, side, upper = info_ref[0], info_ref[1], info_ref[2]
    lane = lax.broadcasted_iota(jnp.int32, (1, 128), 1)
    block = q_refs[0].shape[0]
    keys, ups = 2 * block, team // 2
    up = pl.program_id(2)

    def chunk(arrays, p, b):
        rows = slice(b * block, (b + 1) * block)
        return jnp.concatenate([arrays[2 * p][rows], arrays[2 * p + 1][rows]], axis=0)

    @pl.when((pl.program_id(1) == 0) & (up == 0))
    def _():
        for p in range(ups):
            for b in range(4):
                at = (4 * p + b) * keys
                vt_ref[:, at : at + keys] = chunk(v_refs, p, b).T

    q2 = jnp.concatenate([q_refs[0][...], q_refs[1][...]], axis=0)
    for p in range(1, ups):
        other = jnp.concatenate([q_refs[2 * p][...], q_refs[2 * p + 1][...]], axis=0)
        q2 = jnp.where(up == p, other, q2)
    q2 = q2 * BF16(0.125)

    def positions(p, b):
        row = lax.broadcasted_iota(jnp.int32, (keys, keys), 0)
        return row ^ (side * block) | (4 * (upper ^ p) + b) * keys

    def run(chunks):
        k2 = jnp.concatenate([chunk(k_refs, c // 4, c % 4) for c in range(chunks)], axis=0)
        n = chunks * keys
        outs = []
        for h in range(2):
            qh = jnp.where((lane // 64) == h, q2, BF16(0))
            s = dot(k2, qh, NT)
            if ups == 1:
                last = jnp.where(positions(0, chunks - 1) < length, s[n - keys :], -1e30)
                s = jnp.concatenate([s[: n - keys], last], 0) if chunks > 1 else last
            else:
                valid = [positions(c // 4, c % 4) < length for c in range(chunks)]
                s = jnp.concatenate(
                    [jnp.where(v, s[c * keys : (c + 1) * keys], -1e30) for c, v in enumerate(valid)],
                    axis=0,
                )
            m = jnp.max(s, axis=0, keepdims=True)
            p = jnp.exp2((s - m) * LOG2E)
            all_p = jnp.sum(p, axis=0, keepdims=True)
            o = dot(vt_ref[h * 64 : h * 64 + 64, :n], p.astype(BF16))
            outs.append(o / all_p)
            l_ref[0, h : h + 1] = m + jnp.log(all_p)
        result = jnp.concatenate(outs, 0).T.astype(BF16)
        for p in range(ups):

            @pl.when(up == p)
            def _(p=p):
                o_refs[2 * p][...] = result[:block]
                o_refs[2 * p + 1][...] = result[block:]

    if ups == 1:
        blocks = (length + keys - 1) // keys
        for i in range(4):
            pl.when(blocks == i + 1)(functools.partial(run, i + 1))
    else:
        run(4 * ups)


def attend(info, qkv, part):
    team = len(qkv)
    _, rows, lanes = qkv[0].shape
    span, pairs, ups = team * rows, lanes // 128 // PARTS, team // 2
    block = rows // 4

    def whole(which):
        return [
            pl.BlockSpec((None, rows, 128), lambda h, b, u, _: (which, 0, part * pairs + h))
        ] * team

    return pl.pallas_call(
        functools.partial(attend_kernel, team=team),
        grid_spec=pltpu.PrefetchScalarGridSpec(
            num_scalar_prefetch=1,
            grid=(pairs, 4, ups),
            in_specs=[
                pl.BlockSpec((None, block, 128), lambda h, b, u, _: (0, b, part * pairs + h))
            ]
            * team
            + whole(1)
            + whole(2),
            out_specs=[pl.BlockSpec((block, 128), lambda h, b, u, _: (b, h))] * team
            + [pl.BlockSpec((1, 2, 2 * block), lambda h, b, u, _: (h, 0, b * ups + u))],
            scratch_shapes=[pltpu.VMEM((128, span), BF16)],
        ),
        out_shape=[shape((rows, pairs * 128), BF16)] * team + [shape((pairs, 2, span), F32)],
        compiler_params=params(),
        cost_estimate=cost(
            16 * span * span * pairs * 128, 8 * span * pairs * 128, 2 * span * span * pairs
        ),
        name="attend",
    )(info, *qkv, *qkv, *qkv)


def attend_back_kernel(info_ref, *refs, team):
    q_refs, k_refs, v_refs, o_refs, g_refs = (refs[i * team : (i + 1) * team] for i in range(5))
    l_ref, d_refs = refs[5 * team], refs[5 * team + 1 : 6 * team + 1]
    kt_ref, dk_ref, dv_ref = refs[6 * team + 1 :]
    length, side, upper = info_ref[0], info_ref[1], info_ref[2]
    lane = lax.broadcasted_iota(jnp.int32, (1, 128), 1)
    block = q_refs[0].shape[0]
    keys, ups = 2 * block, team // 2
    b, up = pl.program_id(1), pl.program_id(2)
    first = (4 * (upper ^ up) + b) * keys

    def chunk(arrays, p, c):
        rows = pl.ds(pl.multiple_of(c * block, block), block)
        return jnp.concatenate([arrays[2 * p][rows], arrays[2 * p + 1][rows]], axis=0)

    def queries(arrays):
        value = jnp.concatenate([arrays[0][...], arrays[1][...]], axis=0)
        for p in range(1, ups):
            other = jnp.concatenate([arrays[2 * p][...], arrays[2 * p + 1][...]], axis=0)
            value = jnp.where(up == p, other, value)
        return value

    @pl.when((b == 0) & (up == 0))
    def _():
        for p in range(ups):
            for c in range(4):
                at = (4 * p + c) * keys
                kt_ref[:, at : at + keys] = (chunk(k_refs, p, c) * BF16(0.125)).T
        dk_ref[...] = jnp.zeros_like(dk_ref)
        dv_ref[...] = jnp.zeros_like(dv_ref)

    here = pl.ds(pl.multiple_of(b * block, block), block)

    def put(value):
        for p in range(ups):

            @pl.when(up == p)
            def _(p=p):
                d_refs[2 * p][0, here] = value[:block]
                d_refs[2 * p + 1][0, here] = value[block:]

    @pl.when(first >= length)
    def _():
        put(jnp.zeros((keys, 128), BF16))

    @pl.when(first < length)
    def _():
        q2 = queries(q_refs) * BF16(0.125)
        g2 = queries(g_refs)
        products = (g2.astype(F32) * queries(o_refs).astype(F32)).T
        qs, gs, ls, ds = [], [], [], []
        for h in range(2):
            mine = (lane // 64) == h
            qs.append(jnp.where(mine, q2, BF16(0)))
            gs.append(jnp.where(mine, g2, BF16(0)))
            ls.append(l_ref[0, h : h + 1] * LOG2E)
            ds.append(jnp.sum(products[h * 64 : h * 64 + 64], axis=0, keepdims=True))
        qc = jnp.concatenate(qs, 0)
        gc = jnp.concatenate(gs, 0)
        lc = jnp.concatenate(ls, 1)
        dc = jnp.concatenate(ds, 1)
        acc = (jnp.zeros((64, keys), F32),) * 2
        for p in range(ups):
            start = 4 * (upper ^ p) * keys

            def step(c, acc, masked, p=p, start=start):
                sl = pl.ds(pl.multiple_of((4 * p + c) * keys, keys), keys)
                k2 = chunk(k_refs, p, c)
                v2 = chunk(v_refs, p, c)
                prob = jnp.exp2(dot(k2, qc, NT) * LOG2E - lc)
                if masked:
                    row = lax.broadcasted_iota(jnp.int32, (keys, 1), 0)
                    row = row ^ (side * block) | (start + c * keys)
                    prob = jnp.where(row < length, prob, 0.0)
                gp = dot(v2, gc, NT)
                gs_low = (prob * (gp - dc)).astype(BF16)
                dv_ref[sl] += dot(prob.astype(BF16), gc)
                dk_ref[sl] += dot(gs_low, qc)
                return tuple(
                    acc[h]
                    + dot(kt_ref[h * 64 : h * 64 + 64, sl], gs_low[:, h * keys : (h + 1) * keys])
                    for h in range(2)
                )

            valid = jnp.clip(length - start, 0, 4 * keys)
            full = valid // keys
            acc = lax.fori_loop(0, full, lambda c, a: step(c, a, False), acc)
            acc = lax.cond(
                full * keys < valid, lambda a: step(full, a, True), lambda a: a, acc
            )
        put(jnp.concatenate(acc, 0).T.astype(BF16))

    @pl.when((b == 3) & (up == ups - 1))
    def _():
        for p in range(ups):
            for c in range(4):
                at = (4 * p + c) * keys
                for t, ref in ((1, dk_ref), (2, dv_ref)):
                    for m in range(2):
                        rows = slice(c * block, (c + 1) * block)
                        piece = ref[at + m * block : at + (m + 1) * block]
                        d_refs[2 * p + m][t, rows] = piece.astype(BF16)


def attend_back(info, qkv, mixed, grad, lse, part, sub, subs):
    team = len(qkv)
    _, rows, lanes = qkv[0].shape
    span, pairs, ups = team * rows, lanes // 128 // PARTS // subs, team // 2
    start, near = (part * subs + sub) * pairs, sub * pairs
    block = rows // 4
    spot = pl.BlockSpec((block, 128), lambda h, b, u, _: (b, start + h))

    def whole(which):
        return [
            pl.BlockSpec((None, rows, 128), lambda h, b, u, _: (which, 0, start + h))
        ] * team

    return pl.pallas_call(
        functools.partial(attend_back_kernel, team=team),
        grid_spec=pltpu.PrefetchScalarGridSpec(
            num_scalar_prefetch=1,
            grid=(pairs, 4, ups),
            in_specs=[
                pl.BlockSpec((None, block, 128), lambda h, b, u, _: (0, b, start + h))
            ]
            * team
            + whole(1)
            + whole(2)
            + [pl.BlockSpec((block, 128), lambda h, b, u, _: (b, near + h))] * team
            + [spot] * team
            + [pl.BlockSpec((1, 2, 2 * block), lambda h, b, u, _: (near + h, 0, b * ups + u))],
            out_specs=[pl.BlockSpec((3, rows, 128), lambda h, b, u, _: (0, 0, h))] * team,
            scratch_shapes=[
                pltpu.VMEM((128, span), BF16),
                pltpu.VMEM((span, 128), F32),
                pltpu.VMEM((span, 128), F32),
            ],
        ),
        out_shape=[shape((3, rows, pairs * 128), BF16)] * team,
        compiler_params=params(),
        cost_estimate=cost(
            30 * span * span * pairs * 128, 16 * span * pairs * 128, 2 * span * span * pairs
        ),
        name="attend_back",
    )(info, *qkv, *qkv, *qkv, *mixed, *grad, lse)


def feed_kernel(
    at_ref, x_ref, cot_ref, scale_ref, vec_ref, wo_ref, wg_ref, wu_ref, wd_ref, *refs, team
):
    mix_refs, send_refs = refs[: team * PARTS], refs[team * PARTS : team * (PARTS + 1)]
    (
        delta_ref, gm_ref, gml_ref, n_ref, gl_ref, hid_ref, gg_ref, gu_ref, sum_ref, rows_ref,
        acc_ref, normal_ref, inv_ref,
    ) = refs[team * (PARTS + 1) :]
    step = pl.program_id(1)
    lanes = send_refs[0].shape[1]
    some = mix_refs[0].shape[1]

    def whole(ref):
        return ref[...].reshape(-1, ref.shape[-1])

    def spot(m, first, size):
        return pl.ds(pl.multiple_of((at_ref[0] ^ m) * lanes + first, size), size)

    @pl.when(step == 0)
    def _():
        for i, ref in enumerate(mix_refs):
            rows_ref[:, spot(i % team, i // team * some, some)] = ref[...]
        added = dot(rows_ref[...], whole(wo_ref))
        acc_ref[...] = added
        normal, inverse = normalise(x_ref[...].astype(F32) + added)
        normal_ref[...] = normal
        inv_ref[...] = inverse
        n_ref[...] = (normal * vec_ref[2:3] + vec_ref[3:4]).astype(BF16)
        gl_ref[...] = (cot_ref[...].astype(F32) * scale_ref[...]).astype(BF16)
        gm_ref[...] = jnp.zeros_like(gm_ref)

    wg, wu, wd = whole(wg_ref), whole(wu_ref), whole(wd_ref)
    normed = n_ref[...]
    gate = dot(normed, wg)
    upper = dot(normed, wu)
    sigma = jax.nn.sigmoid(gate)
    silu = gate * sigma
    hidden = (silu * upper).astype(BF16)
    hid_ref[...] = hidden
    grad_hidden = dot(gl_ref[...], wd, NT)
    grad_up = (grad_hidden * silu).astype(BF16)
    grad_gate = (grad_hidden * upper * sigma * (1.0 + gate * (1.0 - sigma))).astype(BF16)
    gu_ref[...] = grad_up
    gg_ref[...] = grad_gate
    acc_ref[...] += dot(hidden, wd)
    gm_ref[...] += dot(grad_gate, wg, NT) + dot(grad_up, wu, NT)

    @pl.when(step == pl.num_programs(1) - 1)
    def _():
        delta_ref[...] = acc_ref[...].astype(BF16)
        grad = gm_ref[...]
        normal = normal_ref[...]

        @pl.when(pl.program_id(0) == 0)
        def _():
            sum_ref[...] = jnp.zeros_like(sum_ref)

        sum_ref[0:1] += jnp.sum(grad * normal, axis=0, keepdims=True)
        sum_ref[1:2] += jnp.sum(grad, axis=0, keepdims=True)
        total_grad = cot_ref[...].astype(F32) * scale_ref[...] + norm_back(
            grad, normal, inv_ref[...], vec_ref[2:3]
        )
        gm_ref[...] = total_grad
        low = total_grad.astype(BF16)
        gml_ref[...] = low
        acc_ref[...] = dot(low, whole(wo_ref), NT)
        for m in range(team):
            send_refs[m][...] = acc_ref[:, spot(m, 0, lanes)].astype(BF16)


def feed(at, tokens, cotangent, scale, mixed, vectors, weights):
    team = len(mixed) // PARTS
    rows, width = tokens.shape
    lanes = width // team
    units = weights.shape[0]
    tall = 4 * ROW_UNIT
    ff = units * tall
    columns = width // FF_BLOCK
    each = min(FEED_ROWS, rows)
    const = pl.BlockSpec((each, width), lambda i, j, _: (i, 0))
    block = pl.BlockSpec((each, FF_BLOCK), lambda i, j, _: (i, j))
    mix = pl.BlockSpec((each, lanes), lambda i, j, _: (i, 0))

    def part(first):
        return pl.BlockSpec(
            (units, ROW_UNIT, FF_BLOCK), lambda i, j, _: (0, first + j // columns, j % columns)
        )

    return pl.pallas_call(
        functools.partial(feed_kernel, team=team),
        grid_spec=pltpu.PrefetchScalarGridSpec(
            num_scalar_prefetch=1,
            grid=(rows // each, ff // FF_BLOCK),
            in_specs=[
                const,
                const,
                pl.BlockSpec((each, 1), lambda i, j, _: (i, 0)),
                pl.BlockSpec((4, width), lambda i, j, _: (0, 0)),
                pl.BlockSpec((units, ROW_UNIT, width), lambda i, j, _: (0, 4, 0)),
                part(5),
                part(9),
                pl.BlockSpec((FF_BLOCK // tall, tall, width), lambda i, j, _: (j, 0, 0)),
            ]
            + [pl.BlockSpec((each, lanes // PARTS), lambda i, j, _: (i, 0))] * len(mixed),
            out_specs=[mix] * team
            + [const, const, const, const, const, block, block, block]
            + [pl.BlockSpec((2, width), lambda i, j, _: (0, 0)), const],
            scratch_shapes=[
                pltpu.VMEM((each, width), F32),
                pltpu.VMEM((each, width), F32),
                pltpu.VMEM((each, 1), F32),
            ],
        ),
        out_shape=[shape((rows, lanes), BF16)] * team
        + [
            shape((rows, width), BF16),
            shape((rows, width), F32),
            shape((rows, width), BF16),
            shape((rows, width), BF16),
            shape((rows, width), BF16),
            shape((rows, ff), BF16),
            shape((rows, ff), BF16),
            shape((rows, ff), BF16),
            shape((2, width), F32),
            shape((rows, width), BF16),
        ],
        compiler_params=params(),
        cost_estimate=cost(
            12 * rows * width * ff + 4 * rows * width * width,
            12 * width * ff + 6 * rows * ff + 30 * rows * width,
            rows * ff,
        ),
        name="feed",
    )(at, tokens, cotangent, scale, vectors, weights, weights, weights, weights, *mixed)


def weight_kernel(core_ref, a_ref, b_ref, *refs, size):
    own_ref, away_ref, at_ref = refs[-3:]
    rows, tall = a_ref.shape
    core = core_ref[0]
    outs = (own_ref, away_ref)

    @pl.when(pl.program_id(1) == 0)
    def _():
        for side in range(2):
            half = core if side == 0 else 1 - core
            for c in range(tall // (2 * size)):
                start = pl.multiple_of((2 * c + half) * size, 128)
                at_ref[side, c * size : (c + 1) * size] = a_ref[:, pl.ds(start, size)].T

    wide = own_ref.shape[-1]
    for side in range(2):
        product = dot(at_ref[side], b_ref[...].reshape(rows, wide)).astype(BF16)
        outs[side][...] = product.reshape(own_ref.shape)


def weight_grad(core, a, b, chunk, shared=None, before=()):
    rows, tall = a.shape
    stacked = b.ndim == 3
    wide = b.shape[0] * b.shape[2] if stacked else b.shape[1]
    if chunk < 128:
        a = a.reshape(rows, tall // (2 * chunk), 2, chunk).swapaxes(1, 2).reshape(rows, tall)
        chunk = tall // 2
    columns = b.shape[2] if stacked else min(1024, wide)
    block = max(1024, 2 * chunk)
    if stacked:
        right = pl.BlockSpec((1, rows, columns), lambda i, j, _: (j, 0, 0))
    else:
        right = pl.BlockSpec((rows, columns), lambda i, j, _: (0, j))
    if shared:
        devices, height, at = shared
        one = tall // 2 // devices
        made = shape((devices, height, wide), BF16)
        out = pl.BlockSpec(
            (block // 2 // one, one, columns), lambda i, j, _: (i, at // one, j)
        )
    else:
        made = shape((tall // 2, wide), BF16)
        out = pl.BlockSpec((block // 2, columns), lambda i, j, _: (i, j))
    return pl.pallas_call(
        functools.partial(weight_kernel, size=chunk),
        grid_spec=pltpu.PrefetchScalarGridSpec(
            num_scalar_prefetch=1,
            grid=(tall // block, wide // columns),
            in_specs=[pl.BlockSpec((rows, block), lambda i, j, _: (0, i)), right]
            + [pl.BlockSpec(memory_space=pl.ANY)] * len(before),
            out_specs=[out, out],
            scratch_shapes=[pltpu.VMEM((2, block // 2, rows), BF16)],
        ),
        input_output_aliases={3: 0, 4: 1} if before else {},
        out_shape=[made] * 2,
        compiler_params=params(),
        cost_estimate=cost(2 * rows * tall * wide, 2 * (rows * tall + rows * wide + tall * wide)),
        name="weight_grad",
    )(core, a, b, *before)


def unturn_kernel(at_ref, c_ref, e_ref, l_ref, *refs, team):
    blocks, out_ref = refs[:-1], refs[-1]
    cosine, early, late = c_ref[...], e_ref[...], l_ref[...]
    which = pl.program_id(0)
    size = blocks[0].shape[-1]
    lanes = size * len(blocks) // team
    for i, ref in enumerate(blocks):
        for at in range(0, size, 128):
            first = (at_ref[0] ^ (i % team)) * lanes + i // team * size + at
            spot = pl.ds(pl.multiple_of(first, 128), 128)

            @pl.when(which < 2)
            def _(ref=ref, at=at, spot=spot):
                piece = turn(ref[0, :, at : at + 128].astype(F32), cosine, -early, -late)
                out_ref[0, :, spot] = piece.astype(BF16)

            @pl.when(which == 2)
            def _(ref=ref, at=at, spot=spot):
                out_ref[0, :, spot] = ref[0, :, at : at + 128]


def unturn(at, blocks, table, team):
    _, rows, lanes = blocks[0].shape
    wide = pl.BlockSpec((rows, 128), lambda j, _: (0, 0))
    count = len(blocks)
    return pl.pallas_call(
        functools.partial(unturn_kernel, team=team),
        grid_spec=pltpu.PrefetchScalarGridSpec(
            num_scalar_prefetch=1,
            grid=(3,),
            in_specs=[wide] * 3 + [pl.BlockSpec((1, rows, lanes), lambda j, _: (j, 0, 0))] * count,
            out_specs=pl.BlockSpec((1, rows, count * lanes), lambda j, _: (j, 0, 0)),
        ),
        out_shape=shape((3, rows, count * lanes), BF16),
        compiler_params=params(),
        cost_estimate=cost(0, 12 * rows * count * lanes),
        name="unturn",
    )(at, *table, *blocks)


def project_back_kernel(x_ref, gm_ref, vec_ref, w_ref, low_ref, *refs, part, lanes, first, last):
    which = pl.program_id(0)
    acc_ref = refs[-1]

    @pl.when(which == 0)
    def _():
        acc_ref[...] = jnp.zeros_like(acc_ref) if first else refs[0][...]

    width = w_ref.shape[-1]
    weight = jnp.concatenate(
        [
            w_ref[0, :, at : at + lanes]
            for at in range(part * lanes, width, PARTS * lanes)
        ],
        axis=1,
    )
    acc_ref[...] += dot(low_ref[0], weight, NT)

    if last:
        out_ref, sum_ref = refs[-3:-1]

        @pl.when(which == 2)
        def _():
            grad = acc_ref[...]
            normal, inverse = normalise(x_ref[...].astype(F32))
            sum_ref[0:1] = jnp.sum(grad * normal, axis=0, keepdims=True)
            sum_ref[1:2] = jnp.sum(grad, axis=0, keepdims=True)
            grad = gm_ref[...] + norm_back(grad, normal, inverse, vec_ref[0:1])
            out_ref[...] = grad.astype(BF16)


def project_back(tokens, grad_middle, vectors, weights, low, part, team, partial):
    rows, width = tokens.shape
    wide = low.shape[-1]
    last = part == PARTS - 1
    const = pl.BlockSpec((rows, width), lambda j: (0, 0))
    return pl.pallas_call(
        functools.partial(
            project_back_kernel, part=part, lanes=wide // team, first=not partial, last=last
        ),
        grid=(3,),
        in_specs=[
            const,
            const,
            pl.BlockSpec((4, width), lambda j: (0, 0)),
            pl.BlockSpec((1, width, width), lambda j: (j, 0, 0)),
            pl.BlockSpec((1, rows, wide), lambda j: (j, 0, 0)),
        ]
        + [const] * len(partial),
        out_specs=[const, pl.BlockSpec((2, width), lambda j: (0, 0))] if last else [const],
        out_shape=(
            [shape((rows, width), BF16), shape((2, width), F32)]
            if last
            else [shape((rows, width), F32)]
        ),
        scratch_shapes=[pltpu.VMEM((rows, width), F32)] if last else [],
        compiler_params=params(),
        cost_estimate=cost(6 * rows * width * wide, 18 * rows * width + 6 * width * width),
        name="project_back",
    )(tokens, grad_middle, vectors, weights, low, *partial)


def place_kernel(me_ref, *refs, masks, pieces):
    count = len(masks)
    halves, (wide_ref, small_ref, sem) = refs[: 2 * count], refs[2 * count :]
    me = me_ref[0]
    for wait in (False, True):
        for t in range(count):
            half = len(masks[t]) // 2
            for j, mask in enumerate(masks[t]):
                source = halves[2 * t + j // half].at[j % half]
                for lane, (first, size, which, to) in enumerate(pieces[t]):
                    origin = source.at[:, first : first + size]
                    if which is None:
                        place = small_ref.at[me ^ mask]
                    else:
                        place = wide_ref.at[which, me ^ mask, :, to : to + size]
                    copy = pltpu.make_async_copy(origin, place, sem.at[t, j, lane])
                    copy.wait() if wait else copy.start()


class Chain:
    def __init__(self, links, own, away, rounds, wire=BF16):
        self.links, self.rounds, self.wire = links, [list(r) for r in rounds], wire
        self.axes = [b for b in range(links.bits - 1, -1, -1) if b != links.core]
        self.dims = (2,) * len(self.axes)
        if own.ndim == 2:
            self.dims += (own.shape[0] * 2 // links.count,)
        self.dims += own.shape[1:]
        self.terms = [own.reshape(self.dims), links.swap(away, 1 << links.core).reshape(self.dims)]

    def hold(self, after):
        self.terms = tie(self.terms, after)
        return self

    def pick(self, mask):
        me, parts, axes = self.links.me() ^ mask, self.terms, list(self.axes)
        for bit in self.rounds[0]:
            at = axes.index(bit)
            parts = [
                lax.dynamic_index_in_dim(p, (me >> bit) & 1, at, keepdims=False) for p in parts
            ]
            axes.pop(at)
        return parts

    def split(self):
        self.masks = [0]
        for bit in self.rounds[0]:
            self.masks += [m | 1 << bit for m in self.masks]
        sent = [total(self.pick(m)).astype(self.wire) for m in self.masks[1:]]
        self.kept = self.pick(0)
        return sent

    def swap(self, sent):
        return [self.links.swap(v, m) for v, m in zip(sent, self.masks[1:])]

    def take(self, received):
        for bit in self.rounds.pop(0):
            self.axes.remove(bit)
        self.terms = self.kept + list(received)

    def result(self):
        return total(self.terms)


class Joined:
    def __init__(self, *chains):
        self.chains, self.links = chains, chains[0].links

    @property
    def rounds(self):
        return self.chains[0].rounds

    def split(self):
        sent = [c.split() for c in self.chains]
        return [jnp.concatenate(v, axis=-1) for v in zip(*sent)]

    def swap(self, sent):
        return self.chains[0].swap(sent)

    def take(self, received):
        first = 0
        for c in self.chains:
            last = first + c.terms[0].shape[-1]
            c.take([v[..., first:last] for v in received])
            first = last


def total(terms):
    return functools.reduce(jnp.add, [t.astype(F32) for t in terms])


def tie(values, *others):
    return lax.optimization_barrier((values, others))[0]


def begin(chains, values):
    sent = [c.split() for c in chains]
    values, sent = lax.optimization_barrier((values, sent))
    for c, v in zip(chains, sent):
        c.received = c.swap(v)
    return values


def finish(chains, after):
    received = tie([c.received for c in chains], after)
    for c, r in zip(chains, received):
        c.take(r)


class Links:
    def __init__(self, mesh):
        self.dp, self.seq = mesh.shape["dp"], mesh.shape["seq"]
        self.count = self.dp * self.seq
        self.bits = self.count.bit_length() - 1
        self.core = self.seq.bit_length() - 1
        seq_bits = list(range(self.core))
        dp_bits = list(range(self.core + 1, self.bits))
        self.dp_bits = [self.core] + dp_bits
        first, last = dp_bits[:1], dp_bits[1:]
        self.seq_first = [[b] for b in seq_bits + dp_bits[::-1]]
        self.seq_last = [[b] for b in seq_bits[::-1] + dp_bits[::-1]]
        self.dp_first = [[b] for b in first + seq_bits + last]
        self.seq_then = [seq_bits[:1], seq_bits[1:], dp_bits]
        self.direct = [seq_bits, dp_bits]
        self.orders = [
            seq_bits + dp_bits,
            seq_bits[::-1] + dp_bits,
            dp_bits[:1] + seq_bits + dp_bits[1:],
            dp_bits[:1] + seq_bits[::-1] + dp_bits[1:],
        ]

        self.team_bits = [self.core] + seq_bits[2:]
        self.team = 2 ** len(self.team_bits)

    def bit(self, which):
        return (self.me() >> which) & 1

    def route(self, k):
        pairs = []
        for i in range(self.count):
            core, y, x = (i >> self.core) & 1, (i >> 1) & 1, i & 1
            rest = i & ~((1 << self.core) | 3)
            pairs.append((i, rest | (y ^ (k >> 1)) << self.core | core << 1 | (x ^ (k & 1))))
        return pairs

    def to_team(self, value):
        wins, rows, width = value.shape
        blocks = value.reshape(wins * 2, rows // 2, width)
        place = 2 * self.bit(0) + self.bit(1)
        return [
            lax.dynamic_index_in_dim(blocks, place ^ (2 * (k & 1) + (k >> 1)), 0, keepdims=False)
            for k in range(4)
        ]

    def move_one(self, sent, k):
        return lax.ppermute(sent, BOTH, self.route(k))

    def move(self, sent):
        return [self.move_one(v, k) for k, v in enumerate(sent)]

    def from_team_blocks(self, value):
        rows, width = value.shape
        blocks = value.reshape(4, rows // 4, width)
        return [
            lax.dynamic_index_in_dim(blocks, self.base() ^ k, 0, keepdims=False) for k in range(4)
        ]

    def back_one(self, sent, k):
        return lax.ppermute(sent, BOTH, [(j, i) for i, j in self.route(k)])

    def in_place(self, received):
        return [received[k] for k in (0, 2, 1, 3)]

    def base(self):
        return 2 * self.bit(self.core) + self.bit(0)

    def member(self):
        return sum(self.bit(b) << i for i, b in enumerate(self.team_bits))

    def exchange(self, values):
        masks = [
            sum(1 << b for i, b in enumerate(self.team_bits) if m >> i & 1)
            for m in range(self.team)
        ]
        return [v if m == 0 else self.swap(v, masks[m]) for m, v in enumerate(values)]

    def me(self):
        return lax.axis_index("dp") * self.seq + lax.axis_index("seq")

    def swap(self, value, mask):
        return lax.ppermute(value, BOTH, [(i, i ^ mask) for i in range(self.count)])

    def own(self):
        return jnp.reshape(lax.axis_index("dp") % 2, (1,))

    def gather(self, values, pieces, width, counts, moved):
        orders = self.orders
        held, masks = [v[None] for v in values], [[0] for v in values]
        levels = self.bits - 1
        early = None
        (held, counts, moved) = lax.optimization_barrier((held, counts, moved))
        for level in range(levels):
            order = [o[levels - 1 - level] for o in orders]
            got = [self.swap(h, 1 << b) for h, b in zip(held, order)]
            masks = [m + [i | 1 << b for i in m] for m, b in zip(masks, order)]
            if level < 2:
                moved[2 * level : 2 * level + 2] = [
                    self.move_one(moved[k], k) for k in (2 * level, 2 * level + 1)
                ]
            if level < len(self.dp_bits):
                counts = counts + self.swap(counts, 1 << self.dp_bits[level])
            held = [jnp.concatenate([h, g], axis=0) for h, g in zip(held, got)]
            if level < 2:
                held, counts, moved = lax.optimization_barrier((held, counts, moved))
            else:
                held, counts = lax.optimization_barrier((held, counts))
            if level == 1:
                early = held
        got = [self.swap(h, 1 << self.core) for h in held]
        masks = [m + [i | 1 << self.core for i in m] for m in masks]
        args = [v for pair in zip(held, got) for v in pair]
        rows = values[0].shape[0]
        wide = (3, self.count, rows, width)
        narrow = (self.count, rows, 128)
        placed = pl.pallas_call(
            functools.partial(place_kernel, masks=masks, pieces=pieces),
            grid_spec=pltpu.PrefetchScalarGridSpec(
                num_scalar_prefetch=1,
                grid=(1,),
                in_specs=[pl.BlockSpec(memory_space=pl.ANY)] * len(args),
                out_specs=[
                    pl.BlockSpec(wide, lambda i, _: (0, 0, 0, 0)),
                    pl.BlockSpec(narrow, lambda i, _: (0, 0, 0)),
                ],
                scratch_shapes=[pltpu.SemaphoreType.DMA((len(values), self.count, 3))],
            ),
            out_shape=[shape(wide, BF16), shape(narrow, BF16)],
            compiler_params=params(),
            name="place",
        )(jnp.reshape(self.me(), (1,)), *args)
        return placed, early, counts, moved


def packed(w_down, w_out, w_gate, w_up, width):
    parts = [w_down, w_out]
    for weight in (w_gate, w_up):
        parts += [weight[:, c : c + width] for c in range(0, weight.shape[1], width)]
    return jnp.concatenate(parts, axis=0)


def regrouped(gathered, each, width):
    if each == ROW_UNIT:
        return gathered
    tall = 4 * each
    down = gathered[:, :tall].reshape(-1, 4 * ROW_UNIT, width)
    parts = [down]
    for at in range(tall, gathered.shape[1], each):
        parts.append(gathered[:, at : at + each].reshape(-1, ROW_UNIT, width))
    return jnp.concatenate(parts, axis=1)


def body(
    links,
    tokens,
    cotangent,
    lengths,
    species,
    ln1_gain,
    ln1_bias,
    w_query,
    w_key,
    w_value,
    w_out,
    ln2_gain,
    ln2_bias,
    w_gate,
    w_up,
    w_down,
):
    wins, rows, width = tokens.shape
    each = w_query.shape[0]
    team = links.team
    lanes = width // team
    share = wins * rows
    scalar = functools.partial(jnp.reshape, shape=(1,))
    member = links.member()
    base = scalar(links.base())

    small = jnp.stack([ln1_gain, ln1_bias, ln2_gain, ln2_bias], axis=1)
    small = jnp.pad(small, ((0, 0), (0, 124)))
    cut = width // 2
    local = [
        jnp.concatenate([w_query, w_key[:, :cut]], axis=1),
        jnp.concatenate([w_key[:, cut:], w_value, small], axis=1),
    ]
    pieces = [
        [(0, width, 0, 0), (width, cut, 1, 0)],
        [(0, cut, 1, cut), (cut, width, 2, 0), (cut + width, 128, None, 0)],
    ]
    species_ids = jnp.arange(SPECIES)
    onehot = (species[:, None] == species_ids[None, :]).astype(F32)
    counts = jnp.sum(onehot * lengths[:, None].astype(F32), axis=0)
    told = jnp.stack([lengths, species])
    told = jnp.stack([told, links.swap(told, 1 << links.core)])
    (qkv_w, small), early, counts, moved = links.gather(
        local, pieces, width, counts, links.to_team(tokens)
    )
    mine = packed(*tie((w_down, w_out, w_gate, w_up), early), width)
    weights = regrouped(lax.all_gather(mine, BOTH, axis=0), each, width)
    qkv_w = qkv_w.reshape(3, width, width)
    vectors = small.reshape(width, 128)[:, :4].T.astype(F32)

    told = lax.dynamic_index_in_dim(told, links.bit(1) ^ links.bit(links.core), 0, keepdims=False)
    told = lax.dynamic_index_in_dim(told, links.bit(0), 1, keepdims=False)
    length, kind = told[0], told[1]
    upper = member >> 1
    half = rows // 2
    block = (4 * upper + jnp.arange(4))[:, None] * rows + links.bit(links.core) * half
    positions = (block + jnp.arange(half)[None, :]).reshape(share)
    table = tables(positions)
    info = jnp.stack([length, member & 1, upper])

    rows_in = arrange(base, moved)
    projected = []
    for m in range(team)[::-1]:
        projected.append(project(scalar(member ^ m), rows_in, qkv_w, vectors, table, lanes))
    projected = projected[::-1]
    normed_one = projected[0][1]
    window_weight = SPECIES * jnp.sum((kind == species_ids) * counts) / jnp.sum(counts)
    row_scale = jnp.where(positions < length, window_weight, 0.0)[:, None]

    qkv = links.exchange([p[0] for p in projected])
    qkv, cot_sent = lax.optimization_barrier((qkv, links.to_team(cotangent)))
    cot_moved = links.move(cot_sent)
    mixed_heads, lse, mixed = [], [], []
    for part in range(PARTS):
        *heads, sums = attend(info, qkv, part)
        mixed_heads.append(heads)
        lse.append(sums)
        mixed += links.exchange(heads)
        if part == 0:
            qkv, cot_moved = lax.optimization_barrier((qkv, tie(cot_moved, sums)))
    cot_in = arrange(base, cot_moved)
    fed = feed(scalar(member), rows_in, cot_in, row_scale, mixed, vectors, weights)
    grad_mixed = fed[:team]
    (
        delta, grad_middle, grad_middle_low, normed_two, grad_low, hidden, grad_gate, grad_up,
        sums_two, mixed_rows,
    ) = fed[team:]
    grad_heads = links.exchange(grad_mixed)

    narrow, broad = width // links.dp, hidden.shape[1] // links.dp
    core = links.own()
    place = scalar(2 * links.bit(0) + links.bit(1))
    shared = (links.count // 2, 5 * each)
    grad_low, sent = lax.optimization_barrier((grad_low, links.from_team_blocks(delta)))
    returned = [links.back_one(sent[k], k) for k in range(2)]
    before = weight_grad(core, hidden, grad_low, broad, shared + (0,))
    low, returned = lax.optimization_barrier((tie(grad_middle_low, before), returned))
    own, away = weight_grad(core, mixed_rows, low, narrow, shared + (4 * each,), before)
    sum_rest = Chain(links, own, away, links.dp_first)
    grad_gate, sent = lax.optimization_barrier((tie(grad_gate, own), sent[2:]))
    returned += [links.back_one(v, k) for k, v in enumerate(sent, 2)]
    own, away = weight_grad(core, normed_two, grad_gate, narrow)
    sum_gate = Chain(links, own, away, links.seq_first)
    grad_up = begin([sum_rest.hold((own, returned))], tie(grad_up, own))
    own, away = weight_grad(core, normed_two, grad_up, narrow)
    sum_up = Chain(links, own, away, links.seq_last)

    def back(part, grads, sub=0, subs=1):
        return attend_back(
            info, qkv, mixed_heads[part], grads, lse[part], part, sub, subs
        )

    def through(part, low, partial):
        return project_back(rows_in, grad_middle, vectors, qkv_w, low, part, team, partial)

    grad_heads = begin([sum_gate.hold(own)], tie(list(grad_heads), own))
    output = settle(place, links.in_place(tie(returned, own)), [tokens])
    grad_heads = begin([sum_up.hold(output)], tie(list(grad_heads), output))
    made = back(0, grad_heads)
    received = links.exchange(made)
    finish([sum_rest, sum_gate, sum_up], made)
    received = begin([sum_gate, sum_up], tie(list(received), made))
    low = unturn(scalar(member), received, table, team)
    own_one, away_one = weight_grad(core, normed_one, low, narrow)
    sum_one = Chain(links, own_one, away_one, links.seq_then)
    (partial,) = through(0, tie(low, own_one), [])
    finish([sum_gate, sum_up], partial)
    if len(links.seq_first) == 4:
        sum_pair = [Joined(sum_gate, sum_up)]
    else:
        sum_pair = [sum_gate, sum_up]
    grad_heads = begin(sum_pair + [sum_rest], tie(list(grad_heads), partial))
    made = back(1, grad_heads)
    received = links.exchange(made)
    chains = sum_pair + [sum_rest]
    finish(chains, made)
    chains.append(sum_one.hold(partial))
    received = begin(chains, tie(list(received), made))
    low = unturn(scalar(member), received, table, team)
    grad_in, sums_one = through(1, low, [partial])
    finish(chains, grad_in)
    chains = [c for c in chains if c.rounds]
    low, sent = begin(chains, (low, links.from_team_blocks(grad_in)))
    home = [links.back_one(v, k) for k, v in enumerate(sent[:2])]
    own_two, away_two = weight_grad(core, normed_one, low, narrow)
    pending = chains
    gains = jnp.concatenate([sums_one, sums_two], axis=0)
    gains = gains.reshape(4, links.dp // 2, 2, width // links.dp).transpose(2, 1, 3, 0)
    gains = gains.reshape(2, width // 2, 4)
    gains = jnp.pad(gains, ((0, 0), (0, 0), (0, 124))).astype(BF16)
    gains = [
        lax.dynamic_index_in_dim(gains, c, 0, keepdims=False) for c in (core[0], 1 - core[0])
    ]
    (own_two, away_two, gains), home = lax.optimization_barrier(((own_two, away_two, gains), home))
    own = jnp.concatenate([own_two, gains[0]], axis=1)
    away = jnp.concatenate([away_two, gains[1]], axis=1)
    last = Chain(links, own, away, links.direct)
    nothing = begin([last], [])
    finish(pending + [last], nothing)
    home += [links.back_one(v, k) for k, v in enumerate(tie(sent[2:], last.terms), 2)]
    pieces = [c for c in sum_pair + [sum_rest] if c.rounds]
    chains = pieces + [Joined(sum_one, last)]
    while chains:
        nothing = begin(chains, [])
        finish(chains, nothing)
        chains = [c for c in chains if c.rounds]
    grad_tokens = settle(place, links.in_place(home), [])

    last = last.result()
    gains = last[:, -128:].T
    merged = jnp.stack([sum_one.result(), last[:, :-128]], axis=1)
    merged = merged.reshape(each, PARTS, 3, team, -1).transpose(0, 2, 3, 1, 4)
    merged = merged.reshape(each, 3, width)
    rest = sum_rest.result()
    return (
        output.reshape(wins, rows, width),
        grad_tokens.reshape(wins, rows, width),
        gains[0],
        gains[1],
        merged[:, 0],
        merged[:, 1],
        merged[:, 2],
        rest[4 * each :],
        gains[2],
        gains[3],
        sum_gate.result(),
        sum_up.result(),
        rest[: 4 * each],
    )


def solution(mesh):
    token = P("dp", "seq", None)
    vector = P(BOTH)
    matrix = P(BOTH, None)
    return jax.shard_map(
        functools.partial(body, Links(mesh)),
        mesh=mesh,
        in_specs=(
            (token, token, P("dp"), P("dp"), vector, vector)
            + (matrix,) * 4
            + (vector, vector)
            + (matrix,) * 3
        ),
        out_specs=(
            (token, token, vector, vector) + (matrix,) * 4 + (vector, vector) + (matrix,) * 3
        ),
        check_vma=False,
    )
```

```python
import functools

import jax
import jax.numpy as jnp
from jax import lax
from jax.experimental import pallas as pl
from jax.experimental.pallas import tpu as pltpu
from jax.sharding import PartitionSpec as P

HEAD_DIM = 64
SPECIES = 8
EPS = 1e-05
LOG2E = 1.4426950408889634
BOTH = ("dp", "seq")
F32 = jnp.float32
BF16 = jnp.bfloat16
FF_BLOCK = 512
FEED_ROWS = 512
PARTS = 2
ROW_UNIT = 32
VMEM = 60 * 2**20

NN = (((1,), (0,)), ((), ()))
NT = (((1,), (1,)), ((), ()))


def dot(a, b, dims=NN):
    return lax.dot_general(a, b, dims, preferred_element_type=F32)


def shape(dims, dtype):
    return jax.ShapeDtypeStruct(dims, dtype)


def params():
    return pltpu.CompilerParams(vmem_limit_bytes=VMEM)


def cost(flops, moved, exps=0):
    return pl.CostEstimate(flops=flops // 64, bytes_accessed=moved // 64, transcendentals=exps // 64)


def normalise(value):
    centered = value - jnp.mean(value, axis=-1, keepdims=True)
    inverse = lax.rsqrt(jnp.mean(centered * centered, axis=-1, keepdims=True) + EPS)
    return centered * inverse, inverse


def norm_back(grad, normal, inverse, gain):
    scaled = grad * gain
    centered = scaled - jnp.mean(scaled, axis=-1, keepdims=True)
    return inverse * (centered - normal * jnp.mean(scaled * normal, axis=-1, keepdims=True))


def turn(value, cosine, early, late):
    return value * cosine + pltpu.roll(value, 96, 1) * early + pltpu.roll(value, 32, 1) * late


def tables(positions):
    half = HEAD_DIM // 2
    freq = 10000.0 ** (-2.0 * jnp.arange(half, dtype=F32) / HEAD_DIM)
    angle = positions.astype(F32)[:, None] * freq[None, :]
    cosine, sine = jnp.cos(angle), jnp.sin(angle)
    zero = jnp.zeros_like(sine)
    return (
        jnp.concatenate([cosine] * 4, axis=1),
        jnp.concatenate([-sine, zero, -sine, zero], axis=1),
        jnp.concatenate([zero, sine, zero, sine], axis=1),
    )


def arrange_kernel(base_ref, *refs):
    for k, ref in enumerate(refs[:-1]):
        refs[-1][base_ref[0] ^ k] = ref[...]


def arrange(base, blocks):
    rows, width = blocks[0].shape
    return pl.pallas_call(
        arrange_kernel,
        grid_spec=pltpu.PrefetchScalarGridSpec(
            num_scalar_prefetch=1,
            grid=(1,),
            in_specs=[pl.BlockSpec((rows, width), lambda i, _: (0, 0))] * len(blocks),
            out_specs=pl.BlockSpec((len(blocks), rows, width), lambda i, _: (0, 0, 0)),
        ),
        out_shape=shape((len(blocks), rows, width), blocks[0].dtype),
        compiler_params=params(),
        cost_estimate=cost(0, 16 * rows * width),
        name="arrange",
    )(base, *blocks).reshape(len(blocks) * rows, width)


def settle_kernel(base_ref, *refs):
    blocks, added, out_ref = refs[:4], refs[4:-1], refs[-1]
    here = pl.program_id(0)

    for k, ref in enumerate(blocks):

        @pl.when((base_ref[0] ^ k) == here)
        def _(ref=ref):
            value = ref[...].astype(F32)
            out_ref[0] = value + added[0][0].astype(F32) if added else value


def settle(base, blocks, added):
    rows, width = blocks[0].shape
    block = pl.BlockSpec((1, rows, width), lambda i, _: (i, 0, 0))
    return pl.pallas_call(
        settle_kernel,
        grid_spec=pltpu.PrefetchScalarGridSpec(
            num_scalar_prefetch=1,
            grid=(4,),
            in_specs=[pl.BlockSpec((rows, width), lambda i, _: (0, 0))] * 4
            + [block] * len(added),
            out_specs=block,
        ),
        out_shape=shape((4, rows, width), F32),
        compiler_params=params(),
        cost_estimate=cost(0, 32 * rows * width),
        name="settle",
    )(base, *blocks, *[a.reshape(4, rows, width) for a in added])


def project_kernel(at_ref, x_ref, w_ref, vec_ref, c_ref, e_ref, l_ref, send_ref, n_ref):
    which = pl.program_id(0)
    _, rows, lanes = send_ref.shape

    @pl.when(which == 0)
    def _():
        normal, _ = normalise(x_ref[...].astype(F32))
        n_ref[...] = (normal * vec_ref[0:1] + vec_ref[1:2]).astype(BF16)

    product = dot(n_ref[...], w_ref[0])
    cosine, early, late = c_ref[...], e_ref[...], l_ref[...]

    def put(rotate):
        for at in range(0, lanes, 128):
            piece = product[:, at : at + 128]
            if rotate:
                piece = turn(piece, cosine, early, late)
            send_ref[0, :, at : at + 128] = piece.astype(BF16)

    pl.when(which < 2)(lambda: put(True))
    pl.when(which == 2)(lambda: put(False))


def project(at, tokens, weights, vectors, table, lanes):
    rows, width = tokens.shape
    wide = pl.BlockSpec((rows, 128), lambda j, _: (0, 0))
    return pl.pallas_call(
        project_kernel,
        grid_spec=pltpu.PrefetchScalarGridSpec(
            num_scalar_prefetch=1,
            grid=(3,),
            in_specs=[
                pl.BlockSpec((rows, width), lambda j, _: (0, 0)),
                pl.BlockSpec((1, width, lanes), lambda j, at: (j, 0, at[0])),
                pl.BlockSpec((4, width), lambda j, _: (0, 0)),
                wide,
                wide,
                wide,
            ],
            out_specs=[
                pl.BlockSpec((1, rows, lanes), lambda j, _: (j, 0, 0)),
                pl.BlockSpec((rows, width), lambda j, _: (0, 0)),
            ],
        ),
        out_shape=[shape((3, rows, lanes), BF16), shape((rows, width), BF16)],
        compiler_params=params(),
        cost_estimate=cost(6 * rows * width * lanes, 6 * rows * lanes + 6 * width * lanes),
        name="project",
    )(at, tokens, weights, vectors, *table)


def attend_kernel(info_ref, *refs, team):
    q_refs, k_refs, v_refs = refs[:team], refs[team : 2 * team], refs[2 * team : 3 * team]
    o_refs, (l_ref, vt_ref) = refs[3 * team : 4 * team], refs[4 * team :]
    length, side, upper = info_ref[0], info_ref[1], info_ref[2]
    lane = lax.broadcasted_iota(jnp.int32, (1, 128), 1)
    block = q_refs[0].shape[0]
    keys, ups = 2 * block, team // 2
    up = pl.program_id(2)

    def chunk(arrays, p, b):
        rows = slice(b * block, (b + 1) * block)
        return jnp.concatenate([arrays[2 * p][rows], arrays[2 * p + 1][rows]], axis=0)

    @pl.when((pl.program_id(1) == 0) & (up == 0))
    def _():
        for p in range(ups):
            for b in range(4):
                at = (4 * p + b) * keys
                vt_ref[:, at : at + keys] = chunk(v_refs, p, b).T

    q2 = jnp.concatenate([q_refs[0][...], q_refs[1][...]], axis=0)
    for p in range(1, ups):
        other = jnp.concatenate([q_refs[2 * p][...], q_refs[2 * p + 1][...]], axis=0)
        q2 = jnp.where(up == p, other, q2)
    q2 = q2 * BF16(0.125)

    def positions(p, b):
        row = lax.broadcasted_iota(jnp.int32, (keys, keys), 0)
        return row ^ (side * block) | (4 * (upper ^ p) + b) * keys

    def run(chunks):
        k2 = jnp.concatenate([chunk(k_refs, c // 4, c % 4) for c in range(chunks)], axis=0)
        n = chunks * keys
        outs = []
        for h in range(2):
            qh = jnp.where((lane // 64) == h, q2, BF16(0))
            s = dot(k2, qh, NT)
            if ups == 1:
                last = jnp.where(positions(0, chunks - 1) < length, s[n - keys :], -1e30)
                s = jnp.concatenate([s[: n - keys], last], 0) if chunks > 1 else last
            else:
                valid = [positions(c // 4, c % 4) < length for c in range(chunks)]
                s = jnp.concatenate(
                    [jnp.where(v, s[c * keys : (c + 1) * keys], -1e30) for c, v in enumerate(valid)],
                    axis=0,
                )
            m = jnp.max(s, axis=0, keepdims=True)
            p = jnp.exp2((s - m) * LOG2E)
            all_p = jnp.sum(p, axis=0, keepdims=True)
            o = dot(vt_ref[h * 64 : h * 64 + 64, :n], p.astype(BF16))
            outs.append(o / all_p)
            l_ref[0, h : h + 1] = m + jnp.log(all_p)
        result = jnp.concatenate(outs, 0).T.astype(BF16)
        for p in range(ups):

            @pl.when(up == p)
            def _(p=p):
                o_refs[2 * p][...] = result[:block]
                o_refs[2 * p + 1][...] = result[block:]

    if ups == 1:
        blocks = (length + keys - 1) // keys
        for i in range(4):
            pl.when(blocks == i + 1)(functools.partial(run, i + 1))
    else:
        run(4 * ups)


def attend(info, qkv, part):
    team = len(qkv)
    _, rows, lanes = qkv[0].shape
    span, pairs, ups = team * rows, lanes // 128 // PARTS, team // 2
    block = rows // 4

    def whole(which):
        return [
            pl.BlockSpec((None, rows, 128), lambda h, b, u, _: (which, 0, part * pairs + h))
        ] * team

    return pl.pallas_call(
        functools.partial(attend_kernel, team=team),
        grid_spec=pltpu.PrefetchScalarGridSpec(
            num_scalar_prefetch=1,
            grid=(pairs, 4, ups),
            in_specs=[
                pl.BlockSpec((None, block, 128), lambda h, b, u, _: (0, b, part * pairs + h))
            ]
            * team
            + whole(1)
            + whole(2),
            out_specs=[pl.BlockSpec((block, 128), lambda h, b, u, _: (b, h))] * team
            + [pl.BlockSpec((1, 2, 2 * block), lambda h, b, u, _: (h, 0, b * ups + u))],
            scratch_shapes=[pltpu.VMEM((128, span), BF16)],
        ),
        out_shape=[shape((rows, pairs * 128), BF16)] * team + [shape((pairs, 2, span), F32)],
        compiler_params=params(),
        cost_estimate=cost(
            16 * span * span * pairs * 128, 8 * span * pairs * 128, 2 * span * span * pairs
        ),
        name="attend",
    )(info, *qkv, *qkv, *qkv)


def attend_back_kernel(info_ref, *refs, team):
    q_refs, k_refs, v_refs, o_refs, g_refs = (refs[i * team : (i + 1) * team] for i in range(5))
    l_ref, d_refs = refs[5 * team], refs[5 * team + 1 : 6 * team + 1]
    kt_ref, dk_ref, dv_ref = refs[6 * team + 1 :]
    length, side, upper = info_ref[0], info_ref[1], info_ref[2]
    lane = lax.broadcasted_iota(jnp.int32, (1, 128), 1)
    block = q_refs[0].shape[0]
    keys, ups = 2 * block, team // 2
    b, up = pl.program_id(1), pl.program_id(2)
    first = (4 * (upper ^ up) + b) * keys

    def chunk(arrays, p, c):
        rows = pl.ds(pl.multiple_of(c * block, block), block)
        return jnp.concatenate([arrays[2 * p][rows], arrays[2 * p + 1][rows]], axis=0)

    def queries(arrays):
        value = jnp.concatenate([arrays[0][...], arrays[1][...]], axis=0)
        for p in range(1, ups):
            other = jnp.concatenate([arrays[2 * p][...], arrays[2 * p + 1][...]], axis=0)
            value = jnp.where(up == p, other, value)
        return value

    @pl.when((b == 0) & (up == 0))
    def _():
        for p in range(ups):
            for c in range(4):
                at = (4 * p + c) * keys
                kt_ref[:, at : at + keys] = (chunk(k_refs, p, c) * BF16(0.125)).T
        dk_ref[...] = jnp.zeros_like(dk_ref)
        dv_ref[...] = jnp.zeros_like(dv_ref)

    here = pl.ds(pl.multiple_of(b * block, block), block)

    def put(value):
        for p in range(ups):

            @pl.when(up == p)
            def _(p=p):
                d_refs[2 * p][0, here] = value[:block]
                d_refs[2 * p + 1][0, here] = value[block:]

    @pl.when(first >= length)
    def _():
        put(jnp.zeros((keys, 128), BF16))

    @pl.when(first < length)
    def _():
        q2 = queries(q_refs) * BF16(0.125)
        g2 = queries(g_refs)
        products = (g2.astype(F32) * queries(o_refs).astype(F32)).T
        qs, gs, ls, ds = [], [], [], []
        for h in range(2):
            mine = (lane // 64) == h
            qs.append(jnp.where(mine, q2, BF16(0)))
            gs.append(jnp.where(mine, g2, BF16(0)))
            ls.append(l_ref[0, h : h + 1] * LOG2E)
            ds.append(jnp.sum(products[h * 64 : h * 64 + 64], axis=0, keepdims=True))
        qc = jnp.concatenate(qs, 0)
        gc = jnp.concatenate(gs, 0)
        lc = jnp.concatenate(ls, 1)
        dc = jnp.concatenate(ds, 1)
        acc = (jnp.zeros((64, keys), F32),) * 2
        for p in range(ups):
            start = 4 * (upper ^ p) * keys

            def step(c, acc, masked, p=p, start=start):
                sl = pl.ds(pl.multiple_of((4 * p + c) * keys, keys), keys)
                k2 = chunk(k_refs, p, c)
                v2 = chunk(v_refs, p, c)
                prob = jnp.exp2(dot(k2, qc, NT) * LOG2E - lc)
                if masked:
                    row = lax.broadcasted_iota(jnp.int32, (keys, 1), 0)
                    row = row ^ (side * block) | (start + c * keys)
                    prob = jnp.where(row < length, prob, 0.0)
                gp = dot(v2, gc, NT)
                gs_low = (prob * (gp - dc)).astype(BF16)
                dv_ref[sl] += dot(prob.astype(BF16), gc)
                dk_ref[sl] += dot(gs_low, qc)
                return tuple(
                    acc[h]
                    + dot(kt_ref[h * 64 : h * 64 + 64, sl], gs_low[:, h * keys : (h + 1) * keys])
                    for h in range(2)
                )

            valid = jnp.clip(length - start, 0, 4 * keys)
            full = valid // keys
            acc = lax.fori_loop(0, full, lambda c, a: step(c, a, False), acc)
            acc = lax.cond(
                full * keys < valid, lambda a: step(full, a, True), lambda a: a, acc
            )
        put(jnp.concatenate(acc, 0).T.astype(BF16))

    @pl.when((b == 3) & (up == ups - 1))
    def _():
        for p in range(ups):
            for c in range(4):
                at = (4 * p + c) * keys
                for t, ref in ((1, dk_ref), (2, dv_ref)):
                    for m in range(2):
                        rows = slice(c * block, (c + 1) * block)
                        piece = ref[at + m * block : at + (m + 1) * block]
                        d_refs[2 * p + m][t, rows] = piece.astype(BF16)


def attend_back(info, qkv, mixed, grad, lse, part, sub, subs):
    team = len(qkv)
    _, rows, lanes = qkv[0].shape
    span, pairs, ups = team * rows, lanes // 128 // PARTS // subs, team // 2
    start, near = (part * subs + sub) * pairs, sub * pairs
    block = rows // 4
    spot = pl.BlockSpec((block, 128), lambda h, b, u, _: (b, start + h))

    def whole(which):
        return [
            pl.BlockSpec((None, rows, 128), lambda h, b, u, _: (which, 0, start + h))
        ] * team

    return pl.pallas_call(
        functools.partial(attend_back_kernel, team=team),
        grid_spec=pltpu.PrefetchScalarGridSpec(
            num_scalar_prefetch=1,
            grid=(pairs, 4, ups),
            in_specs=[
                pl.BlockSpec((None, block, 128), lambda h, b, u, _: (0, b, start + h))
            ]
            * team
            + whole(1)
            + whole(2)
            + [pl.BlockSpec((block, 128), lambda h, b, u, _: (b, near + h))] * team
            + [spot] * team
            + [pl.BlockSpec((1, 2, 2 * block), lambda h, b, u, _: (near + h, 0, b * ups + u))],
            out_specs=[pl.BlockSpec((3, rows, 128), lambda h, b, u, _: (0, 0, h))] * team,
            scratch_shapes=[
                pltpu.VMEM((128, span), BF16),
                pltpu.VMEM((span, 128), F32),
                pltpu.VMEM((span, 128), F32),
            ],
        ),
        out_shape=[shape((3, rows, pairs * 128), BF16)] * team,
        compiler_params=params(),
        cost_estimate=cost(
            30 * span * span * pairs * 128, 16 * span * pairs * 128, 2 * span * span * pairs
        ),
        name="attend_back",
    )(info, *qkv, *qkv, *qkv, *mixed, *grad, lse)


def feed_kernel(
    at_ref, x_ref, cot_ref, scale_ref, vec_ref, wo_ref, wg_ref, wu_ref, wd_ref, *refs, team
):
    mix_refs, send_refs = refs[: team * PARTS], refs[team * PARTS : team * (PARTS + 1)]
    (
        delta_ref, gm_ref, gml_ref, n_ref, gl_ref, hid_ref, gg_ref, gu_ref, sum_ref, rows_ref,
        acc_ref, normal_ref, inv_ref,
    ) = refs[team * (PARTS + 1) :]
    step = pl.program_id(1)
    lanes = send_refs[0].shape[1]
    some = mix_refs[0].shape[1]

    def whole(ref):
        return ref[...].reshape(-1, ref.shape[-1])

    def spot(m, first, size):
        return pl.ds(pl.multiple_of((at_ref[0] ^ m) * lanes + first, size), size)

    @pl.when(step == 0)
    def _():
        for i, ref in enumerate(mix_refs):
            rows_ref[:, spot(i % team, i // team * some, some)] = ref[...]
        added = dot(rows_ref[...], whole(wo_ref))
        acc_ref[...] = added
        normal, inverse = normalise(x_ref[...].astype(F32) + added)
        normal_ref[...] = normal
        inv_ref[...] = inverse
        n_ref[...] = (normal * vec_ref[2:3] + vec_ref[3:4]).astype(BF16)
        gl_ref[...] = (cot_ref[...].astype(F32) * scale_ref[...]).astype(BF16)
        gm_ref[...] = jnp.zeros_like(gm_ref)

    wg, wu, wd = whole(wg_ref), whole(wu_ref), whole(wd_ref)
    normed = n_ref[...]
    gate = dot(normed, wg)
    upper = dot(normed, wu)
    sigma = jax.nn.sigmoid(gate)
    silu = gate * sigma
    hidden = (silu * upper).astype(BF16)
    hid_ref[...] = hidden
    grad_hidden = dot(gl_ref[...], wd, NT)
    grad_up = (grad_hidden * silu).astype(BF16)
    grad_gate = (grad_hidden * upper * sigma * (1.0 + gate * (1.0 - sigma))).astype(BF16)
    gu_ref[...] = grad_up
    gg_ref[...] = grad_gate
    acc_ref[...] += dot(hidden, wd)
    gm_ref[...] += dot(grad_gate, wg, NT) + dot(grad_up, wu, NT)

    @pl.when(step == pl.num_programs(1) - 1)
    def _():
        delta_ref[...] = acc_ref[...].astype(BF16)
        grad = gm_ref[...]
        normal = normal_ref[...]

        @pl.when(pl.program_id(0) == 0)
        def _():
            sum_ref[...] = jnp.zeros_like(sum_ref)

        sum_ref[0:1] += jnp.sum(grad * normal, axis=0, keepdims=True)
        sum_ref[1:2] += jnp.sum(grad, axis=0, keepdims=True)
        total_grad = cot_ref[...].astype(F32) * scale_ref[...] + norm_back(
            grad, normal, inv_ref[...], vec_ref[2:3]
        )
        gm_ref[...] = total_grad
        low = total_grad.astype(BF16)
        gml_ref[...] = low
        acc_ref[...] = dot(low, whole(wo_ref), NT)
        for m in range(team):
            send_refs[m][...] = acc_ref[:, spot(m, 0, lanes)].astype(BF16)


def feed(at, tokens, cotangent, scale, mixed, vectors, weights):
    team = len(mixed) // PARTS
    rows, width = tokens.shape
    lanes = width // team
    units = weights.shape[0]
    tall = 4 * ROW_UNIT
    ff = units * tall
    columns = width // FF_BLOCK
    each = min(FEED_ROWS, rows)
    const = pl.BlockSpec((each, width), lambda i, j, _: (i, 0))
    block = pl.BlockSpec((each, FF_BLOCK), lambda i, j, _: (i, j))
    mix = pl.BlockSpec((each, lanes), lambda i, j, _: (i, 0))

    def part(first):
        return pl.BlockSpec(
            (units, ROW_UNIT, FF_BLOCK), lambda i, j, _: (0, first + j // columns, j % columns)
        )

    return pl.pallas_call(
        functools.partial(feed_kernel, team=team),
        grid_spec=pltpu.PrefetchScalarGridSpec(
            num_scalar_prefetch=1,
            grid=(rows // each, ff // FF_BLOCK),
            in_specs=[
                const,
                const,
                pl.BlockSpec((each, 1), lambda i, j, _: (i, 0)),
                pl.BlockSpec((4, width), lambda i, j, _: (0, 0)),
                pl.BlockSpec((units, ROW_UNIT, width), lambda i, j, _: (0, 4, 0)),
                part(5),
                part(9),
                pl.BlockSpec((FF_BLOCK // tall, tall, width), lambda i, j, _: (j, 0, 0)),
            ]
            + [pl.BlockSpec((each, lanes // PARTS), lambda i, j, _: (i, 0))] * len(mixed),
            out_specs=[mix] * team
            + [const, const, const, const, const, block, block, block]
            + [pl.BlockSpec((2, width), lambda i, j, _: (0, 0)), const],
            scratch_shapes=[
                pltpu.VMEM((each, width), F32),
                pltpu.VMEM((each, width), F32),
                pltpu.VMEM((each, 1), F32),
            ],
        ),
        out_shape=[shape((rows, lanes), BF16)] * team
        + [
            shape((rows, width), BF16),
            shape((rows, width), F32),
            shape((rows, width), BF16),
            shape((rows, width), BF16),
            shape((rows, width), BF16),
            shape((rows, ff), BF16),
            shape((rows, ff), BF16),
            shape((rows, ff), BF16),
            shape((2, width), F32),
            shape((rows, width), BF16),
        ],
        compiler_params=params(),
        cost_estimate=cost(
            12 * rows * width * ff + 4 * rows * width * width,
            12 * width * ff + 6 * rows * ff + 30 * rows * width,
            rows * ff,
        ),
        name="feed",
    )(at, tokens, cotangent, scale, vectors, weights, weights, weights, weights, *mixed)


def weight_kernel(core_ref, a_ref, b_ref, *refs, size):
    own_ref, away_ref, at_ref = refs[-3:]
    rows, tall = a_ref.shape
    core = core_ref[0]
    outs = (own_ref, away_ref)

    @pl.when(pl.program_id(1) == 0)
    def _():
        for side in range(2):
            half = core if side == 0 else 1 - core
            for c in range(tall // (2 * size)):
                start = pl.multiple_of((2 * c + half) * size, 128)
                at_ref[side, c * size : (c + 1) * size] = a_ref[:, pl.ds(start, size)].T

    wide = own_ref.shape[-1]
    for side in range(2):
        product = dot(at_ref[side], b_ref[...].reshape(rows, wide)).astype(BF16)
        outs[side][...] = product.reshape(own_ref.shape)


def weight_grad(core, a, b, chunk, shared=None, before=()):
    rows, tall = a.shape
    stacked = b.ndim == 3
    wide = b.shape[0] * b.shape[2] if stacked else b.shape[1]
    if chunk < 128:
        a = a.reshape(rows, tall // (2 * chunk), 2, chunk).swapaxes(1, 2).reshape(rows, tall)
        chunk = tall // 2
    columns = b.shape[2] if stacked else min(1024, wide)
    block = max(1024, 2 * chunk)
    if stacked:
        right = pl.BlockSpec((1, rows, columns), lambda i, j, _: (j, 0, 0))
    else:
        right = pl.BlockSpec((rows, columns), lambda i, j, _: (0, j))
    if shared:
        devices, height, at = shared
        one = tall // 2 // devices
        made = shape((devices, height, wide), BF16)
        out = pl.BlockSpec(
            (block // 2 // one, one, columns), lambda i, j, _: (i, at // one, j)
        )
    else:
        made = shape((tall // 2, wide), BF16)
        out = pl.BlockSpec((block // 2, columns), lambda i, j, _: (i, j))
    return pl.pallas_call(
        functools.partial(weight_kernel, size=chunk),
        grid_spec=pltpu.PrefetchScalarGridSpec(
            num_scalar_prefetch=1,
            grid=(tall // block, wide // columns),
            in_specs=[pl.BlockSpec((rows, block), lambda i, j, _: (0, i)), right]
            + [pl.BlockSpec(memory_space=pl.ANY)] * len(before),
            out_specs=[out, out],
            scratch_shapes=[pltpu.VMEM((2, block // 2, rows), BF16)],
        ),
        input_output_aliases={3: 0, 4: 1} if before else {},
        out_shape=[made] * 2,
        compiler_params=params(),
        cost_estimate=cost(2 * rows * tall * wide, 2 * (rows * tall + rows * wide + tall * wide)),
        name="weight_grad",
    )(core, a, b, *before)


def unturn_kernel(at_ref, c_ref, e_ref, l_ref, *refs, team):
    blocks, out_ref = refs[:-1], refs[-1]
    cosine, early, late = c_ref[...], e_ref[...], l_ref[...]
    which = pl.program_id(0)
    size = blocks[0].shape[-1]
    lanes = size * len(blocks) // team
    for i, ref in enumerate(blocks):
        for at in range(0, size, 128):
            first = (at_ref[0] ^ (i % team)) * lanes + i // team * size + at
            spot = pl.ds(pl.multiple_of(first, 128), 128)

            @pl.when(which < 2)
            def _(ref=ref, at=at, spot=spot):
                piece = turn(ref[0, :, at : at + 128].astype(F32), cosine, -early, -late)
                out_ref[0, :, spot] = piece.astype(BF16)

            @pl.when(which == 2)
            def _(ref=ref, at=at, spot=spot):
                out_ref[0, :, spot] = ref[0, :, at : at + 128]


def unturn(at, blocks, table, team):
    _, rows, lanes = blocks[0].shape
    wide = pl.BlockSpec((rows, 128), lambda j, _: (0, 0))
    count = len(blocks)
    return pl.pallas_call(
        functools.partial(unturn_kernel, team=team),
        grid_spec=pltpu.PrefetchScalarGridSpec(
            num_scalar_prefetch=1,
            grid=(3,),
            in_specs=[wide] * 3 + [pl.BlockSpec((1, rows, lanes), lambda j, _: (j, 0, 0))] * count,
            out_specs=pl.BlockSpec((1, rows, count * lanes), lambda j, _: (j, 0, 0)),
        ),
        out_shape=shape((3, rows, count * lanes), BF16),
        compiler_params=params(),
        cost_estimate=cost(0, 12 * rows * count * lanes),
        name="unturn",
    )(at, *table, *blocks)


def project_back_kernel(x_ref, gm_ref, vec_ref, w_ref, low_ref, *refs, part, lanes, first, last):
    which = pl.program_id(0)
    acc_ref = refs[-1]

    @pl.when(which == 0)
    def _():
        acc_ref[...] = jnp.zeros_like(acc_ref) if first else refs[0][...]

    width = w_ref.shape[-1]
    weight = jnp.concatenate(
        [
            w_ref[0, :, at : at + lanes]
            for at in range(part * lanes, width, PARTS * lanes)
        ],
        axis=1,
    )
    acc_ref[...] += dot(low_ref[0], weight, NT)

    if last:
        out_ref, sum_ref = refs[-3:-1]

        @pl.when(which == 2)
        def _():
            grad = acc_ref[...]
            normal, inverse = normalise(x_ref[...].astype(F32))
            sum_ref[0:1] = jnp.sum(grad * normal, axis=0, keepdims=True)
            sum_ref[1:2] = jnp.sum(grad, axis=0, keepdims=True)
            grad = gm_ref[...] + norm_back(grad, normal, inverse, vec_ref[0:1])
            out_ref[...] = grad.astype(BF16)


def project_back(tokens, grad_middle, vectors, weights, low, part, team, partial):
    rows, width = tokens.shape
    wide = low.shape[-1]
    last = part == PARTS - 1
    const = pl.BlockSpec((rows, width), lambda j: (0, 0))
    return pl.pallas_call(
        functools.partial(
            project_back_kernel, part=part, lanes=wide // team, first=not partial, last=last
        ),
        grid=(3,),
        in_specs=[
            const,
            const,
            pl.BlockSpec((4, width), lambda j: (0, 0)),
            pl.BlockSpec((1, width, width), lambda j: (j, 0, 0)),
            pl.BlockSpec((1, rows, wide), lambda j: (j, 0, 0)),
        ]
        + [const] * len(partial),
        out_specs=[const, pl.BlockSpec((2, width), lambda j: (0, 0))] if last else [const],
        out_shape=(
            [shape((rows, width), BF16), shape((2, width), F32)]
            if last
            else [shape((rows, width), F32)]
        ),
        scratch_shapes=[pltpu.VMEM((rows, width), F32)] if last else [],
        compiler_params=params(),
        cost_estimate=cost(6 * rows * width * wide, 18 * rows * width + 6 * width * width),
        name="project_back",
    )(tokens, grad_middle, vectors, weights, low, *partial)


def place_kernel(me_ref, *refs, masks, pieces):
    count = len(masks)
    halves, (wide_ref, small_ref, sem) = refs[: 2 * count], refs[2 * count :]
    me = me_ref[0]
    for wait in (False, True):
        for t in range(count):
            half = len(masks[t]) // 2
            for j, mask in enumerate(masks[t]):
                source = halves[2 * t + j // half].at[j % half]
                for lane, (first, size, which, to) in enumerate(pieces[t]):
                    origin = source.at[:, first : first + size]
                    if which is None:
                        place = small_ref.at[me ^ mask]
                    else:
                        place = wide_ref.at[which, me ^ mask, :, to : to + size]
                    copy = pltpu.make_async_copy(origin, place, sem.at[t, j, lane])
                    copy.wait() if wait else copy.start()


class Chain:
    def __init__(self, links, own, away, rounds, wire=BF16):
        self.links, self.rounds, self.wire = links, [list(r) for r in rounds], wire
        self.axes = [b for b in range(links.bits - 1, -1, -1) if b != links.core]
        self.dims = (2,) * len(self.axes)
        if own.ndim == 2:
            self.dims += (own.shape[0] * 2 // links.count,)
        self.dims += own.shape[1:]
        self.terms = [own.reshape(self.dims), links.swap(away, 1 << links.core).reshape(self.dims)]

    def hold(self, after):
        self.terms = tie(self.terms, after)
        return self

    def pick(self, mask):
        me, parts, axes = self.links.me() ^ mask, self.terms, list(self.axes)
        for bit in self.rounds[0]:
            at = axes.index(bit)
            parts = [
                lax.dynamic_index_in_dim(p, (me >> bit) & 1, at, keepdims=False) for p in parts
            ]
            axes.pop(at)
        return parts

    def split(self):
        self.masks = [0]
        for bit in self.rounds[0]:
            self.masks += [m | 1 << bit for m in self.masks]
        sent = [total(self.pick(m)).astype(self.wire) for m in self.masks[1:]]
        self.kept = self.pick(0)
        return sent

    def swap(self, sent):
        return [self.links.swap(v, m) for v, m in zip(sent, self.masks[1:])]

    def take(self, received):
        for bit in self.rounds.pop(0):
            self.axes.remove(bit)
        self.terms = self.kept + list(received)

    def result(self):
        return total(self.terms)


class Joined:
    def __init__(self, *chains):
        self.chains, self.links = chains, chains[0].links

    @property
    def rounds(self):
        return self.chains[0].rounds

    def split(self):
        sent = [c.split() for c in self.chains]
        return [jnp.concatenate(v, axis=-1) for v in zip(*sent)]

    def swap(self, sent):
        return self.chains[0].swap(sent)

    def take(self, received):
        first = 0
        for c in self.chains:
            last = first + c.terms[0].shape[-1]
            c.take([v[..., first:last] for v in received])
            first = last


def total(terms):
    return functools.reduce(jnp.add, [t.astype(F32) for t in terms])


def tie(values, *others):
    return lax.optimization_barrier((values, others))[0]


def begin(chains, values):
    sent = [c.split() for c in chains]
    values, sent = lax.optimization_barrier((values, sent))
    for c, v in zip(chains, sent):
        c.received = c.swap(v)
    return values


def finish(chains, after):
    received = tie([c.received for c in chains], after)
    for c, r in zip(chains, received):
        c.take(r)


class Links:
    def __init__(self, mesh):
        self.dp, self.seq = mesh.shape["dp"], mesh.shape["seq"]
        self.count = self.dp * self.seq
        self.bits = self.count.bit_length() - 1
        self.core = self.seq.bit_length() - 1
        seq_bits = list(range(self.core))
        dp_bits = list(range(self.core + 1, self.bits))
        self.dp_bits = [self.core] + dp_bits
        first, last = dp_bits[:1], dp_bits[1:]
        self.seq_first = [[b] for b in seq_bits + dp_bits[::-1]]
        self.seq_last = [[b] for b in seq_bits[::-1] + dp_bits[::-1]]
        self.dp_first = [[b] for b in first + seq_bits + last]
        self.seq_then = [seq_bits[:1], seq_bits[1:], dp_bits]
        self.direct = [seq_bits, dp_bits]
        self.orders = [
            seq_bits + dp_bits,
            seq_bits[::-1] + dp_bits,
            dp_bits[:1] + seq_bits + dp_bits[1:],
            dp_bits[:1] + seq_bits[::-1] + dp_bits[1:],
        ]

        self.team_bits = [self.core] + seq_bits[2:]
        self.team = 2 ** len(self.team_bits)

    def bit(self, which):
        return (self.me() >> which) & 1

    def route(self, k):
        pairs = []
        for i in range(self.count):
            core, y, x = (i >> self.core) & 1, (i >> 1) & 1, i & 1
            rest = i & ~((1 << self.core) | 3)
            pairs.append((i, rest | (y ^ (k >> 1)) << self.core | core << 1 | (x ^ (k & 1))))
        return pairs

    def to_team(self, value):
        wins, rows, width = value.shape
        blocks = value.reshape(wins * 2, rows // 2, width)
        place = 2 * self.bit(0) + self.bit(1)
        return [
            lax.dynamic_index_in_dim(blocks, place ^ (2 * (k & 1) + (k >> 1)), 0, keepdims=False)
            for k in range(4)
        ]

    def move_one(self, sent, k):
        return lax.ppermute(sent, BOTH, self.route(k))

    def move(self, sent):
        return [self.move_one(v, k) for k, v in enumerate(sent)]

    def from_team_blocks(self, value):
        rows, width = value.shape
        blocks = value.reshape(4, rows // 4, width)
        return [
            lax.dynamic_index_in_dim(blocks, self.base() ^ k, 0, keepdims=False) for k in range(4)
        ]

    def back_one(self, sent, k):
        return lax.ppermute(sent, BOTH, [(j, i) for i, j in self.route(k)])

    def in_place(self, received):
        return [received[k] for k in (0, 2, 1, 3)]

    def base(self):
        return 2 * self.bit(self.core) + self.bit(0)

    def member(self):
        return sum(self.bit(b) << i for i, b in enumerate(self.team_bits))

    def exchange(self, values):
        masks = [
            sum(1 << b for i, b in enumerate(self.team_bits) if m >> i & 1)
            for m in range(self.team)
        ]
        return [v if m == 0 else self.swap(v, masks[m]) for m, v in enumerate(values)]

    def me(self):
        return lax.axis_index("dp") * self.seq + lax.axis_index("seq")

    def swap(self, value, mask):
        return lax.ppermute(value, BOTH, [(i, i ^ mask) for i in range(self.count)])

    def own(self):
        return jnp.reshape(lax.axis_index("dp") % 2, (1,))

    def gather(self, values, pieces, width, counts, moved):
        orders = self.orders
        held, masks = [v[None] for v in values], [[0] for v in values]
        levels = self.bits - 1
        early = None
        (held, counts, moved) = lax.optimization_barrier((held, counts, moved))
        for level in range(levels):
            order = [o[levels - 1 - level] for o in orders]
            got = [self.swap(h, 1 << b) for h, b in zip(held, order)]
            masks = [m + [i | 1 << b for i in m] for m, b in zip(masks, order)]
            if level == 1:
                early = got
            if level < 2:
                moved[2 * level : 2 * level + 2] = [
                    self.move_one(moved[k], k) for k in (2 * level, 2 * level + 1)
                ]
            if level < len(self.dp_bits):
                counts = counts + self.swap(counts, 1 << self.dp_bits[level])
            held = [jnp.concatenate([h, g], axis=0) for h, g in zip(held, got)]
            if level < 2:
                held, counts, moved = lax.optimization_barrier((held, counts, moved))
            else:
                held, counts = lax.optimization_barrier((held, counts))
        got = [self.swap(h, 1 << self.core) for h in held]
        masks = [m + [i | 1 << self.core for i in m] for m in masks]
        args = [v for pair in zip(held, got) for v in pair]
        rows = values[0].shape[0]
        wide = (3, self.count, rows, width)
        narrow = (self.count, rows, 128)
        placed = pl.pallas_call(
            functools.partial(place_kernel, masks=masks, pieces=pieces),
            grid_spec=pltpu.PrefetchScalarGridSpec(
                num_scalar_prefetch=1,
                grid=(1,),
                in_specs=[pl.BlockSpec(memory_space=pl.ANY)] * len(args),
                out_specs=[
                    pl.BlockSpec(wide, lambda i, _: (0, 0, 0, 0)),
                    pl.BlockSpec(narrow, lambda i, _: (0, 0, 0)),
                ],
                scratch_shapes=[pltpu.SemaphoreType.DMA((len(values), self.count, 3))],
            ),
            out_shape=[shape(wide, BF16), shape(narrow, BF16)],
            compiler_params=params(),
            name="place",
        )(jnp.reshape(self.me(), (1,)), *args)
        return placed, early, counts, moved


def packed(w_down, w_out, w_gate, w_up, width):
    parts = [w_down, w_out]
    for weight in (w_gate, w_up):
        parts += [weight[:, c : c + width] for c in range(0, weight.shape[1], width)]
    return jnp.concatenate(parts, axis=0)


def regrouped(gathered, each, width):
    if each == ROW_UNIT:
        return gathered
    tall = 4 * each
    down = gathered[:, :tall].reshape(-1, 4 * ROW_UNIT, width)
    parts = [down]
    for at in range(tall, gathered.shape[1], each):
        parts.append(gathered[:, at : at + each].reshape(-1, ROW_UNIT, width))
    return jnp.concatenate(parts, axis=1)


def body(
    links,
    tokens,
    cotangent,
    lengths,
    species,
    ln1_gain,
    ln1_bias,
    w_query,
    w_key,
    w_value,
    w_out,
    ln2_gain,
    ln2_bias,
    w_gate,
    w_up,
    w_down,
):
    wins, rows, width = tokens.shape
    each = w_query.shape[0]
    team = links.team
    lanes = width // team
    share = wins * rows
    scalar = functools.partial(jnp.reshape, shape=(1,))
    member = links.member()
    base = scalar(links.base())

    small = jnp.stack([ln1_gain, ln1_bias, ln2_gain, ln2_bias], axis=1)
    small = jnp.pad(small, ((0, 0), (0, 124)))
    cut = width // 2
    local = [
        jnp.concatenate([w_query, w_key[:, :cut]], axis=1),
        jnp.concatenate([w_key[:, cut:], w_value, small], axis=1),
    ]
    pieces = [
        [(0, width, 0, 0), (width, cut, 1, 0)],
        [(0, cut, 1, cut), (cut, width, 2, 0), (cut + width, 128, None, 0)],
    ]
    species_ids = jnp.arange(SPECIES)
    onehot = (species[:, None] == species_ids[None, :]).astype(F32)
    counts = jnp.sum(onehot * lengths[:, None].astype(F32), axis=0)
    told = jnp.stack([lengths, species])
    told = jnp.stack([told, links.swap(told, 1 << links.core)])
    (qkv_w, small), early, counts, moved = links.gather(
        local, pieces, width, counts, links.to_team(tokens)
    )
    mine = packed(*tie((w_down, w_out, w_gate, w_up), early), width)
    weights = regrouped(lax.all_gather(mine, BOTH, axis=0), each, width)
    qkv_w = qkv_w.reshape(3, width, width)
    vectors = small.reshape(width, 128)[:, :4].T.astype(F32)

    told = lax.dynamic_index_in_dim(told, links.bit(1) ^ links.bit(links.core), 0, keepdims=False)
    told = lax.dynamic_index_in_dim(told, links.bit(0), 1, keepdims=False)
    length, kind = told[0], told[1]
    upper = member >> 1
    half = rows // 2
    block = (4 * upper + jnp.arange(4))[:, None] * rows + links.bit(links.core) * half
    positions = (block + jnp.arange(half)[None, :]).reshape(share)
    table = tables(positions)
    info = jnp.stack([length, member & 1, upper])

    rows_in = arrange(base, moved)
    projected = []
    for m in range(team)[::-1]:
        projected.append(project(scalar(member ^ m), rows_in, qkv_w, vectors, table, lanes))
    projected = projected[::-1]
    normed_one = projected[0][1]
    window_weight = SPECIES * jnp.sum((kind == species_ids) * counts) / jnp.sum(counts)
    row_scale = jnp.where(positions < length, window_weight, 0.0)[:, None]

    qkv = links.exchange([p[0] for p in projected])
    qkv, cot_sent = lax.optimization_barrier((qkv, links.to_team(cotangent)))
    cot_moved = links.move(cot_sent)
    mixed_heads, lse, mixed = [], [], []
    for part in range(PARTS):
        *heads, sums = attend(info, qkv, part)
        mixed_heads.append(heads)
        lse.append(sums)
        mixed += links.exchange(heads)
        if part == 0:
            qkv, cot_moved = lax.optimization_barrier((qkv, tie(cot_moved, sums)))
    cot_in = arrange(base, cot_moved)
    fed = feed(scalar(member), rows_in, cot_in, row_scale, mixed, vectors, weights)
    grad_mixed = fed[:team]
    (
        delta, grad_middle, grad_middle_low, normed_two, grad_low, hidden, grad_gate, grad_up,
        sums_two, mixed_rows,
    ) = fed[team:]
    grad_heads = links.exchange(grad_mixed)

    narrow, broad = width // links.dp, hidden.shape[1] // links.dp
    core = links.own()
    place = scalar(2 * links.bit(0) + links.bit(1))
    shared = (links.count // 2, 5 * each)
    grad_low, sent = lax.optimization_barrier((grad_low, links.from_team_blocks(delta)))
    returned = [links.back_one(sent[k], k) for k in range(2)]
    before = weight_grad(core, hidden, grad_low, broad, shared + (0,))
    low, returned = lax.optimization_barrier((tie(grad_middle_low, before), returned))
    own, away = weight_grad(core, mixed_rows, low, narrow, shared + (4 * each,), before)
    sum_rest = Chain(links, own, away, links.dp_first)
    grad_gate, sent = lax.optimization_barrier((tie(grad_gate, own), sent[2:]))
    returned += [links.back_one(v, k) for k, v in enumerate(sent, 2)]
    own, away = weight_grad(core, normed_two, grad_gate, narrow)
    sum_gate = Chain(links, own, away, links.seq_first)
    grad_up = begin([sum_rest.hold((own, returned))], tie(grad_up, own))
    own, away = weight_grad(core, normed_two, grad_up, narrow)
    sum_up = Chain(links, own, away, links.seq_last)

    def back(part, grads, sub=0, subs=1):
        return attend_back(
            info, qkv, mixed_heads[part], grads, lse[part], part, sub, subs
        )

    def through(part, low, partial):
        return project_back(rows_in, grad_middle, vectors, qkv_w, low, part, team, partial)

    grad_heads = begin([sum_gate.hold(own)], tie(list(grad_heads), own))
    output = settle(place, links.in_place(tie(returned, own)), [tokens])
    grad_heads = begin([sum_up.hold(output)], tie(list(grad_heads), output))
    made = back(0, grad_heads)
    received = links.exchange(made)
    finish([sum_rest, sum_gate, sum_up], made)
    received = begin([sum_gate, sum_up], tie(list(received), made))
    low = unturn(scalar(member), received, table, team)
    own_one, away_one = weight_grad(core, normed_one, low, narrow)
    sum_one = Chain(links, own_one, away_one, links.seq_then)
    (partial,) = through(0, tie(low, own_one), [])
    finish([sum_gate, sum_up], partial)
    if len(links.seq_first) == 4:
        sum_pair = [Joined(sum_gate, sum_up)]
    else:
        sum_pair = [sum_gate, sum_up]
    grad_heads = begin(sum_pair + [sum_rest], tie(list(grad_heads), partial))
    made = back(1, grad_heads)
    received = links.exchange(made)
    chains = sum_pair + [sum_rest]
    finish(chains, made)
    chains.append(sum_one.hold(partial))
    received = begin(chains, tie(list(received), made))
    low = unturn(scalar(member), received, table, team)
    grad_in, sums_one = through(1, low, [partial])
    finish(chains, grad_in)
    chains = [c for c in chains if c.rounds]
    low, sent = begin(chains, (low, links.from_team_blocks(grad_in)))
    home = [links.back_one(v, k) for k, v in enumerate(sent[:2])]
    own_two, away_two = weight_grad(core, normed_one, low, narrow)
    pending = chains
    gains = jnp.concatenate([sums_one, sums_two], axis=0)
    gains = gains.reshape(4, links.dp // 2, 2, width // links.dp).transpose(2, 1, 3, 0)
    gains = gains.reshape(2, width // 2, 4)
    gains = jnp.pad(gains, ((0, 0), (0, 0), (0, 124))).astype(BF16)
    gains = [
        lax.dynamic_index_in_dim(gains, c, 0, keepdims=False) for c in (core[0], 1 - core[0])
    ]
    (own_two, away_two, gains), home = lax.optimization_barrier(((own_two, away_two, gains), home))
    own = jnp.concatenate([own_two, gains[0]], axis=1)
    away = jnp.concatenate([away_two, gains[1]], axis=1)
    last = Chain(links, own, away, links.direct)
    nothing = begin([last], [])
    finish(pending + [last], nothing)
    home += [links.back_one(v, k) for k, v in enumerate(tie(sent[2:], last.terms), 2)]
    pieces = [c for c in sum_pair + [sum_rest] if c.rounds]
    chains = pieces + [Joined(sum_one, last)]
    while chains:
        nothing = begin(chains, [])
        finish(chains, nothing)
        chains = [c for c in chains if c.rounds]
    grad_tokens = settle(place, links.in_place(home), [])

    last = last.result()
    gains = last[:, -128:].T
    merged = jnp.stack([sum_one.result(), last[:, :-128]], axis=1)
    merged = merged.reshape(each, PARTS, 3, team, -1).transpose(0, 2, 3, 1, 4)
    merged = merged.reshape(each, 3, width)
    rest = sum_rest.result()
    return (
        output.reshape(wins, rows, width),
        grad_tokens.reshape(wins, rows, width),
        gains[0],
        gains[1],
        merged[:, 0],
        merged[:, 1],
        merged[:, 2],
        rest[4 * each :],
        gains[2],
        gains[3],
        sum_gate.result(),
        sum_up.result(),
        rest[: 4 * each],
    )


def solution(mesh):
    token = P("dp", "seq", None)
    vector = P(BOTH)
    matrix = P(BOTH, None)
    return jax.shard_map(
        functools.partial(body, Links(mesh)),
        mesh=mesh,
        in_specs=(
            (token, token, P("dp"), P("dp"), vector, vector)
            + (matrix,) * 4
            + (vector, vector)
            + (matrix,) * 3
        ),
        out_specs=(
            (token, token, vector, vector) + (matrix,) * 4 + (vector, vector) + (matrix,) * 3
        ),
        check_vma=False,
    )
```
